32 devices in a mesh: dp: 8 (over y, x, core), tensor: 4 (over z).
Axes of the slice: x: 2, y: 2, z: 4, core: 2. Of those that a mesh axis runs over, the one named last changes fastest.
Arguments:
- layer_input: bfloat16 [16384, 768], P('dp'), may hold values from -6 to 6
- segment_ids: int32 [16384], P('dp'), may hold values from -1 to 3, as said below
- w_qkv: bfloat16 [768, 12, 192], P(None, 'tensor'), may hold values from -0.21875 to 0.21875
- qv_bias: bfloat16 [12, 128], P('tensor'), may hold values from -3 to 3
- w_out: bfloat16 [768, 768], P('tensor'), may hold values from -0.875 to 0.875
- out_bias: bfloat16 [768], replicated, may hold values from -2 to 2
- norm1_gain: bfloat16 [768], replicated, may hold values from 0.25 to 1.75
- norm1_bias: bfloat16 [768], replicated, may hold values from -2 to 2
- w_up: bfloat16 [768, 3072], P(None, 'tensor'), may hold values from -0.21875 to 0.21875
- up_bias: bfloat16 [3072], P('tensor'), may hold values from -3 to 3
- w_down: bfloat16 [3072, 768], P('tensor'), may hold values from -0.109375 to 0.109375
- down_bias: bfloat16 [768], replicated, may hold values from -2 to 2
- norm2_gain: bfloat16 [768], replicated, may hold values from 0.25 to 1.75
- norm2_bias: bfloat16 [768], replicated, may hold values from -2 to 2
- out_cotangent: bfloat16 [16384, 768], P(('dp', 'tensor')), may hold values from -6 to 6
Outputs:
- layer_output: bfloat16 [16384, 768], P(('dp', 'tensor'))
- input_grad: float32 [16384, 768], P(('dp', 'tensor'))
- grad_qkv: float32 [768, 12, 192], P(None, 'tensor')
- grad_qv_bias: float32 [12, 128], P('tensor')
- grad_out: float32 [768, 768], P('tensor')
- grad_out_bias: float32 [768], replicated
- grad_norm1_gain: float32 [768], replicated
- grad_norm1_bias: float32 [768], replicated
- grad_up: float32 [768, 3072], P(None, 'tensor')
- grad_up_bias: float32 [3072], P('tensor')
- grad_down: float32 [3072, 768], P('tensor')
- grad_down_bias: float32 [768], replicated
- grad_norm2_gain: float32 [768], replicated
- grad_norm2_bias: float32 [768], replicated
The draws below stay inside these ranges and needn't reach their ends.
Inputs may be any that keep to these rules, and one draw needn't show every extreme that they name: `segment_ids`: the 8 blocks of 2048 consecutive tokens (those of one index of dp) each hold their live rows first: some wholly live rows, then one row whose live tokens form a prefix of 256 tokens or more, then wholly padded rows (-1). One block is wholly live; every other block has padding. In a live row the segment numbers start at 0 and never fall; a wholly live row has exactly 4 segments.
All inputs are finite; a program needn't handle non-finite values.
Results may differ from the reference program's by a relative error of at most 0.02.
Values may be sent and summed in bfloat16 or wider, within the bound.
A program may use at most 128 MiB of HBM per device.

```python
import jax
import jax.numpy as jnp
from jax import lax

D = 768
HEADS = 12
HD = 64
FF = 3072
SEQ = 1024
CUTS = 3
ROW_CAP = 2
TOKENS = 16384
N_DP = 8
N_TENSOR = 4


def draw_segment_ids(key, part):
    key = jax.random.fold_in(key, 17)
    live_key, full_key, tail_key, cut_key = jax.random.split(key, 4)
    group_rows = jax.random.randint(live_key, (N_DP,), 1, ROW_CAP + 1)
    full_group = jax.random.randint(full_key, (), 0, N_DP)
    is_full = jnp.arange(N_DP) == full_group
    group_rows = jnp.where(is_full, ROW_CAP, group_rows)
    tail_live = jax.random.randint(tail_key, (N_DP,), SEQ // 4, SEQ)
    tail_live = jnp.where(is_full, SEQ, tail_live)
    row_keys = jax.random.split(cut_key, N_DP * ROW_CAP)
    cut_points = jax.vmap(lambda row_key: jax.random.permutation(row_key, SEQ - 1)[:CUTS] + 1)(row_keys)
    positions = jnp.arange(SEQ)
    numbers = jnp.sum((cut_points[:, None, :] <= positions[None, :, None]).astype(jnp.int32), axis=-1)
    numbers = numbers.reshape(N_DP, ROW_CAP, SEQ)
    row_place = jnp.arange(ROW_CAP)[None, :, None]
    whole_live = row_place < group_rows[:, None, None] - 1
    tail_row = (row_place == group_rows[:, None, None] - 1) & (positions[None, None, :] < tail_live[:, None, None])
    live_mask = whole_live | tail_row
    return jnp.where(live_mask, numbers, -1).reshape(N_DP * ROW_CAP * SEQ).astype(jnp.int32)


def levels(key, extent, shards, least, top_value):
    gain = 1.0
    for axis_at, blocks in shards:
        draws = jax.random.uniform(jax.random.fold_in(jax.random.fold_in(key, 6), axis_at), (blocks,), jnp.float32, least / len(shards), top_value / len(shards))
        gain = gain * jnp.repeat(jnp.exp(draws), extent[axis_at] // blocks).reshape((-1,) + (1,) * (len(extent) - 1 - axis_at))
    return gain


def bell_draw(stream_key, shape, width, reach, cuts=(), dtype=jnp.bfloat16):
    loudness = levels(stream_key, shape, cuts, -0.22, 0.18) if cuts else 1.0
    values = jax.random.normal(stream_key, shape, jnp.float32) * width * loudness
    return jnp.minimum(jnp.maximum(values, -reach), reach).astype(dtype)


def setup_inputs(seed: int = 0) -> dict:
    streams_of = jax.random.split(jax.random.key(seed), 16)
    layer_input = bell_draw(streams_of[0], (TOKENS, D), 1.0, 6.0, ((0, 8),))
    segment_ids = draw_segment_ids(jax.random.fold_in(streams_of[15], 71), 0)
    w_qkv = bell_draw(streams_of[2], (D, HEADS, 3 * HD), D ** -0.5, 0.21875, ((1, 4),))
    qv_bias = bell_draw(streams_of[3], (HEADS, 2 * HD), 0.5, 3.0, ((0, 4),))
    w_out = bell_draw(streams_of[4], (HEADS * HD, D), (D // 16) ** -0.5, 0.875, ((0, 4),))
    out_bias = bell_draw(streams_of[5], (D,), 0.3, 2.0)
    norm1_gain = jnp.clip(1.0 + 0.15 * jax.random.normal(streams_of[6], (D,), jnp.float32), 0.25, 1.75).astype(jnp.bfloat16)
    norm1_bias = bell_draw(streams_of[7], (D,), 0.3, 2.0)
    w_up = bell_draw(streams_of[8], (D, FF), D ** -0.5, 0.21875, ((1, 4),))
    up_bias = bell_draw(streams_of[9], (FF,), 0.5, 3.0, ((0, 4),))
    w_down = bell_draw(streams_of[10], (FF, D), FF ** -0.5, 0.109375, ((0, 4),))
    down_bias = bell_draw(streams_of[11], (D,), 0.3, 2.0)
    norm2_gain = jnp.clip(1.0 + 0.15 * jax.random.normal(streams_of[12], (D,), jnp.float32), 0.25, 1.75).astype(jnp.bfloat16)
    norm2_bias = bell_draw(streams_of[13], (D,), 0.3, 2.0)
    out_cotangent = bell_draw(streams_of[14], (TOKENS, D), 1.0, 6.0, ((0, 32),))
    return dict(layer_input=layer_input, segment_ids=segment_ids, w_qkv=w_qkv, qv_bias=qv_bias, w_out=w_out, out_bias=out_bias, norm1_gain=norm1_gain, norm1_bias=norm1_bias, w_up=w_up, up_bias=up_bias, w_down=w_down, down_bias=down_bias, norm2_gain=norm2_gain, norm2_bias=norm2_bias, out_cotangent=out_cotangent)


@jax.custom_vjp
def low(v):
    return lax.optimization_barrier(v.astype(jnp.bfloat16)).astype(jnp.float32)

@jax.custom_vjp
def low_back(v):
    return v

def low_keep(v):
    return (low(v), None)

def low_pass(kept, grad):
    return (grad,)

def back_keep(v):
    return (v, None)

def back_low(kept, grad):
    return (low(grad),)
low.defvjp(low_keep, low_pass)
low_back.defvjp(back_keep, back_low)
EPSILON = 1e-06
MASKED = -1e+30
PRECISE = lax.Precision.HIGHEST

def layer_norm(summed, norm_gain, norm_shift):
    row_mean = lax.optimization_barrier(jnp.mean(summed, axis=-1, keepdims=True))
    centred = summed - row_mean
    spread = lax.optimization_barrier(jnp.mean(centred * centred, axis=-1, keepdims=True))
    return centred * lax.rsqrt(spread + EPSILON) * norm_gain + norm_shift

def attend_row(queries, keys_row, values_row, segment):
    score_scale = float(HD) ** (-0.5)
    raw_scores = low_back(jnp.einsum('qhd,khd->hqk', queries, keys_row, precision=PRECISE))
    allowed = segment[:, None] == segment[None, :]
    scores = jnp.where(allowed[None], raw_scores * score_scale, MASKED)
    probability = low(jax.nn.softmax(scores, axis=-1))
    return jnp.einsum('hqk,khd->qhd', probability, values_row, precision=PRECISE)

def blockwise_product(left_side, right_side):
    block_width = left_side.shape[1] // N_TENSOR
    summed = jnp.zeros((left_side.shape[0], right_side.shape[1]), jnp.float32)
    for block_index in range(N_TENSOR):
        lower_edge = block_index * block_width
        block_term = jnp.dot(left_side[:, lower_edge:lower_edge + block_width], right_side[lower_edge:lower_edge + block_width], precision=PRECISE)
        summed = summed + low(block_term)
    return summed

def forward(layer_input, w_qkv, qv_bias, w_out, out_bias, norm1_gain, norm1_bias, w_up, up_bias, w_down, down_bias, norm2_gain, norm2_bias, segment_ids):
    token_count = layer_input.shape[0]
    row_count = token_count // SEQ
    projected = jnp.dot(layer_input, w_qkv.reshape(D, HEADS * 3 * HD), precision=PRECISE).reshape(token_count, HEADS, 3 * HD)
    key_zeros = jnp.zeros((HEADS, HD), jnp.float32)
    joined_bias = jnp.concatenate([qv_bias[:, :HD], key_zeros, qv_bias[:, HD:]], axis=1)
    projected = low(low_back(projected + joined_bias)).reshape(row_count, SEQ, HEADS, 3 * HD)
    checked = jax.checkpoint(attend_row)
    attended = lax.map(lambda packed: checked(*packed), (projected[..., :HD], projected[..., HD:2 * HD], projected[..., 2 * HD:], segment_ids.reshape(row_count, SEQ)))
    attended = low(low_back(attended.reshape(token_count, HEADS * HD)))
    attn_branch = low_back(blockwise_product(attended, w_out))
    first_sum = layer_input + attn_branch + out_bias
    hidden = layer_norm(first_sum, norm1_gain, norm1_bias)
    up_pre = low_back(jnp.dot(low(hidden), w_up, precision=PRECISE) + up_bias)
    activation = low(jax.nn.gelu(up_pre, approximate=False))
    ffn_branch = low_back(blockwise_product(activation, w_down))
    second_sum = hidden + ffn_branch + down_bias
    return layer_norm(second_sum, norm2_gain, norm2_bias)

def reference(layer_input, segment_ids, w_qkv, qv_bias, w_out, out_bias, norm1_gain, norm1_bias, w_up, up_bias, w_down, down_bias, norm2_gain, norm2_bias, out_cotangent):
    floats = [matrix.astype(jnp.float32) for matrix in (layer_input, w_qkv, qv_bias, w_out, out_bias, norm1_gain, norm1_bias, w_up, up_bias, w_down, down_bias, norm2_gain, norm2_bias)]

    def forward_fn(*params):
        return forward(*params, segment_ids)
    output, pullback = jax.vjp(forward_fn, *floats)
    live_mask = (segment_ids >= 0).astype(jnp.float32)
    gradients = pullback(out_cotangent.astype(jnp.float32) * live_mask[:, None])
    return (output.astype(jnp.bfloat16), gradients[0], gradients[1], gradients[2], gradients[3], gradients[4], gradients[5], gradients[6], gradients[7], gradients[8], gradients[9], gradients[10], gradients[11], gradients[12])
```

```python
import jax
import jax.numpy as jnp
from jax import lax
from jax.sharding import PartitionSpec as P

SEQ = 1024


EPSILON = 1e-06
MASKED = -1e30
LOW = jnp.bfloat16
HIGH = jnp.float32


def dot_nn(left, right):
    return lax.dot_general(left, right, (((1,), (0,)), ((), ())), preferred_element_type=HIGH)


def dot_nt(left, right):
    return lax.dot_general(left, right, (((1,), (1,)), ((), ())), preferred_element_type=HIGH)


def dot_tn(left, right):
    return lax.dot_general(left, right, (((0,), (0,)), ((), ())), preferred_element_type=HIGH)


def norm_forward(summed):
    mean = jnp.mean(summed, axis=-1, keepdims=True)
    centred = summed - mean
    spread = jnp.mean(centred * centred, axis=-1, keepdims=True)
    inverse = lax.rsqrt(spread + EPSILON)
    return centred * inverse, inverse


def norm_backward(xhat, inverse, scaled):
    return inverse * (
        scaled
        - jnp.mean(scaled, axis=-1, keepdims=True)
        - xhat * jnp.mean(scaled * xhat, axis=-1, keepdims=True)
    )


def gelu_parts(u):
    phi_cdf = 0.5 * (1.0 + lax.erf(u * (2.0**-0.5)))
    density = jnp.exp(-0.5 * u * u) * 0.3989422804014327
    return u * phi_cdf, phi_cdf + u * density


def column_sum(values):
    return jnp.sum(values, axis=0, keepdims=True)


def on_device(
    layer_input,
    segment_ids,
    w_qkv,
    qv_bias,
    w_out,
    out_bias,
    norm1_gain,
    norm1_bias,
    w_up,
    up_bias,
    w_down,
    down_bias,
    norm2_gain,
    norm2_bias,
    out_cotangent,
):
    n_tensor = lax.axis_size("tensor")
    place = lax.axis_index("tensor")
    n_dp = lax.axis_size("dp")
    dp_place = lax.axis_index("dp")
    tokens, width = layer_input.shape
    share = tokens // n_tensor
    local_heads = qv_bias.shape[0]
    heads = local_heads * n_tensor
    head_dim = qv_bias.shape[1] // 2
    score_scale = float(head_dim) ** (-0.5)
    shares_per_row = SEQ // share
    row_start = (place // shares_per_row) * SEQ
    own_start = place * share
    in_row = (place % shares_per_row) * share

    units = w_up.shape[1]
    qkv_rows = w_qkv.reshape(width, local_heads, 3, head_dim).transpose(2, 1, 3, 0).reshape(-1, width)
    local = jnp.concatenate([qkv_rows, w_out, w_up.T, w_down], axis=0)
    slab = local.shape[0] // n_dp
    mine = lax.dynamic_slice_in_dim(local, dp_place * slab, slab, 0)
    everything = lax.all_gather(mine, ("tensor", "dp"), axis=0, tiled=True)
    everything = everything.reshape(n_tensor, local.shape[0], width)
    local_width = local_heads * head_dim
    q_rows = everything[:, :local_width].reshape(-1, width)
    k_rows = everything[:, local_width : 2 * local_width].reshape(-1, width)
    v_rows = everything[:, 2 * local_width : 3 * local_width].reshape(-1, width)
    at = 3 * local_width
    out_rows = everything[:, at : at + local_width].reshape(-1, width)
    at += local_width
    up_rows = everything[:, at : at + units].reshape(-1, width)
    at += units
    down_rows = everything[:, at : at + units].reshape(-1, width)
    small = jnp.concatenate([qv_bias.reshape(-1), up_bias])
    small = lax.all_gather(small, "tensor", axis=0, tiled=False)
    qv_full = small[:, : local_heads * 2 * head_dim].reshape(heads, 2 * head_dim).astype(HIGH)
    up_bias_full = small[:, local_heads * 2 * head_dim :].reshape(-1).astype(HIGH)
    q_bias = qv_full[:, :head_dim].reshape(-1)
    v_bias = qv_full[:, head_dim:].reshape(-1)

    row_input = lax.dynamic_slice_in_dim(layer_input, row_start, SEQ, 0)
    own_input = lax.dynamic_slice_in_dim(layer_input, own_start, share, 0)
    row_segments = lax.dynamic_slice_in_dim(segment_ids, row_start, SEQ, 0)
    own_segments = lax.dynamic_slice_in_dim(segment_ids, own_start, share, 0)

    queries = (dot_nt(own_input, q_rows) + q_bias).astype(LOW).reshape(share, heads, head_dim)
    keys = dot_nt(row_input, k_rows).astype(LOW).reshape(SEQ, heads, head_dim)
    values = (dot_nt(row_input, v_rows) + v_bias).astype(LOW).reshape(SEQ, heads, head_dim)
    allowed = own_segments[:, None] == row_segments[None, :]
    scores = jnp.einsum("qhd,khd->hqk", queries, keys, preferred_element_type=HIGH) * score_scale
    scores = jnp.where(allowed[None], scores, MASKED)
    top = jnp.max(scores, axis=-1, keepdims=True)
    total = jnp.sum(jnp.exp(scores - top), axis=-1, keepdims=True)
    probability = jnp.exp(scores - (top + jnp.log(total)))
    probability_low = probability.astype(LOW)
    attended = jnp.einsum("hqk,khd->qhd", probability_low, values, preferred_element_type=HIGH)
    attended = attended.astype(LOW).reshape(share, -1)

    first_sum = own_input.astype(HIGH) + dot_nn(attended, out_rows) + out_bias.astype(HIGH)
    gain_first = norm1_gain.astype(HIGH)
    gain_second = norm2_gain.astype(HIGH)
    xhat_first, inverse_first = norm_forward(first_sum)
    hidden = xhat_first * gain_first + norm1_bias.astype(HIGH)
    hidden_low = hidden.astype(LOW)
    up_pre = dot_nt(hidden_low, up_rows) + up_bias_full
    gelu_value, gelu_slope = gelu_parts(up_pre)
    activation = gelu_value.astype(LOW)
    second_sum = hidden + dot_nn(activation, down_rows) + down_bias.astype(HIGH)
    xhat_second, inverse_second = norm_forward(second_sum)
    output = (xhat_second * gain_second + norm2_bias.astype(HIGH)).astype(LOW)

    live = (own_segments >= 0).astype(HIGH)
    cotangent = out_cotangent.astype(HIGH) * live[:, None]
    grad_second = norm_backward(xhat_second, inverse_second, cotangent * gain_second)
    second_low = grad_second.astype(LOW)
    grad_down = dot_tn(activation, second_low)
    grad_up_pre = (dot_nt(second_low, down_rows) * gelu_slope).astype(LOW)
    grad_up = dot_tn(grad_up_pre, hidden_low)
    grad_hidden = grad_second + dot_nn(grad_up_pre, up_rows)
    grad_first = norm_backward(xhat_first, inverse_first, grad_hidden * gain_first)
    first_low = grad_first.astype(LOW)
    grad_out = dot_tn(attended, first_low)
    grad_attended = dot_nt(first_low, out_rows).astype(LOW).reshape(share, heads, head_dim)

    grad_values = jnp.einsum(
        "hqk,qhd->khd", probability_low, grad_attended, preferred_element_type=HIGH
    )
    grad_probs = jnp.einsum("qhd,khd->hqk", grad_attended, values, preferred_element_type=HIGH)
    inner = jnp.sum(probability * grad_probs, axis=-1, keepdims=True)
    grad_raw = (probability * (grad_probs - inner) * score_scale).astype(LOW)
    grad_queries = jnp.einsum("hqk,khd->qhd", grad_raw, keys, preferred_element_type=HIGH)
    grad_keys = jnp.einsum("hqk,qhd->khd", grad_raw, queries, preferred_element_type=HIGH)
    grad_queries = grad_queries.astype(LOW).reshape(share, -1)
    grad_keys = grad_keys.astype(LOW).reshape(SEQ, -1)
    grad_values = grad_values.astype(LOW).reshape(SEQ, -1)
    grad_q_rows = dot_tn(grad_queries, own_input)
    grad_k_rows = dot_tn(grad_keys, row_input)
    grad_v_rows = dot_tn(grad_values, row_input)

    row_term = dot_nn(grad_keys, k_rows) + dot_nn(grad_values, v_rows)
    row_term = row_term.reshape(shares_per_row, share, width)
    my_half = place % shares_per_row
    input_grad = grad_first + dot_nn(grad_queries, q_rows) + row_term[my_half]
    for step in range(1, shares_per_row):
        pairs = [
            (p, (p // shares_per_row) * shares_per_row + (p + step) % shares_per_row)
            for p in range(n_tensor)
        ]
        sent = row_term[(my_half + step) % shares_per_row].astype(LOW)
        input_grad = input_grad + lax.ppermute(sent, "tensor", pairs).astype(HIGH)

    def by_shard(rows):
        return rows.astype(LOW).reshape(n_tensor, -1, width)

    gradients = jnp.concatenate(
        [
            by_shard(grad_q_rows),
            by_shard(grad_k_rows),
            by_shard(grad_v_rows),
            by_shard(grad_out),
            by_shard(grad_up),
            by_shard(grad_down),
        ],
        axis=1,
    )
    rows_all = gradients.shape[1]
    slab = rows_all // n_dp
    gradients = gradients.reshape(n_tensor, n_dp, slab, width).transpose(1, 0, 2, 3)
    part = lax.psum_scatter(gradients.reshape(-1, width), "dp", scatter_dimension=0, tiled=True)
    part = lax.psum_scatter(part, "tensor", scatter_dimension=0, tiled=True)
    summed = lax.all_gather(part, "dp", axis=0, tiled=True).astype(HIGH)
    at = 3 * local_width
    grad_qkv = (
        summed[:at].reshape(3, local_heads, head_dim, width).transpose(3, 1, 0, 2)
    ).reshape(width, local_heads, 3 * head_dim)
    grad_out = summed[at : at + local_width]
    at += local_width
    grad_up = summed[at : at + units].T
    at += units
    grad_down = summed[at : at + units]

    vectors = lax.psum(
        (
            jnp.sum(grad_queries.astype(HIGH), axis=0).reshape(heads, head_dim),
            jnp.sum(grad_values.astype(HIGH), axis=0).reshape(heads, head_dim),
            jnp.sum(grad_up_pre.astype(HIGH), axis=0),
            jnp.sum(grad_first, axis=0),
            jnp.sum(grad_hidden * xhat_first, axis=0),
            jnp.sum(grad_hidden, axis=0),
            jnp.sum(grad_second, axis=0),
            jnp.sum(cotangent * xhat_second, axis=0),
            jnp.sum(cotangent, axis=0),
        ),
        ("dp", "tensor"),
    )
    grad_qv = jnp.concatenate([vectors[0], vectors[1]], axis=1)
    grad_qv_bias = lax.dynamic_slice_in_dim(grad_qv, place * local_heads, local_heads, 0)
    grad_up_bias = lax.dynamic_slice_in_dim(vectors[2], place * units, units, 0)
    return (
        output,
        input_grad,
        grad_qkv,
        grad_qv_bias,
        grad_out,
        vectors[3],
        vectors[4],
        vectors[5],
        grad_up,
        grad_up_bias,
        grad_down,
        vectors[6],
        vectors[7],
        vectors[8],
    )


def solution(mesh):
    return jax.shard_map(
        on_device,
        mesh=mesh,
        in_specs=(
            P("dp", None),
            P("dp"),
            P(None, "tensor", None),
            P("tensor", None),
            P("tensor", None),
            P(),
            P(),
            P(),
            P(None, "tensor"),
            P("tensor"),
            P("tensor", None),
            P(),
            P(),
            P(),
            P(("dp", "tensor"), None),
        ),
        out_specs=(
            P(("dp", "tensor"), None),
            P(("dp", "tensor"), None),
            P(None, "tensor", None),
            P("tensor", None),
            P("tensor", None),
            P(),
            P(),
            P(),
            P(None, "tensor"),
            P("tensor"),
            P("tensor", None),
            P(),
            P(),
            P(),
        ),
        check_vma=False,
    )
```

```python
import functools

import jax
import jax.numpy as jnp
from jax import lax
from jax.experimental import pallas as pl
from jax.experimental.pallas import tpu as pltpu
from jax.sharding import PartitionSpec as P

SEQ = 1024


EPSILON = 1e-06
MASKED = -1e30
LOW = jnp.bfloat16
HIGH = jnp.float32


def dot_nn(left, right):
    return lax.dot_general(left, right, (((1,), (0,)), ((), ())), preferred_element_type=HIGH)


def dot_nt(left, right):
    return lax.dot_general(left, right, (((1,), (1,)), ((), ())), preferred_element_type=HIGH)


def dot_tn(left, right):
    return lax.dot_general(left, right, (((0,), (0,)), ((), ())), preferred_element_type=HIGH)


def norm_forward(summed):
    mean = jnp.mean(summed, axis=-1, keepdims=True)
    centred = summed - mean
    spread = jnp.mean(centred * centred, axis=-1, keepdims=True)
    inverse = lax.rsqrt(spread + EPSILON)
    return centred * inverse, inverse


def norm_backward(xhat, inverse, scaled):
    return inverse * (
        scaled
        - jnp.mean(scaled, axis=-1, keepdims=True)
        - xhat * jnp.mean(scaled * xhat, axis=-1, keepdims=True)
    )


def gelu_parts(u):
    phi_cdf = 0.5 * (1.0 + lax.erf(u * (2.0**-0.5)))
    density = jnp.exp(-0.5 * u * u) * 0.3989422804014327
    return u * phi_cdf, phi_cdf + u * density


def column_sum(values):
    return jnp.sum(values, axis=0, keepdims=True)

MESH = pl.DeviceIdType.MESH
VMEM_LIMIT = 60 * 1024 * 1024


class Place:
    def __init__(self, n_tensor):
        self.z = lax.axis_index("tensor")
        self.dp = lax.axis_index("dp")
        self.core = lax.rem(self.dp, 2)
        self.a = lax.rem(self.dp // 2, 2)
        self.b = lax.rem(self.dp // 4, 2)
        self.to_core = (self.dp + 1 - 2 * self.core, self.z)
        self.to_a = (self.dp + 2 - 4 * self.a, self.z)
        self.to_b = (self.dp + 4 - 8 * self.b, self.z)
        self.others = [lax.rem(self.z + step, n_tensor) for step in range(1, n_tensor)]
        if n_tensor == 4:
            near = self.z + 1 - 2 * lax.rem(self.z, 2)
            upper = self.z // 2
            self.others = [near, 2 - upper, 3 - 3 * upper]

    def partners(self):
        return [self.to_core, self.to_a, self.to_b] + [(self.dp, z) for z in self.others]


def meet(place):
    barrier = pltpu.get_barrier_semaphore()
    partners = place.partners()
    for partner in partners:
        pl.semaphore_signal(barrier, inc=1, device_id=partner, device_id_type=MESH)
    pl.semaphore_wait(barrier, len(partners))


def remote(src, dst, send, recv, target):
    return pltpu.make_async_remote_copy(
        src_ref=src,
        dst_ref=dst,
        send_sem=send,
        recv_sem=recv,
        device_id=target,
        device_id_type=MESH,
    )


class Gather:
    def __init__(self, place, whole, local, send, recv, group):
        self.place, self.whole, self.local = place, whole, local
        self.send, self.recv, self.group = send, recv, group
        self.quarter = whole.shape[1] // 4
        self.half = whole.shape[2] // 2

    def window(self, a, b, side):
        rows = pl.ds(pl.multiple_of((a * 2 + b) * self.quarter, 16), self.quarter)
        return rows, pl.ds(pl.multiple_of(side * self.half, 128), self.half)

    def piece(self, z, a, b, side):
        rows, columns = self.window(a, b, side)
        return self.whole.at[z, rows, columns]

    def sems(self, z, slot):
        return self.send.at[self.group, z, slot], self.recv.at[self.group, z, slot]

    def pass_on(self, z, slot, a, b, side, target):
        part = self.piece(z, a, b, side)
        return remote(part, part, *self.sems(z, slot), target)

    def along(self, z):
        p = self.place
        rows, columns = self.window(p.a, p.b, p.core)
        return remote(
            self.local.at[rows, columns],
            self.whole.at[p.z, rows, columns],
            self.send.at[self.group, z, 0],
            self.recv.at[self.group, p.z, 0],
            (p.dp, z),
        )

    def start(self):
        for z in self.place.others:
            self.along(z).start()

    def first(self, z):
        p = self.place
        self.pass_on(z, 0, p.a, p.b, p.core, p.to_core).wait_recv()
        self.pass_on(z, 1, p.a, p.b, p.core, p.to_a).start()
        self.pass_on(z, 2, p.a, p.b, p.core, p.to_b).start()
        self.pass_on(z, 4, p.a, p.b, p.core, p.to_core).start()

    def turn(self, z):
        p = self.place
        odd = lax.rem(z + self.group, 2)
        a = p.a * odd + (1 - p.a) * (1 - odd)
        b = p.b * (1 - odd) + (1 - p.b) * odd
        target = odd * p.to_a[0] + (1 - odd) * p.to_b[0]
        return self.pass_on(z, 3, a, b, p.core, (target, p.z))

    def second(self, z):
        p = self.place
        self.pass_on(z, 1, 1 - p.a, p.b, p.core, p.to_a).wait_recv()
        self.pass_on(z, 2, p.a, 1 - p.b, p.core, p.to_b).wait_recv()
        self.turn(z).start()
        self.pass_on(z, 5, 1 - p.a, p.b, p.core, p.to_core).start()
        self.pass_on(z, 6, p.a, 1 - p.b, p.core, p.to_core).start()

    def third(self, z):
        p = self.place
        self.pass_on(z, 3, 1 - p.a, 1 - p.b, p.core, p.to_a).wait_recv()
        self.pass_on(z, 7, 1 - p.a, 1 - p.b, p.core, p.to_core).start()

    def last(self, z):
        p = self.place
        side = 1 - p.core
        self.pass_on(z, 4, p.a, p.b, side, p.to_core).wait_recv()
        self.pass_on(z, 5, 1 - p.a, p.b, side, p.to_core).wait_recv()
        self.pass_on(z, 6, p.a, 1 - p.b, side, p.to_core).wait_recv()
        self.pass_on(z, 7, 1 - p.a, 1 - p.b, side, p.to_core).wait_recv()

    def finish(self):
        p = self.place
        for z in p.others:
            self.along(z).wait_send()
            self.pass_on(z, 1, p.a, p.b, p.core, p.to_a).wait_send()
            self.pass_on(z, 2, p.a, p.b, p.core, p.to_b).wait_send()
            self.turn(z).wait_send()
            self.pass_on(z, 4, p.a, p.b, p.core, p.to_core).wait_send()
            self.pass_on(z, 5, 1 - p.a, p.b, p.core, p.to_core).wait_send()
            self.pass_on(z, 6, p.a, 1 - p.b, p.core, p.to_core).wait_send()
            self.pass_on(z, 7, 1 - p.a, 1 - p.b, p.core, p.to_core).wait_send()


def segment_bias(own_segments, row_segments):
    return jnp.where(own_segments == row_segments, 0.0, MASKED)


def gather_attend(
    n_tensor,
    heads,
    scale,
    row_input,
    own_segments,
    row_segments,
    local_a,
    local_b,
    local_c,
    local_small,
    out_a,
    whole_b,
    whole_c,
    small,
    attended,
    queries,
    keys,
    values,
    log_totals,
    whole_a,
    small_land,
    bias,
    mixed,
    send,
    recv,
    small_send,
    small_recv,
    copy_sem,
):
    place = Place(n_tensor)
    share = own_segments.shape[0]
    shares_per_row = row_input.shape[0] // share
    group_rows = local_a.shape[0] // 3
    size = group_rows // heads
    in_row = pl.ds(pl.multiple_of(lax.rem(place.z, shares_per_row) * share, share), share)
    meet(place)
    gather_a = Gather(place, whole_a, local_a, send, recv, 0)
    gather_b = Gather(place, whole_b, local_b, send, recv, 1)
    gather_c = Gather(place, whole_c, local_c, send, recv, 2)

    def small_copy(z):
        return remote(
            local_small, small_land.at[place.z], small_send.at[z], small_recv.at[place.z], (place.dp, z)
        )

    def small_arrival(z):
        return remote(
            local_small, small_land.at[z], small_send.at[z], small_recv.at[z], (place.dp, z)
        )

    for z in place.others:
        small_copy(z).start()
    gather_a.start()
    own_a = pltpu.make_async_copy(local_a, whole_a.at[place.z], copy_sem.at[0])
    own_b = pltpu.make_async_copy(local_b, whole_b.at[place.z], copy_sem.at[1])
    own_c = pltpu.make_async_copy(local_c, whole_c.at[place.z], copy_sem.at[2])
    own_a.start()
    small_land[place.z] = local_small[...]
    bias[...] = segment_bias(own_segments[...], row_segments[...])
    own_a.wait()

    def save_a(z, slot):
        return pltpu.make_async_copy(whole_a.at[z], out_a.at[z], copy_sem.at[slot])

    def attend(z, between):
        weights = whole_a[z]
        q_bias = small_land[z, 0:1, :group_rows]
        v_bias = small_land[z, 1:2, :group_rows]
        q = dot_nt(row_input[in_row], weights[:group_rows]) + q_bias
        q = q.astype(LOW)
        k = dot_nt(row_input[...], weights[group_rows : 2 * group_rows]).astype(LOW)
        v = (dot_nt(row_input[...], weights[2 * group_rows :]) + v_bias).astype(LOW)
        for head in range(heads):
            part = slice(head * size, (head + 1) * size)
            queries[z, head] = q[:, part] * scale
            keys[z, head] = k[:, part]
            values[z, head] = v[:, part]

        def one_head(head, carry):
            chunk = min(256, share)
            for at in range(0, share, chunk):
                rows = pl.ds(at, chunk)
                scores = dot_nt(queries[z, head, rows], keys[z, head]) + bias[rows]
                top = jnp.max(scores, axis=-1, keepdims=True)
                raised = jnp.exp(scores - top)
                total = jnp.sum(raised, axis=-1, keepdims=True)
                summed = dot_nn(raised.astype(LOW), values[z, head])
                mixed[head, rows] = (summed / total).astype(LOW)
                log_totals[z, head, rows] = top + jnp.log(total)
            for at, service in enumerate(between):
                pl.when(head == at)(service)
            return carry

        lax.fori_loop(0, heads, one_head, 0)
        attended[z] = jnp.concatenate([mixed[head] for head in range(heads)], axis=-1)

    near, middle, far = place.others

    def services(*steps):
        def run():
            for step, z in steps:
                step(z)

        return run

    def start_b():
        gather_b.start()
        own_b.start()

    def start_c():
        gather_c.start()
        own_c.start()

    attend(place.z, [start_b, start_c])
    save_a(place.z, 3).start()
    for z in place.others:
        gather_a.first(z)
    for z in place.others:
        gather_a.second(z)
    for z in place.others:
        gather_a.third(z)
        small_arrival(z).wait_recv()
    gather_a.last(near)
    attend(
        near,
        [
            services((gather_b.first, near)),
            services((gather_b.first, middle)),
            services((gather_b.second, near), (gather_b.first, far)),
        ],
    )
    save_a(near, 4).start()
    gather_a.last(middle)
    attend(
        middle,
        [
            services((gather_b.third, near), (gather_b.second, middle), (gather_c.first, near)),
            services((gather_b.second, far), (gather_b.third, middle)),
            services((gather_b.third, far), (gather_c.first, middle), (gather_c.second, near)),
        ],
    )
    save_a(middle, 5).start()
    gather_a.last(far)
    attend(
        far,
        [
            services((gather_c.first, far)),
            services((gather_c.second, middle), (gather_c.third, near)),
            services(),
        ],
    )
    save_a(far, 6).start()
    gather_c.second(far)
    gather_c.third(middle)
    gather_c.third(far)
    small[...] = small_land[...]
    for z in place.others:
        gather_b.last(z)
        gather_c.last(z)
        small_copy(z).wait_send()
    for gather in (gather_a, gather_b, gather_c):
        gather.finish()
    own_b.wait()
    own_c.wait()
    for slot, z in enumerate([place.z] + place.others):
        save_a(z, 3 + slot).wait()


def attend_back(
    n_tensor,
    heads,
    scale,
    row_input,
    own_segments,
    row_segments,
    first_low,
    whole_a,
    whole_out,
    queries,
    keys,
    values,
    log_totals,
    grad_a,
    bias_sums,
    own_term,
    row_term,
    bias,
    grad_mixed,
    grad_q,
    grad_k,
    grad_v,
):
    z_here = lax.axis_index("tensor")
    share = own_segments.shape[0]
    shares_per_row = row_input.shape[0] // share
    group_rows = whole_a.shape[1] // 3
    size = group_rows // heads
    in_row = pl.ds(pl.multiple_of(lax.rem(z_here, shares_per_row) * share, share), share)
    bias[...] = segment_bias(own_segments[...], row_segments[...])
    own_term[...] = jnp.zeros_like(own_term)
    row_term[...] = jnp.zeros_like(row_term)

    def one_shard(z, carry):
        incoming = dot_nt(first_low[...], whole_out[z]).astype(LOW)
        for head in range(heads):
            grad_mixed[head] = incoming[:, head * size : (head + 1) * size]

        def one_head(head, inner):
            q, k, v = queries[z, head], keys[z, head], values[z, head]
            up = grad_mixed[head]
            chance = jnp.exp(dot_nt(q, k) + bias[...] - log_totals[z, head])
            change = chance * dot_nt(up, v)
            change = change - chance * jnp.sum(change, axis=-1, keepdims=True)
            change = change.astype(LOW)
            grad_q[head] = (dot_nn(change, k) * scale).astype(LOW)
            grad_k[head] = dot_nn(q.T, change).astype(LOW)
            grad_v[head] = dot_nn(up.T, chance.astype(LOW)).astype(LOW)
            return inner

        lax.fori_loop(0, heads, one_head, 0)
        dq = jnp.concatenate([grad_q[head] for head in range(heads)], axis=-1)
        dk = grad_k[...].reshape(group_rows, -1)
        dv = grad_v[...].reshape(group_rows, -1)
        x_own, x_row = row_input[in_row], row_input[...]
        grad_a[z, :group_rows] = dot_tn(dq, x_own).astype(LOW)
        grad_a[z, group_rows : 2 * group_rows] = dot_nn(dk, x_row).astype(LOW)
        grad_a[z, 2 * group_rows :] = dot_nn(dv, x_row).astype(LOW)
        weights = whole_a[z]
        own_term[...] += dot_nn(dq, weights[:group_rows])
        row_term[...] += dot_tn(
            jnp.concatenate([dk, dv], axis=0), weights[group_rows:]
        )
        ones = jnp.ones((8, x_row.shape[0]), LOW)
        bias_sums[z, 0:8, :group_rows] = dot_nn(ones[:, :share], dq)
        bias_sums[z, 8:16, :group_rows] = dot_nt(ones, dv)
        return carry

    lax.fori_loop(0, n_tensor, one_shard, 0)


def on_device(
    layer_input,
    segment_ids,
    w_qkv,
    qv_bias,
    w_out,
    out_bias,
    norm1_gain,
    norm1_bias,
    w_up,
    up_bias,
    w_down,
    down_bias,
    norm2_gain,
    norm2_bias,
    out_cotangent,
):
    n_tensor = lax.axis_size("tensor")
    place = lax.axis_index("tensor")
    n_dp = lax.axis_size("dp")
    dp_place = lax.axis_index("dp")
    tokens, width = layer_input.shape
    share = tokens // n_tensor
    local_heads = qv_bias.shape[0]
    heads = local_heads * n_tensor
    head_dim = qv_bias.shape[1] // 2
    score_scale = float(head_dim) ** (-0.5)
    shares_per_row = SEQ // share
    row_start = (place // shares_per_row) * SEQ
    own_start = place * share
    in_row = (place % shares_per_row) * share

    units = w_up.shape[1]
    local_width = local_heads * head_dim
    local_a = w_qkv.reshape(width, local_heads, 3, head_dim).transpose(2, 1, 3, 0).reshape(-1, width)
    local_b = jnp.concatenate([w_out, w_up], axis=0)
    local_c = w_down
    local_small = jnp.zeros((8, width), HIGH)
    local_small = local_small.at[0, :local_width].set(qv_bias[:, :head_dim].reshape(-1).astype(HIGH))
    local_small = local_small.at[1, :local_width].set(qv_bias[:, head_dim:].reshape(-1).astype(HIGH))
    local_small = local_small.at[2, :units].set(up_bias.astype(HIGH))

    row_input = lax.dynamic_slice_in_dim(layer_input, row_start, SEQ, 0)
    own_input = lax.dynamic_slice_in_dim(layer_input, own_start, share, 0)
    row_segments = lax.dynamic_slice_in_dim(segment_ids, row_start, SEQ, 0)
    own_segments = lax.dynamic_slice_in_dim(segment_ids, own_start, share, 0)

    own_column, row_line = own_segments[:, None], row_segments[None, :]
    vmem = pl.BlockSpec(memory_space=pltpu.VMEM)
    anywhere = pl.BlockSpec(memory_space=pl.ANY)
    shape_a = (n_tensor,) + local_a.shape
    shape_b = (n_tensor,) + local_b.shape
    shape_c = (n_tensor,) + local_c.shape
    per_head = (n_tensor, local_heads)
    whole_a, whole_b, whole_c, small, attended, queries, keys, values, log_totals = pl.pallas_call(
        functools.partial(gather_attend, n_tensor, local_heads, score_scale),
        out_shape=(
            jax.ShapeDtypeStruct(shape_a, LOW),
            jax.ShapeDtypeStruct(shape_b, LOW),
            jax.ShapeDtypeStruct(shape_c, LOW),
            jax.ShapeDtypeStruct((n_tensor,) + local_small.shape, HIGH),
            jax.ShapeDtypeStruct((n_tensor, share, local_width), LOW),
            jax.ShapeDtypeStruct(per_head + (share, head_dim), LOW),
            jax.ShapeDtypeStruct(per_head + (SEQ, head_dim), LOW),
            jax.ShapeDtypeStruct(per_head + (SEQ, head_dim), LOW),
            jax.ShapeDtypeStruct(per_head + (share, 1), HIGH),
        ),
        in_specs=[vmem, vmem, vmem, anywhere, anywhere, anywhere, vmem],
        out_specs=(anywhere, anywhere, anywhere, vmem, vmem, vmem, vmem, vmem, vmem),
        scratch_shapes=[
            pltpu.VMEM(shape_a, LOW),
            pltpu.VMEM((n_tensor,) + local_small.shape, HIGH),
            pltpu.VMEM((share, SEQ), HIGH),
            pltpu.VMEM((local_heads, share, head_dim), LOW),
            pltpu.SemaphoreType.DMA((3, n_tensor, 8)),
            pltpu.SemaphoreType.DMA((3, n_tensor, 8)),
            pltpu.SemaphoreType.DMA((n_tensor,)),
            pltpu.SemaphoreType.DMA((n_tensor,)),
            pltpu.SemaphoreType.DMA((8,)),
        ],
        compiler_params=pltpu.CompilerParams(
            collective_id=0, has_side_effects=True, vmem_limit_bytes=VMEM_LIMIT
        ),
        name="gather_attend",
    )(row_input, own_column, row_line, local_a, local_b, local_c, local_small)
    out_rows = whole_b[:, :local_width]
    up_cols = whole_b[:, local_width:]
    down_rows = whole_c
    up_bias_full = small[:, 2, :units]

    first_sum = own_input.astype(HIGH) + out_bias.astype(HIGH)
    for z in range(n_tensor):
        first_sum = first_sum + dot_nn(attended[z], out_rows[z])
    gain_first = norm1_gain.astype(HIGH)
    gain_second = norm2_gain.astype(HIGH)
    xhat_first, inverse_first = norm_forward(first_sum)
    hidden = xhat_first * gain_first + norm1_bias.astype(HIGH)
    hidden_low = hidden.astype(LOW)
    second_sum = hidden + down_bias.astype(HIGH)
    slopes, activations = [], []
    for z in range(n_tensor):
        gelu_value, gelu_slope = gelu_parts(dot_nn(hidden_low, up_cols[z]) + up_bias_full[z])
        activations.append(gelu_value.astype(LOW))
        slopes.append(gelu_slope)
        second_sum = second_sum + dot_nn(activations[z], down_rows[z])
    xhat_second, inverse_second = norm_forward(second_sum)
    output = (xhat_second * gain_second + norm2_bias.astype(HIGH)).astype(LOW)

    live = (own_segments >= 0).astype(HIGH)
    cotangent = out_cotangent.astype(HIGH) * live[:, None]
    grad_second = norm_backward(xhat_second, inverse_second, cotangent * gain_second)
    second_low = grad_second.astype(LOW)
    grad_hidden = grad_second
    grads_up, grads_down, grad_ups = [], [], []
    for z in range(n_tensor):
        grads_down.append(dot_tn(activations[z], second_low).astype(LOW))
        grad_up_pre = (dot_nt(second_low, down_rows[z]) * slopes[z]).astype(LOW)
        grads_up.append(dot_tn(hidden_low, grad_up_pre).astype(LOW))
        grad_hidden = grad_hidden + dot_nt(grad_up_pre, up_cols[z])
        grad_ups.append(jnp.sum(grad_up_pre.astype(HIGH), axis=0))
    grad_first = norm_backward(xhat_first, inverse_first, grad_hidden * gain_first)
    first_low = grad_first.astype(LOW)
    grads_out = [dot_tn(attended[z], first_low).astype(LOW) for z in range(n_tensor)]

    grad_a, bias_sums, own_term, row_term = pl.pallas_call(
        functools.partial(attend_back, n_tensor, local_heads, score_scale),
        out_shape=(
            jax.ShapeDtypeStruct(shape_a, LOW),
            jax.ShapeDtypeStruct((n_tensor, 16, width), HIGH),
            jax.ShapeDtypeStruct((share, width), HIGH),
            jax.ShapeDtypeStruct((SEQ, width), HIGH),
        ),
        in_specs=[vmem] * 10,
        out_specs=(vmem,) * 4,
        scratch_shapes=[
            pltpu.VMEM((share, SEQ), HIGH),
            pltpu.VMEM((local_heads, share, head_dim), LOW),
            pltpu.VMEM((local_heads, share, head_dim), LOW),
            pltpu.VMEM((local_heads, head_dim, SEQ), LOW),
            pltpu.VMEM((local_heads, head_dim, SEQ), LOW),
        ],
        compiler_params=pltpu.CompilerParams(vmem_limit_bytes=VMEM_LIMIT),
        name="attend_back",
    )(
        row_input, own_column, row_line, first_low, whole_a, out_rows, queries, keys, values, log_totals
    )

    row_term = row_term.reshape(shares_per_row, share, width)
    my_half = place % shares_per_row
    input_grad = grad_first + own_term + row_term[my_half]
    for step in range(1, shares_per_row):
        pairs = [
            (p, (p // shares_per_row) * shares_per_row + (p + step) % shares_per_row)
            for p in range(n_tensor)
        ]
        sent = row_term[(my_half + step) % shares_per_row].astype(LOW)
        input_grad = input_grad + lax.ppermute(sent, "tensor", pairs).astype(HIGH)

    gradients = jnp.stack(
        [
            jnp.concatenate([grad_a[z], grads_out[z], grads_up[z], grads_down[z]], axis=0)
            for z in range(n_tensor)
        ]
    )
    rows_all = gradients.shape[1]
    slab = rows_all // n_dp
    gradients = gradients.reshape(n_tensor, n_dp, slab, width).transpose(1, 0, 2, 3)
    part = lax.psum_scatter(gradients.reshape(-1, width), "dp", scatter_dimension=0, tiled=True)
    part = lax.psum_scatter(part, "tensor", scatter_dimension=0, tiled=True)
    summed = lax.all_gather(part, "dp", axis=0, tiled=True).astype(HIGH)
    at = 3 * local_width
    grad_qkv = (
        summed[:at].reshape(3, local_heads, head_dim, width).transpose(3, 1, 0, 2)
    ).reshape(width, local_heads, 3 * head_dim)
    grad_out = summed[at : at + local_width]
    at += local_width
    grad_up = summed[at : at + width]
    at += width
    grad_down = summed[at : at + units]

    vectors = lax.psum(
        (
            bias_sums[:, 0, :local_width].reshape(heads, head_dim),
            bias_sums[:, 8, :local_width].reshape(heads, head_dim),
            jnp.concatenate(grad_ups),
            jnp.sum(grad_first, axis=0),
            jnp.sum(grad_hidden * xhat_first, axis=0),
            jnp.sum(grad_hidden, axis=0),
            jnp.sum(grad_second, axis=0),
            jnp.sum(cotangent * xhat_second, axis=0),
            jnp.sum(cotangent, axis=0),
        ),
        ("dp", "tensor"),
    )
    grad_qv = jnp.concatenate([vectors[0], vectors[1]], axis=1)
    grad_qv_bias = lax.dynamic_slice_in_dim(grad_qv, place * local_heads, local_heads, 0)
    grad_up_bias = lax.dynamic_slice_in_dim(vectors[2], place * units, units, 0)
    return (
        output,
        input_grad,
        grad_qkv,
        grad_qv_bias,
        grad_out,
        vectors[3],
        vectors[4],
        vectors[5],
        grad_up,
        grad_up_bias,
        grad_down,
        vectors[6],
        vectors[7],
        vectors[8],
    )


def solution(mesh):
    return jax.shard_map(
        on_device,
        mesh=mesh,
        in_specs=(
            P("dp", None),
            P("dp"),
            P(None, "tensor", None),
            P("tensor", None),
            P("tensor", None),
            P(),
            P(),
            P(),
            P(None, "tensor"),
            P("tensor"),
            P("tensor", None),
            P(),
            P(),
            P(),
            P(("dp", "tensor"), None),
        ),
        out_specs=(
            P(("dp", "tensor"), None),
            P(("dp", "tensor"), None),
            P(None, "tensor", None),
            P("tensor", None),
            P("tensor", None),
            P(),
            P(),
            P(),
            P(None, "tensor"),
            P("tensor"),
            P("tensor", None),
            P(),
            P(),
            P(),
        ),
        check_vma=False,
    )
```

```python
import functools

import jax
import jax.numpy as jnp
from jax import lax
from jax.experimental import pallas as pl
from jax.experimental.pallas import tpu as pltpu
from jax.sharding import PartitionSpec as P

SEQ = 1024


EPSILON = 1e-06
MASKED = -1e30
LOW = jnp.bfloat16
HIGH = jnp.float32
MESH = pl.DeviceIdType.MESH
VMEM_LIMIT = 60 * 1024 * 1024


def dot_nn(left, right):
    return lax.dot_general(left, right, (((1,), (0,)), ((), ())), preferred_element_type=HIGH)


def dot_nt(left, right):
    return lax.dot_general(left, right, (((1,), (1,)), ((), ())), preferred_element_type=HIGH)


def dot_tn(left, right):
    return lax.dot_general(left, right, (((0,), (0,)), ((), ())), preferred_element_type=HIGH)


def norm_forward(summed):
    mean = jnp.mean(summed, axis=-1, keepdims=True)
    centred = summed - mean
    spread = jnp.mean(centred * centred, axis=-1, keepdims=True)
    inverse = lax.rsqrt(spread + EPSILON)
    return centred * inverse, inverse


def norm_backward(xhat, inverse, scaled):
    return inverse * (
        scaled
        - jnp.mean(scaled, axis=-1, keepdims=True)
        - xhat * jnp.mean(scaled * xhat, axis=-1, keepdims=True)
    )


def gelu_parts(u):
    phi_cdf = 0.5 * (1.0 + lax.erf(u * (2.0**-0.5)))
    density = jnp.exp(-0.5 * u * u) * 0.3989422804014327
    return u * phi_cdf, phi_cdf + u * density


def column_sum(values):
    return jnp.sum(values, axis=0, keepdims=True)


def segment_bias(own_segments, row_segments):
    return jnp.where(own_segments == row_segments, 0.0, MASKED)


class Place:
    def __init__(self, n_tensor):
        self.n_tensor = n_tensor
        self.z = lax.axis_index("tensor")
        self.dp = lax.axis_index("dp")
        self.core = lax.rem(self.dp, 2)
        self.a = lax.rem(self.dp // 2, 2)
        self.b = lax.rem(self.dp // 4, 2)
        self.to_core = (self.dp + 1 - 2 * self.core, self.z)
        self.to_a = (self.dp + 2 - 4 * self.a, self.z)
        self.to_b = (self.dp + 4 - 8 * self.b, self.z)
        self.others = [lax.rem(self.z + step, n_tensor) for step in range(1, n_tensor)]
        if n_tensor == 4:
            near = self.z + 1 - 2 * lax.rem(self.z, 2)
            upper = self.z // 2
            self.others = [near, 2 - upper, 3 - 3 * upper]

    def pick(self, at, order):
        chosen = order[0]
        for index in range(1, len(order)):
            chosen = jnp.where(at == index, order[index], chosen)
        return chosen


def meet(partners):
    barrier = pltpu.get_barrier_semaphore()
    for partner in partners:
        pl.semaphore_signal(barrier, inc=1, device_id=partner, device_id_type=MESH)
    pl.semaphore_wait(barrier, len(partners))


def remote(src, dst, send, recv, target):
    return pltpu.make_async_remote_copy(
        src_ref=src,
        dst_ref=dst,
        send_sem=send,
        recv_sem=recv,
        device_id=target,
        device_id_type=MESH,
    )


class Spread:
    def __init__(self, place, whole, send, recv, group):
        self.place, self.whole, self.send, self.recv, self.group = place, whole, send, recv, group
        self.mine = None
        self.quarter = whole.shape[2] // 4
        self.half = whole.shape[3] // 2

    def odd(self, z):
        return lax.rem(z + self.group, 2)

    def piece(self, z, a, b, side):
        odd = self.odd(z)
        row = odd * (2 * b + a) + (1 - odd) * (2 * a + b)
        rows = pl.ds(pl.multiple_of(row * self.quarter, 16), self.quarter)
        return self.whole.at[self.group, z, rows, pl.ds(pl.multiple_of(side * self.half, 128), self.half)]

    def pass_on(self, z, slot, a, b, side, target):
        part = self.piece(z, a, b, side)
        send = self.send.at[self.group, z, slot]
        recv = self.recv.at[self.group, z, slot % 8]
        source = self.mine if self.mine is not None and slot in (1, 2, 4) else part
        return remote(source, part, send, recv, target)

    def turn(self, z):
        p = self.place
        odd = self.odd(z)
        a = p.a * odd + (1 - p.a) * (1 - odd)
        b = p.b * (1 - odd) + (1 - p.b) * odd
        target = odd * p.to_a[0] + (1 - odd) * p.to_b[0]
        return self.pass_on(z, 3, a, b, p.core, (target, p.z))

    def hand_out(self, z):
        p = self.place
        self.pass_on(z, 1, p.a, p.b, p.core, p.to_a).start()
        self.pass_on(z, 2, p.a, p.b, p.core, p.to_b).start()
        self.pass_on(z, 4, p.a, p.b, p.core, p.to_core).start()

    def second(self, z):
        p = self.place
        self.pass_on(z, 1, 1 - p.a, p.b, p.core, p.to_a).wait_recv()
        self.pass_on(z, 2, p.a, 1 - p.b, p.core, p.to_b).wait_recv()
        self.turn(z).start()
        self.pass_on(z, 5, 1 - p.a, p.b, p.core, p.to_core).start()
        self.pass_on(z, 6, p.a, 1 - p.b, p.core, p.to_core).start()

    def third(self, z):
        p = self.place
        self.pass_on(z, 3, 1 - p.a, 1 - p.b, p.core, p.to_a).wait_recv()
        self.pass_on(z, 7, 1 - p.a, 1 - p.b, p.core, p.to_core).start()

    def last(self, z):
        p = self.place
        side = 1 - p.core
        self.pass_on(z, 4, p.a, p.b, side, p.to_core).wait_recv()
        self.pass_on(z, 5, 1 - p.a, p.b, side, p.to_core).wait_recv()
        self.pass_on(z, 6, p.a, 1 - p.b, side, p.to_core).wait_recv()
        self.pass_on(z, 7, 1 - p.a, 1 - p.b, side, p.to_core).wait_recv()

    def sent(self, z):
        p = self.place
        self.pass_on(z, 1, p.a, p.b, p.core, p.to_a).wait_send()
        self.pass_on(z, 2, p.a, p.b, p.core, p.to_b).wait_send()
        self.turn(z).wait_send()
        self.pass_on(z, 4, p.a, p.b, p.core, p.to_core).wait_send()
        self.pass_on(z, 5, 1 - p.a, p.b, p.core, p.to_core).wait_send()
        self.pass_on(z, 6, p.a, 1 - p.b, p.core, p.to_core).wait_send()
        self.pass_on(z, 7, 1 - p.a, 1 - p.b, p.core, p.to_core).wait_send()


class Gather(Spread):
    def along(self, z):
        p = self.place
        part = self.piece(p.z, p.a, p.b, p.core)
        send, recv = self.send.at[self.group, z, 0], self.recv.at[self.group, p.z, 0]
        return remote(part, part, send, recv, (p.dp, z))

    def onward(self, z):
        p = self.place
        target = jnp.where(z < p.z, p.z + 1, p.z - 1)
        copy = self.pass_on(z, 8, p.a, p.b, p.core, (p.dp, target))
        return (target >= 0) & (target < p.n_tensor), copy

    def start(self):
        p = self.place
        for z in (p.z - 1, p.z + 1):
            pl.when((z >= 0) & (z < p.n_tensor))(self.along(z).start)

    def first(self, z):
        p = self.place
        self.pass_on(z, 0, p.a, p.b, p.core, p.to_core).wait_recv()
        there, copy = self.onward(z)
        pl.when(there)(copy.start)
        self.hand_out(z)

    def finish(self):
        p = self.place
        for z in (p.z - 1, p.z + 1):
            pl.when((z >= 0) & (z < p.n_tensor))(self.along(z).wait_send)
        for z in p.others:
            there, copy = self.onward(z)
            pl.when(there)(copy.wait_send)
            self.sent(z)


def forward_kernel(
    n_tensor,
    heads,
    scale,
    layer_input,
    own_segments,
    row_segments,
    local_a,
    w_up,
    w_down,
    local_small,
    vectors,
    out_w,
    out_q,
    out_k,
    out_v,
    out_totals,
    out_attended,
    out_activation,
    out_slope,
    small,
    hidden_low,
    xhat,
    inverse,
    second_sum,
    weights,
    row_input,
    bias,
    q_all,
    k_all,
    v_all,
    totals,
    attended,
    activation,
    slope,
    queries,
    keys,
    values,
    mixed,
    send,
    recv,
    small_send,
    small_recv,
    copy_sem,
    save_sem,
):
    place = Place(n_tensor)
    share = own_segments.shape[0]
    length = row_input.shape[0]
    shares_per_row = length // share
    width = row_input.shape[1]
    group_rows = q_all.shape[2]
    size = group_rows // heads
    in_row = pl.ds(pl.multiple_of(lax.rem(place.z, shares_per_row) * share, share), share)
    row_start = pl.multiple_of(place.z // shares_per_row * length, length)
    near, middle, far = place.others

    own = [
        pltpu.make_async_copy(source, weights.at[group, place.z], copy_sem.at[group])
        for group, source in enumerate((local_a, w_up, w_down))
    ]
    load_input = pltpu.make_async_copy(
        layer_input.at[pl.ds(row_start, length)], row_input, copy_sem.at[3]
    )
    for copy in own:
        copy.start()
    load_input.start()
    meet([place.to_core, place.to_a, place.to_b] + [(place.dp, z) for z in place.others])
    gathers = [Gather(place, weights, send, recv, group) for group in range(3)]
    gather_a, gather_b, gather_c = gathers

    def small_copy(z):
        sems = small_send.at[z], small_recv.at[place.z]
        return remote(local_small, small.at[place.z], *sems, (place.dp, z))

    def small_arrival(z):
        return remote(local_small, small.at[z], small_send.at[z], small_recv.at[z], (place.dp, z))

    own[0].wait()
    gather_a.start()
    for z in place.others:
        small_copy(z).start()
    own[1].wait()
    gather_b.start()
    own[2].wait()
    gather_c.start()
    small[place.z] = local_small[...]
    bias[...] = segment_bias(own_segments[...], row_segments[...])
    load_input.wait()

    saves = []

    def save(source, target):
        copy = pltpu.make_async_copy(source, target, save_sem.at[len(saves)])
        copy.start()
        saves.append(copy)

    def attend(z, between):
        weight = weights.at[0, z]
        q_bias = small[z, 0:1, :group_rows]
        v_bias = small[z, 1:2, :group_rows]
        x_row = row_input[...]
        q = dot_nt(row_input[in_row], weight[:group_rows]) + q_bias
        q = q.astype(LOW) * scale
        k = dot_nt(x_row, weight[group_rows : 2 * group_rows]).astype(LOW)
        v = (dot_nt(x_row, weight[2 * group_rows : 3 * group_rows]) + v_bias).astype(LOW)
        q_all[z], k_all[z], v_all[z] = q, k, v
        for head in range(heads):
            part = slice(head * size, (head + 1) * size)
            queries[head], keys[head], values[head] = q[:, part], k[:, part], v[:, part]

        def one_head(head, carry):
            chunk = min(256, share)
            for at in range(0, share, chunk):
                rows = pl.ds(at, chunk)
                scores = dot_nt(queries[head, rows], keys[head]) + bias[rows]
                top = jnp.max(scores, axis=-1, keepdims=True)
                raised = jnp.exp(scores - top)
                total = jnp.sum(raised, axis=-1, keepdims=True)
                summed = dot_nn(raised.astype(LOW), values[head])
                mixed[head, rows] = (summed / total).astype(LOW)
                totals[z, head, rows] = top + jnp.log(total)
            for at, service in enumerate(between):
                pl.when(head == at)(service)
            return carry

        lax.fori_loop(0, heads, one_head, 0)
        attended[z] = jnp.concatenate([mixed[head] for head in range(heads)], axis=-1)
        save(weights.at[0, z], out_w.at[0, z])
        save(q_all.at[z], out_q.at[z])
        save(k_all.at[z], out_k.at[z])
        save(v_all.at[z], out_v.at[z])
        save(totals.at[z], out_totals.at[z])
        save(attended.at[z], out_attended.at[z])

    def services(*steps):
        def run():
            for step, z in steps:
                step(z)

        return run

    attend(place.z, [])
    save(weights.at[1, place.z], out_w.at[1, place.z])
    save(weights.at[2, place.z], out_w.at[2, place.z])
    services(
        (gather_a.first, near),
        (gather_a.first, middle),
        (gather_a.second, near),
        (gather_a.first, far),
        (gather_a.second, middle),
        (gather_a.third, near),
        (gather_b.first, near),
        (gather_a.second, far),
        (gather_a.third, middle),
        (gather_c.first, near),
        (gather_a.third, far),
        (gather_b.second, near),
        (gather_b.first, middle),
        (gather_a.last, near),
    )()
    for z in place.others:
        small_arrival(z).wait_recv()
    attend(
        near,
        [
            services((gather_c.second, near), (gather_c.first, middle)),
            services((gather_b.third, near), (gather_b.second, middle)),
            services((gather_c.third, near), (gather_b.first, far)),
        ],
    )
    gather_a.last(middle)
    attend(
        middle,
        [
            services((gather_c.second, middle), (gather_c.first, far)),
            services((gather_b.third, middle)),
            services((gather_b.second, far)),
        ],
    )
    gather_a.last(far)
    attend(
        far,
        [
            services((gather_c.third, middle)),
            services((gather_c.second, far)),
            services((gather_b.third, far)),
        ],
    )

    out_bias, gain, shift, down_bias = (vectors[at : at + 1] for at in range(4))
    first_sum = row_input[in_row].astype(HIGH) + out_bias
    for z in range(n_tensor):
        first_sum = first_sum + dot_nn(attended[z], weights[0, z, 3 * group_rows :])
    normed, spread = norm_forward(first_sum)
    xhat[...] = normed
    inverse[...] = spread
    hidden = normed * gain + shift
    hidden_low[...] = hidden.astype(LOW)
    second_sum[...] = hidden + down_bias

    order = [place.z] + place.others

    def one_shard(at, carry):
        z = place.pick(at, order)

        @pl.when(at > 0)
        def _():
            pl.when(at == 1)(services((gather_c.third, far)))
            gather_b.last(z)
            gather_c.last(z)

        raw = dot_nn(hidden_low[...], weights[1, z]) + small[z, 2:3]
        value, rise = gelu_parts(raw)
        activation[z] = value.astype(LOW)
        slope[z] = rise.astype(LOW)
        second_sum[...] += dot_nn(activation[z], weights[2, z])
        return carry

    lax.fori_loop(0, n_tensor, one_shard, 0)
    for z in place.others:
        save(weights.at[1, z], out_w.at[1, z])
        save(weights.at[2, z], out_w.at[2, z])
    save(activation, out_activation)
    save(slope, out_slope)
    for z in place.others:
        small_copy(z).wait_send()
    for gather in gathers:
        gather.finish()
    for copy in saves:
        copy.wait()


class Reduce:
    def __init__(self, place, grads, lands, pieces, send, recv, wide, group):
        self.place, self.grads, self.pieces = place, grads, pieces
        self.wide_flips, self.wide_out, self.wide_land, self.wide_send, self.wide_recv = wide
        self.core_land, self.first_land, self.second_land, self.far_land = lands
        self.send, self.recv, self.group = send, recv, group
        self.half = grads.shape[2] // 2
        self.quarter = grads.shape[2] // 4
        self.side = grads.shape[3] // 2

    def columns(self, side):
        return pl.ds(pl.multiple_of(side * self.side, 128), self.side)

    def axes(self, z):
        p = self.place
        odd = lax.rem(z + self.group, 2)
        ahead, behind = odd * p.b + (1 - odd) * p.a, odd * p.a + (1 - odd) * p.b
        to_first = odd * p.to_b[0] + (1 - odd) * p.to_a[0]
        to_second = odd * p.to_a[0] + (1 - odd) * p.to_b[0]
        return ahead, behind, (to_first, p.z), (to_second, p.z)

    def rows(self, start, size):
        return pl.ds(pl.multiple_of(start, 16), size)

    def copy(self, z, slot, source, target_ref, target):
        send, recv = self.send.at[self.group, z, slot], self.recv.at[self.group, z, slot]
        return remote(source, target_ref, send, recv, target)

    def core_copy(self, z):
        p, group = self.place, self.group
        source = self.grads.at[group, z, :, self.columns(1 - p.core)]
        return self.copy(z, 0, source, self.core_land.at[group, z], p.to_core)

    def first_copy(self, z):
        ahead, _, target, _ = self.axes(z)
        source = self.core_land.at[self.group, z, self.rows((1 - ahead) * self.half, self.half)]
        return self.copy(z, 1, source, self.first_land.at[self.group, z], target)

    def second_copy(self, z):
        ahead, behind, _, target = self.axes(z)
        start = ahead * self.half + (1 - behind) * self.quarter
        source = self.core_land.at[self.group, z, self.rows(start, self.quarter)]
        return self.copy(z, 2, source, self.second_land.at[self.group, z], target)

    def kept(self, z):
        ahead, behind, _, _ = self.axes(z)
        return self.rows(ahead * self.half + behind * self.quarter, self.quarter)

    def far_copy(self, z):
        p, group = self.place, self.group
        source = self.core_land.at[group, z, self.kept(z)]
        send, recv = self.send.at[group, z, 3], self.recv.at[group, p.z, 3]
        return remote(source, self.far_land.at[group, p.z], send, recv, (p.dp, z))

    def far_arrival(self, z):
        p, group = self.place, self.group
        land = self.far_land.at[group, z]
        return remote(land, land, self.send.at[group, z, 3], self.recv.at[group, z, 3], (p.dp, z))

    def wide_copy(self, at):
        group = self.group
        sems = self.wide_send.at[group, at], self.wide_recv.at[group, at]
        target = (self.wide_flips[at], self.place.z)
        return remote(self.wide_out.at[group, at], self.wide_land.at[group, at], *sems, target)

    def start(self, z):
        self.core_copy(z).start()

    def add(self, target, rows, other):
        target[rows] = (target[rows].astype(HIGH) + other.astype(HIGH)).astype(LOW)

    def first(self, z):
        p = self.place
        self.core_copy(z).wait_recv()
        mine = self.grads[self.group, z, :, self.columns(p.core)]
        land = self.core_land.at[self.group, z]
        self.add(land, slice(None), mine)
        self.first_copy(z).start()

    def second(self, z):
        ahead, _, _, _ = self.axes(z)
        self.first_copy(z).wait_recv()
        land = self.core_land.at[self.group, z]
        self.add(land, self.rows(ahead * self.half, self.half), self.first_land[self.group, z])
        self.second_copy(z).start()

    def third(self, z):
        self.second_copy(z).wait_recv()
        land = self.core_land.at[self.group, z]
        self.add(land, self.kept(z), self.second_land[self.group, z])
        pl.when(z != self.place.z)(self.far_copy(z).start)

    def fourth(self):
        p = self.place
        total = self.core_land[self.group, p.z, self.kept(p.z)].astype(HIGH)
        for z in p.others:
            self.far_arrival(z).wait_recv()
            total = total + self.far_land[self.group, z].astype(HIGH)
        for at in range(len(self.wide_flips)):
            self.wide_out[self.group, at] = total.astype(LOW)
            copy = self.wide_copy(at)
            copy.start()
            copy.wait_recv()
            total = self.wide_out[self.group, at].astype(HIGH) + self.wide_land[self.group, at].astype(HIGH)
        self.pieces[self.group] = total.astype(LOW)

    def finish(self):
        p = self.place
        for z in [p.z] + p.others:
            self.core_copy(z).wait_send()
            self.first_copy(z).wait_send()
            self.second_copy(z).wait_send()
        for z in p.others:
            self.far_copy(z).wait_send()
        for at in range(len(self.wide_flips)):
            self.wide_copy(at).wait_send()


class Return(Spread):
    def __init__(self, place, whole, pieces, send, recv, keep_sem, group):
        super().__init__(place, whole, send, recv, group)
        self.mine = pieces.at[group]
        p = place
        self.keep = pltpu.make_async_copy(self.mine, self.piece(0, p.a, p.b, p.core), keep_sem.at[group])

    def hand_out(self, z):
        super().hand_out(z)
        self.keep.start()

    def sent(self, z):
        super().sent(z)
        self.keep.wait()

    def odd(self, z):
        return lax.rem(self.place.z + self.group, 2)


def backward_kernel(
    n_tensor,
    heads,
    scale,
    layer_input,
    own_segments,
    row_segments,
    vectors,
    in_cotangent,
    in_w,
    in_q,
    in_k,
    in_v,
    in_totals,
    in_attended,
    in_activation,
    in_slope,
    in_hidden,
    in_xhat,
    in_inverse,
    in_second,
    out_layer,
    out_partial,
    out_landed,
    out_summed,
    out_sums,
    weights,
    core_land,
    first_land,
    second_land,
    far_land,
    pieces,
    activation,
    slope,
    row_input,
    bias,
    q_all,
    k_all,
    v_all,
    totals,
    attended,
    queries,
    keys,
    values,
    grad_mixed,
    grad_k,
    grad_v,
    inverse,
    terms,
    hidden_low,
    grad_low,
    spare,
    landed,
    sums,
    sums_land,
    sums_far,
    send,
    recv,
    final_send,
    final_recv,
    wide_out,
    wide_land,
    wide_send,
    wide_recv,
    load_sem,
    weight_sem,
    stream_sem,
    term_send,
    term_recv,
    sums_send,
    sums_recv,
    save_sem,
    keep_sem,
):
    place = Place(n_tensor)
    share = own_segments.shape[0]
    length = row_input.shape[0]
    shares_per_row = length // share
    group_rows = q_all.shape[2]
    size = group_rows // heads
    my_share = lax.rem(place.z, shares_per_row)
    in_row = pl.ds(pl.multiple_of(my_share * share, share), share)
    row_start = pl.multiple_of(place.z // shares_per_row * length, length)
    order = list(reversed(place.others)) + [place.z]
    bits = sums_land.shape[0]
    flips = [place.dp + (1 << bit) - (2 << bit) * lax.rem(place.dp // (1 << bit), 2) for bit in range(bits)]

    accum, xhat = terms.at[0], terms.at[1]

    def load(source, target, at):
        copy = pltpu.make_async_copy(source, target, load_sem.at[at])
        copy.start()
        return copy

    def weight_load(group, z):
        return pltpu.make_async_copy(in_w.at[group, z], weights.at[group, z], weight_sem.at[group, z])

    def stream(at, sources, first_sem):
        z, slot = place.pick(at, order), lax.rem(at, 2)
        return [
            pltpu.make_async_copy(source.at[z], target.at[slot], stream_sem.at[first_sem + index, slot])
            for index, (source, target) in enumerate(sources)
        ]

    ffn_streams = [(in_activation, activation), (in_slope, slope)]
    head_streams = [
        (in_q, q_all),
        (in_k, k_all),
        (in_v, v_all),
        (in_totals, totals),
        (in_attended, attended),
    ]

    early = [
        load(source, target, at)
        for at, (source, target) in enumerate(
            [(in_second, accum), (in_cotangent, spare.at[0]), (in_xhat, xhat), (in_inverse, inverse), (in_hidden, hidden_low)]
        )
    ]
    for copy in stream(0, ffn_streams, 0):
        copy.start()
    for z in order:
        weight_load(2, z).start()
        weight_load(1, z).start()
    late = load(layer_input.at[pl.ds(row_start, length)], row_input, 5)
    for z in order:
        weight_load(0, z).start()
    for copy in stream(0, head_streams, 2):
        copy.start()
    meet([(flip, place.z) for flip in flips] + [(place.dp, z) for z in place.others])
    lands = (core_land, first_land, second_land, far_land)
    wide = (flips[3:], wide_out, wide_land, wide_send, wide_recv)
    reduces = [Reduce(place, weights, lands, pieces, send, recv, wide, group) for group in range(3)]
    returns = [
        Return(place, out_summed, pieces, final_send, final_recv, keep_sem, group) for group in range(3)
    ]
    reduce_a, reduce_b, reduce_c = reduces
    sums[0] = jnp.zeros(sums.shape[1:], HIGH)
    bias[...] = segment_bias(own_segments[...], row_segments[...])
    gain_first, gain_second, shift_second = vectors[1:2], vectors[4:5], vectors[5:6]

    for copy in early:
        copy.wait()
    band = min(128, share)

    def second_norm(at, carry):
        rows = pl.ds(pl.multiple_of(at * band, band), band)
        normed, spread = norm_forward(accum[rows])
        live = (own_segments[rows] >= 0).astype(HIGH)
        cotangent = spare[0, rows].astype(HIGH) * live
        spare[0, rows] = (normed * gain_second + shift_second).astype(LOW)
        grad_second = norm_backward(normed, spread, cotangent * gain_second)
        sums[0, n_tensor, 4:5] += column_sum(cotangent * normed)
        sums[0, n_tensor, 5:6] += column_sum(cotangent)
        sums[0, n_tensor, 3:4] += column_sum(grad_second)
        grad_low[rows] = grad_second.astype(LOW)
        accum[rows] = grad_second
        return carry

    lax.fori_loop(0, share // band, second_norm, 0)
    save_layer = pltpu.make_async_copy(spare.at[0], out_layer, save_sem.at[0])
    save_layer.start()

    def feed_forward(at, carry):
        z, slot = place.pick(at, order), lax.rem(at, 2)
        before = place.pick(at - 1, order)

        @pl.when(at + 1 < n_tensor)
        def _():
            for copy in stream(at + 1, ffn_streams, 0):
                copy.start()

        for copy in stream(at, ffn_streams, 0):
            copy.wait()
        weight_load(2, z).wait()
        low = grad_low[...]
        grad_up = (dot_nt(low, weights[2, z]) * slope[slot].astype(HIGH)).astype(LOW)
        weights[2, z] = dot_tn(activation[slot], low).astype(LOW)
        reduce_c.start(z)
        pl.when(at >= 1)(functools.partial(reduce_b.first, before))
        pl.when(at >= 3)(functools.partial(reduce_b.second, order[0]))
        weight_load(1, z).wait()
        accum[...] += dot_nt(grad_up, weights[1, z])
        weights[1, z] = dot_tn(hidden_low[...], grad_up).astype(LOW)
        reduce_b.start(z)
        sums[0, z, 2:3] = column_sum(grad_up.astype(HIGH))
        reduce_c.first(z)
        pl.when(at == 2)(functools.partial(reduce_c.second, order[0]))
        return carry

    lax.fori_loop(0, n_tensor, feed_forward, 0)

    def first_norm(at, carry):
        rows = pl.ds(pl.multiple_of(at * band, band), band)
        grad_hidden, normed = accum[rows], xhat[rows]
        grad_first = norm_backward(normed, inverse[rows], grad_hidden * gain_first)
        sums[0, n_tensor, 0:1] += column_sum(grad_first)
        sums[0, n_tensor, 1:2] += column_sum(grad_hidden * normed)
        sums[0, n_tensor, 2:3] += column_sum(grad_hidden)
        accum[rows] = grad_first
        grad_low[rows] = grad_first.astype(LOW)
        return carry

    lax.fori_loop(0, share // band, first_norm, 0)
    for index in range(shares_per_row):
        terms[1 + index] = jnp.zeros(accum.shape, HIGH)
    reduce_b.first(order[-1])
    late.wait()

    def attend(at, carry):
        z, slot = place.pick(at, order), lax.rem(at, 2)
        after = place.pick(at + 1, order)
        before, earlier = place.pick(at - 1, order), place.pick(at - 2, order)

        @pl.when(at + 1 < n_tensor)
        def _():
            for copy in stream(at + 1, head_streams, 2):
                copy.start()

        for copy in stream(at, head_streams, 2):
            copy.wait()
        weight_load(0, z).wait()
        incoming = dot_nt(grad_low[...], weights[0, z, 3 * group_rows :]).astype(LOW)
        weights[0, z, 3 * group_rows :] = dot_tn(attended[slot], grad_low[...]).astype(LOW)
        for head in range(heads):
            part = slice(head * size, (head + 1) * size)
            queries[head], keys[head] = q_all[slot, :, part], k_all[slot, :, part]
            values[head], grad_mixed[head] = v_all[slot, :, part], incoming[:, part]
        pl.when(at >= 1)(functools.partial(reduce_a.first, before))

        def one_head(head, inner):
            k, v = keys[head], values[head]
            grad_kt = jnp.zeros((size, length), HIGH)
            grad_vt = jnp.zeros((size, length), HIGH)
            chunk = min(256, share)
            for start in range(0, share, chunk):
                rows = pl.ds(start, chunk)
                q, up = queries[head, rows], grad_mixed[head, rows]
                chance = jnp.exp(dot_nt(q, k) + bias[rows] - totals[slot, head, rows])
                change = chance * dot_nt(up, v)
                change = change - chance * jnp.sum(change, axis=-1, keepdims=True)
                change = change.astype(LOW)
                grad_kt = grad_kt + dot_nn(q.T, change)
                grad_vt = grad_vt + dot_nn(up.T, chance.astype(LOW))
                grad_mixed[head, rows] = (dot_nn(change, k) * scale).astype(LOW)
            grad_k[head] = grad_kt.astype(LOW)
            grad_v[head] = grad_vt.astype(LOW)

            @pl.when(head == 0)
            def _():
                reduce_c.third(z)
                pl.when(at + 1 < n_tensor)(functools.partial(reduce_c.second, after))

            pl.when(head == 1)(functools.partial(reduce_b.third, z))

            @pl.when(head == 2)
            def _():
                pl.when(at + 1 < n_tensor)(functools.partial(reduce_b.second, after))
                pl.when(at >= 3)(functools.partial(reduce_a.third, order[0]))
                pl.when(at >= 2)(functools.partial(reduce_a.second, earlier))

            return inner

        lax.fori_loop(0, heads, one_head, 0)
        dq = jnp.concatenate([grad_mixed[head] for head in range(heads)], axis=-1)
        dk = grad_k[...].reshape(group_rows, length)
        dv = grad_v[...].reshape(group_rows, length)
        x_row = row_input[...]
        accum[...] += dot_nn(dq, weights[0, z, :group_rows])
        row_term = dot_tn(jnp.concatenate([dk, dv], axis=0), weights[0, z, group_rows : 3 * group_rows])
        for index in range(shares_per_row):
            terms[1 + index] += row_term[index * share : (index + 1) * share]
        weights[0, z, :group_rows] = dot_tn(dq, row_input[in_row]).astype(LOW)
        weights[0, z, group_rows : 2 * group_rows] = dot_nn(dk, x_row).astype(LOW)
        weights[0, z, 2 * group_rows : 3 * group_rows] = dot_nn(dv, x_row).astype(LOW)
        reduce_a.start(z)
        ones = jnp.ones((8, length), LOW)
        sums[0, z, 0:1, :group_rows] = dot_nn(ones[:, :share], dq)[0:1]
        sums[0, z, 1:2, :group_rows] = dot_nt(ones, dv)[0:1]
        return carry

    lax.fori_loop(0, n_tensor, attend, 0)

    save_layer.wait()
    term_copies = []
    for step in range(1, shares_per_row):
        other = lax.rem(my_share + step, shares_per_row)
        spare[step - 1] = terms[1 + other].astype(LOW)
        partner = place.z - my_share + other
        copy = remote(
            spare.at[step - 1], landed.at[step - 1], term_send.at[step - 1], term_recv.at[step - 1], (place.dp, partner)
        )
        copy.start()
        term_copies.append(copy)
    accum[...] += terms[1 + my_share]
    save_partial = pltpu.make_async_copy(accum, out_partial, save_sem.at[1])
    save_partial.start()

    def sum_copy(bit):
        return remote(
            sums.at[bit], sums_land.at[bit], sums_send.at[bit], sums_recv.at[bit], (flips[bit], place.z)
        )

    def fold(bit):
        sum_copy(bit).wait_recv()
        sums[bit + 1] = sums[bit] + sums_land[bit]

    def far_sum(z):
        sems = sums_send.at[bits + z], sums_recv.at[bits + place.z]
        return remote(sums.at[bits], sums_far.at[place.z], *sems, (place.dp, z))

    def far_sum_arrival(z):
        sems = sums_send.at[bits + z], sums_recv.at[bits + z]
        return remote(sums.at[bits], sums_far.at[z], *sems, (place.dp, z))

    return_a, return_b, return_c = returns
    sum_copy(0).start()
    reduce_c.fourth()
    return_c.hand_out(0)
    reduce_b.fourth()
    return_b.hand_out(0)
    reduce_a.first(order[3])
    reduce_a.second(order[2])
    reduce_a.third(order[1])
    fold(0)
    sum_copy(1).start()
    return_c.second(0)
    return_b.second(0)
    reduce_a.second(order[3])
    reduce_a.third(order[2])
    fold(1)
    sum_copy(2).start()
    return_c.third(0)
    return_b.third(0)
    reduce_a.third(order[3])
    reduce_a.fourth()
    return_a.hand_out(0)
    for bit in range(2, bits):
        fold(bit)
        if bit + 1 < bits:
            sum_copy(bit + 1).start()
    for z in place.others:
        far_sum(z).start()
    sums_far[place.z] = sums[bits]
    return_c.last(0)
    return_b.last(0)
    return_a.second(0)
    for copy in term_copies:
        copy.wait_recv()
    save_landed = pltpu.make_async_copy(landed, out_landed, save_sem.at[5])
    save_landed.start()
    return_a.third(0)
    for z in place.others:
        far_sum_arrival(z).wait_recv()
    total = sums_far[0]
    for z in range(1, n_tensor):
        total = total + sums_far[z]
    out_sums[...] = total
    return_a.last(0)
    save_partial.wait()
    save_landed.wait()
    for copy in term_copies:
        copy.wait_send()
    for bit in range(bits):
        sum_copy(bit).wait_send()
    for z in place.others:
        far_sum(z).wait_send()
    for reduce in reduces:
        reduce.finish()
    for part in returns:
        part.sent(0)


def on_device(
    layer_input,
    segment_ids,
    w_qkv,
    qv_bias,
    w_out,
    out_bias,
    norm1_gain,
    norm1_bias,
    w_up,
    up_bias,
    w_down,
    down_bias,
    norm2_gain,
    norm2_bias,
    out_cotangent,
):
    n_tensor = lax.axis_size("tensor")
    place = lax.axis_index("tensor")
    n_dp = lax.axis_size("dp")
    bits = n_dp.bit_length() - 1
    tokens, width = layer_input.shape
    share = tokens // n_tensor
    heads = qv_bias.shape[0]
    head_dim = qv_bias.shape[1] // 2
    score_scale = float(head_dim) ** (-0.5)
    shares_per_row = SEQ // share
    group_rows = heads * head_dim

    local_a = w_qkv.reshape(width, heads, 3, head_dim).transpose(2, 1, 3, 0).reshape(-1, width)
    local_a = jnp.concatenate([local_a, w_out], axis=0)
    local_small = jnp.concatenate(
        [
            jnp.pad(qv_bias[:, :head_dim].reshape(1, -1), ((0, 0), (0, width - group_rows))),
            jnp.pad(qv_bias[:, head_dim:].reshape(1, -1), ((0, 0), (0, width - group_rows))),
            up_bias.reshape(1, -1),
            jnp.zeros((5, width), LOW),
        ]
    ).astype(HIGH)
    vectors = jnp.stack(
        [out_bias, norm1_gain, norm1_bias, down_bias, norm2_gain, norm2_bias, out_bias, out_bias]
    ).astype(HIGH)
    row_start = (place // shares_per_row) * SEQ
    own_segments = lax.dynamic_slice_in_dim(segment_ids, place * share, share, 0)[:, None]
    row_segments = lax.dynamic_slice_in_dim(segment_ids, row_start, SEQ, 0)[None, :]

    vmem = pl.BlockSpec(memory_space=pltpu.VMEM)
    anywhere = pl.BlockSpec(memory_space=pl.ANY)

    def low(*shape):
        return jax.ShapeDtypeStruct(shape, LOW)

    def high(*shape):
        return jax.ShapeDtypeStruct(shape, HIGH)

    def low_scratch(*shape):
        return pltpu.VMEM(shape, LOW)

    def high_scratch(*shape):
        return pltpu.VMEM(shape, HIGH)

    dma = pltpu.SemaphoreType.DMA
    whole = (3, n_tensor, width, width)
    (w, q, k, v, totals, attended, activation, slope, small, hidden, xhat, inverse, second_sum) = pl.pallas_call(
        functools.partial(forward_kernel, n_tensor, heads, score_scale),
        out_shape=(
            low(*whole),
            low(n_tensor, share, group_rows),
            low(n_tensor, SEQ, group_rows),
            low(n_tensor, SEQ, group_rows),
            high(n_tensor, heads, share, 1),
            low(n_tensor, share, group_rows),
            low(n_tensor, share, width),
            low(n_tensor, share, width),
            high(n_tensor, 8, width),
            low(share, width),
            high(share, width),
            high(share, 1),
            high(share, width),
        ),
        in_specs=[anywhere, vmem, vmem, anywhere, anywhere, anywhere, vmem, vmem],
        out_specs=(anywhere,) * 8 + (vmem,) * 5,
        scratch_shapes=[
            low_scratch(*whole),
            low_scratch(SEQ, width),
            high_scratch(share, SEQ),
            low_scratch(n_tensor, share, group_rows),
            low_scratch(n_tensor, SEQ, group_rows),
            low_scratch(n_tensor, SEQ, group_rows),
            high_scratch(n_tensor, heads, share, 1),
            low_scratch(n_tensor, share, group_rows),
            low_scratch(n_tensor, share, width),
            low_scratch(n_tensor, share, width),
            low_scratch(heads, share, head_dim),
            low_scratch(heads, SEQ, head_dim),
            low_scratch(heads, SEQ, head_dim),
            low_scratch(heads, share, head_dim),
            dma((3, n_tensor, 9)),
            dma((3, n_tensor, 8)),
            dma((n_tensor,)),
            dma((n_tensor,)),
            dma((4,)),
            dma((40,)),
        ],
        compiler_params=pltpu.CompilerParams(
            collective_id=0, has_side_effects=True, vmem_limit_bytes=VMEM_LIMIT
        ),
        name="forward",
    )(layer_input, own_segments, row_segments, local_a, w_up, w_down, local_small, vectors)

    half, side = width // 2, width // 2
    quarter = width // 4
    wide = max(bits - 3, 1)
    layer_output, partial, landed, summed, sums = pl.pallas_call(
        functools.partial(backward_kernel, n_tensor, heads, score_scale),
        out_shape=(
            low(share, width),
            high(share, width),
            low(shares_per_row - 1, share, width),
            low(3, 1, width, width),
            high(n_tensor + 1, 8, width),
        ),
        in_specs=[anywhere, vmem, vmem, vmem] + [anywhere] * 13,
        out_specs=(anywhere,) * 4 + (vmem,),
        scratch_shapes=[
            low_scratch(*whole),
            low_scratch(3, n_tensor, width, side),
            low_scratch(3, n_tensor, half, side),
            low_scratch(3, n_tensor, quarter, side),
            low_scratch(3, n_tensor, quarter, side),
            low_scratch(3, quarter, side),
            low_scratch(2, share, width),
            low_scratch(2, share, width),
            low_scratch(SEQ, width),
            high_scratch(share, SEQ),
            low_scratch(2, share, group_rows),
            low_scratch(2, SEQ, group_rows),
            low_scratch(2, SEQ, group_rows),
            high_scratch(2, heads, share, 1),
            low_scratch(2, share, group_rows),
            low_scratch(heads, share, head_dim),
            low_scratch(heads, SEQ, head_dim),
            low_scratch(heads, SEQ, head_dim),
            low_scratch(heads, share, head_dim),
            low_scratch(heads, head_dim, SEQ),
            low_scratch(heads, head_dim, SEQ),
            high_scratch(share, 1),
            high_scratch(1 + shares_per_row, share, width),
            low_scratch(share, width),
            low_scratch(share, width),
            low_scratch(shares_per_row - 1, share, width),
            low_scratch(shares_per_row - 1, share, width),
            high_scratch(bits + 1, n_tensor + 1, 8, width),
            high_scratch(bits, n_tensor + 1, 8, width),
            high_scratch(n_tensor, n_tensor + 1, 8, width),
            dma((3, n_tensor, 4)),
            dma((3, n_tensor, 4)),
            dma((3, 1, 9)),
            dma((3, 1, 8)),
            low_scratch(3, wide, quarter, side),
            low_scratch(3, wide, quarter, side),
            dma((3, wide)),
            dma((3, wide)),
            dma((8,)),
            dma((3, n_tensor)),
            dma((7, 2)),
            dma((shares_per_row - 1,)),
            dma((shares_per_row - 1,)),
            dma((bits + n_tensor,)),
            dma((bits + n_tensor,)),
            dma((6,)),
            dma((3,)),
        ],
        compiler_params=pltpu.CompilerParams(
            collective_id=1, has_side_effects=True, vmem_limit_bytes=VMEM_LIMIT
        ),
        name="backward",
    )(
        layer_input,
        own_segments,
        row_segments,
        vectors,
        out_cotangent,
        w,
        q,
        k,
        v,
        totals,
        attended,
        activation,
        slope,
        hidden,
        xhat,
        inverse,
        second_sum,
    )

    input_grad = partial
    for step in range(shares_per_row - 1):
        input_grad = input_grad + landed[step].astype(HIGH)
    summed = summed[:, 0].astype(HIGH)
    grad_qkv = summed[0, : 3 * group_rows].reshape(3, heads, head_dim, width).transpose(3, 1, 0, 2)
    mine = lax.dynamic_slice_in_dim(sums, place, 1, 0)[0]
    every = sums[n_tensor]
    grad_qv_bias = jnp.concatenate(
        [mine[at, :group_rows].reshape(heads, head_dim) for at in range(2)], axis=1
    )
    return (
        layer_output,
        input_grad,
        grad_qkv.reshape(width, heads, 3 * head_dim),
        grad_qv_bias,
        summed[0, 3 * group_rows :],
        every[0],
        every[1],
        every[2],
        summed[1],
        mine[2],
        summed[2],
        every[3],
        every[4],
        every[5],
    )


def solution(mesh):
    return jax.shard_map(
        on_device,
        mesh=mesh,
        in_specs=(
            P("dp", None),
            P("dp"),
            P(None, "tensor", None),
            P("tensor", None),
            P("tensor", None),
            P(),
            P(),
            P(),
            P(None, "tensor"),
            P("tensor"),
            P("tensor", None),
            P(),
            P(),
            P(),
            P(("dp", "tensor"), None),
        ),
        out_specs=(
            P(("dp", "tensor"), None),
            P(("dp", "tensor"), None),
            P(None, "tensor", None),
            P("tensor", None),
            P("tensor", None),
            P(),
            P(),
            P(),
            P(None, "tensor"),
            P("tensor"),
            P("tensor", None),
            P(),
            P(),
            P(),
        ),
        check_vma=False,
    )
```

```python
import functools

import jax
import jax.numpy as jnp
from jax import lax
from jax.experimental import pallas as pl
from jax.experimental.pallas import tpu as pltpu
from jax.sharding import PartitionSpec as P

SEQ = 1024


EPSILON = 1e-06
MASKED = -1e30
LOW = jnp.bfloat16
HIGH = jnp.float32
MESH = pl.DeviceIdType.MESH
VMEM_LIMIT = 62 * 1024 * 1024


def dot_nn(left, right):
    return lax.dot_general(left, right, (((1,), (0,)), ((), ())), preferred_element_type=HIGH)


def dot_nt(left, right):
    return lax.dot_general(left, right, (((1,), (1,)), ((), ())), preferred_element_type=HIGH)


def dot_tn(left, right):
    return lax.dot_general(left, right, (((0,), (0,)), ((), ())), preferred_element_type=HIGH)


def norm_forward(summed):
    mean = jnp.mean(summed, axis=-1, keepdims=True)
    centred = summed - mean
    spread = jnp.mean(centred * centred, axis=-1, keepdims=True)
    inverse = lax.rsqrt(spread + EPSILON)
    return centred * inverse, inverse


def norm_backward(xhat, inverse, scaled):
    return inverse * (
        scaled
        - jnp.mean(scaled, axis=-1, keepdims=True)
        - xhat * jnp.mean(scaled * xhat, axis=-1, keepdims=True)
    )


def gelu_parts(u):
    phi_cdf = 0.5 * (1.0 + lax.erf(u * (2.0**-0.5)))
    density = jnp.exp(-0.5 * u * u) * 0.3989422804014327
    return u * phi_cdf, phi_cdf + u * density


def column_sum(values):
    return jnp.sum(values, axis=0, keepdims=True)


def as_row(vector):
    return vector[...].astype(HIGH).reshape(1, -1)


def as_column(row):
    return jnp.broadcast_to(row, (8, row.shape[1])).T[:, :1]


def segment_rows(segment_ids, own_start, share, row_start, length):
    own = segment_ids[pl.ds(own_start, share)].astype(HIGH).reshape(1, share)
    return as_column(own), segment_ids[pl.ds(row_start, length)].astype(HIGH).reshape(1, length)


def segment_bias(own_segments, row_segments):
    return jnp.where(own_segments == row_segments, 0.0, MASKED)


class Place:
    def __init__(self, n_tensor):
        self.n_tensor = n_tensor
        self.z = lax.axis_index("tensor")
        self.dp = lax.axis_index("dp")
        self.core = lax.rem(self.dp, 2)
        self.a = lax.rem(self.dp // 2, 2)
        self.b = lax.rem(self.dp // 4, 2)
        self.to_core = (self.dp + 1 - 2 * self.core, self.z)
        self.to_a = (self.dp + 2 - 4 * self.a, self.z)
        self.to_b = (self.dp + 4 - 8 * self.b, self.z)
        self.others = [lax.rem(self.z + step, n_tensor) for step in range(1, n_tensor)]
        if n_tensor == 4:
            near = self.z + 1 - 2 * lax.rem(self.z, 2)
            upper = self.z // 2
            self.others = [near, 2 - upper, 3 - 3 * upper]

    def pick(self, at, order):
        chosen = order[0]
        for index in range(1, len(order)):
            chosen = jnp.where(at == index, order[index], chosen)
        return chosen


def meet(partners):
    barrier = pltpu.get_barrier_semaphore()
    for partner in partners:
        pl.semaphore_signal(barrier, inc=1, device_id=partner, device_id_type=MESH)
    pl.semaphore_wait(barrier, len(partners))


def remote(src, dst, send, recv, target):
    return pltpu.make_async_remote_copy(
        src_ref=src,
        dst_ref=dst,
        send_sem=send,
        recv_sem=recv,
        device_id=target,
        device_id_type=MESH,
    )


class Spread:
    def __init__(self, place, whole, send, recv, group, block):
        self.place, self.whole, self.send, self.recv, self.group = place, whole, send, recv, group
        self.matrix, self.base, size = block
        self.mine = None
        self.quarter = size // 4
        self.half = whole.shape[3] // 2

    def odd(self, z):
        return lax.rem(z + self.group, 2)

    def piece(self, z, a, b, side):
        odd = self.odd(z)
        row = odd * (2 * b + a) + (1 - odd) * (2 * a + b)
        rows = pl.ds(pl.multiple_of(self.base + row * self.quarter, 16), self.quarter)
        return self.whole.at[self.matrix, z, rows, pl.ds(pl.multiple_of(side * self.half, 128), self.half)]

    def pass_on(self, z, slot, a, b, side, target):
        part = self.piece(z, a, b, side)
        send = self.send.at[self.group, z, slot]
        recv = self.recv.at[self.group, z, slot % 8]
        source = self.mine if self.mine is not None and slot in (1, 2, 4) else part
        return remote(source, part, send, recv, target)

    def turn(self, z):
        p = self.place
        odd = self.odd(z)
        a = p.a * odd + (1 - p.a) * (1 - odd)
        b = p.b * (1 - odd) + (1 - p.b) * odd
        target = odd * p.to_a[0] + (1 - odd) * p.to_b[0]
        return self.pass_on(z, 3, a, b, p.core, (target, p.z))

    def hand_out(self, z):
        p = self.place
        self.pass_on(z, 1, p.a, p.b, p.core, p.to_a).start()
        self.pass_on(z, 2, p.a, p.b, p.core, p.to_b).start()
        self.pass_on(z, 4, p.a, p.b, p.core, p.to_core).start()

    def second(self, z):
        p = self.place
        self.pass_on(z, 1, 1 - p.a, p.b, p.core, p.to_a).wait_recv()
        self.pass_on(z, 2, p.a, 1 - p.b, p.core, p.to_b).wait_recv()
        self.turn(z).start()
        self.pass_on(z, 5, 1 - p.a, p.b, p.core, p.to_core).start()
        self.pass_on(z, 6, p.a, 1 - p.b, p.core, p.to_core).start()

    def third(self, z):
        p = self.place
        self.pass_on(z, 3, 1 - p.a, 1 - p.b, p.core, p.to_a).wait_recv()
        self.pass_on(z, 7, 1 - p.a, 1 - p.b, p.core, p.to_core).start()

    def last(self, z):
        p = self.place
        side = 1 - p.core
        self.pass_on(z, 4, p.a, p.b, side, p.to_core).wait_recv()
        self.pass_on(z, 5, 1 - p.a, p.b, side, p.to_core).wait_recv()
        self.pass_on(z, 6, p.a, 1 - p.b, side, p.to_core).wait_recv()
        self.pass_on(z, 7, 1 - p.a, 1 - p.b, side, p.to_core).wait_recv()

    def sent(self, z):
        p = self.place
        self.pass_on(z, 1, p.a, p.b, p.core, p.to_a).wait_send()
        self.pass_on(z, 2, p.a, p.b, p.core, p.to_b).wait_send()
        self.turn(z).wait_send()
        self.pass_on(z, 4, p.a, p.b, p.core, p.to_core).wait_send()
        self.pass_on(z, 5, 1 - p.a, p.b, p.core, p.to_core).wait_send()
        self.pass_on(z, 6, p.a, 1 - p.b, p.core, p.to_core).wait_send()
        self.pass_on(z, 7, 1 - p.a, 1 - p.b, p.core, p.to_core).wait_send()


class Gather(Spread):
    def along(self, z):
        p = self.place
        part = self.piece(p.z, p.a, p.b, p.core)
        send, recv = self.send.at[self.group, z, 0], self.recv.at[self.group, p.z, 0]
        return remote(part, part, send, recv, (p.dp, z))

    def onward(self, z):
        p = self.place
        target = jnp.where(z < p.z, p.z + 1, p.z - 1)
        copy = self.pass_on(z, 8, p.a, p.b, p.core, (p.dp, target))
        return (target >= 0) & (target < p.n_tensor), copy

    def start(self):
        p = self.place
        for z in (p.z - 1, p.z + 1):
            pl.when((z >= 0) & (z < p.n_tensor))(self.along(z).start)

    def first(self, z):
        p = self.place
        self.pass_on(z, 0, p.a, p.b, p.core, p.to_core).wait_recv()
        there, copy = self.onward(z)
        pl.when(there)(copy.start)
        self.hand_out(z)

    def finish(self):
        p = self.place
        for z in (p.z - 1, p.z + 1):
            pl.when((z >= 0) & (z < p.n_tensor))(self.along(z).wait_send)
        for z in p.others:
            there, copy = self.onward(z)
            pl.when(there)(copy.wait_send)
            self.sent(z)


FORWARD_PLAN = (
    {
        "0.4": ("Fan",),
        "need.1": ("San", "Fam", "Fbn", "Tan", "Faf", "Lan",),
        "1.0": ("Sam",),
        "1.1": ("Fbm",),
        "1.4": ("Sbn",),
        "need.2": ("Fbf", "Saf", "Tam", "Lam",),
        "2.0": ("Sbm",),
        "2.1": ("Fcn",),
        "2.3": ("Tbn",),
        "need.3": ("Lbn", "Taf", "Fcm", "Sbf", "Laf",),
        "3.0": ("Tbm",),
        "3.1": ("Fcf",),
        "3.3": ("Lbm",),
        "3.4": ("Scn",),
        "ffn.0": ("Scm", "Tbf",),
        "ffn.1": ("Lbf", "Scf", "Tcn", "Tcm", "Lcn",),
        "ffn.2": ("Tcf", "Lcm",),
        "ffn.3": ("Lcf",),
    },
    {
        "0.4": ("Fan", "Fam",),
        "need.1": ("Faf", "San", "Fbn", "Fbm", "Sam", "Fbf", "Saf", "Tan", "Lan",),
        "1.0": ("Sbn",),
        "1.2": ("Fcn",),
        "1.3": ("Sbm",),
        "need.2": ("Taf", "Tam", "Fcm", "Laf", "Lam",),
        "2.0": ("Fcf", "Sbf", "Tbn",),
        "2.3": ("Scn",),
        "2.4": ("Lbn",),
        "3.0": ("Tbm",),
        "3.3": ("Lbm",),
        "3.5": ("Scm",),
        "ffn.0": ("Scf", "Tbf",),
        "ffn.1": ("Tcn", "Lbf", "Lcn",),
        "ffn.2": ("Tcm", "Tcf", "Lcm",),
        "ffn.3": ("Lcf",),
    },
)


def forward_kernel(
    n_tensor,
    heads,
    scale,
    layer_input,
    segment_ids,
    local_qkv,
    w_out,
    w_up,
    w_down,
    local_small,
    out_bias,
    norm1_gain,
    norm1_bias,
    down_bias,
    out_w,
    out_q,
    out_k,
    out_v,
    out_totals,
    out_attended,
    out_activation,
    out_slope,
    small,
    hidden_low,
    xhat,
    inverse,
    second_sum,
    weights,
    row_input,
    bias,
    q_all,
    k_all,
    v_all,
    totals,
    attended,
    activation,
    slope,
    queries,
    keys,
    values,
    mixed,
    send,
    recv,
    small_send,
    small_recv,
    copy_sem,
    save_sem,
    shard_sem,
):
    place = Place(n_tensor)
    share = hidden_low.shape[0]
    length, width = row_input.shape
    shares_per_row = length // share
    group_rows = q_all.shape[2]
    size = group_rows // heads
    in_row = pl.ds(pl.multiple_of(lax.rem(place.z, shares_per_row) * share, share), share)
    row_start = pl.multiple_of(place.z // shares_per_row * length, length)
    near, middle, far = place.others

    mine = weights.at[0, place.z]
    pairs = [
        (local_qkv, mine.at[pl.ds(0, 3 * group_rows)]),
        (w_out, mine.at[pl.ds(3 * group_rows, group_rows)]),
        (w_up, weights.at[1, place.z]),
        (w_down, weights.at[2, place.z]),
    ]
    own = [
        pltpu.make_async_copy(source, target, copy_sem.at[at]) for at, (source, target) in enumerate(pairs)
    ]
    load_input = pltpu.make_async_copy(
        layer_input.at[pl.ds(row_start, length)], row_input, copy_sem.at[4]
    )
    for copy in own:
        copy.start()
    load_input.start()
    meet([place.to_core, place.to_a, place.to_b] + [(place.dp, z) for z in place.others])
    gathers = [Gather(place, weights, send, recv, group, (group, 0, width)) for group in range(3)]
    gather_a, gather_b, gather_c = gathers

    def small_copy(z):
        sems = small_send.at[z], small_recv.at[place.z]
        return remote(local_small, small.at[place.z], *sems, (place.dp, z))

    def small_arrival(z):
        return remote(local_small, small.at[z], small_send.at[z], small_recv.at[z], (place.dp, z))

    own[0].wait()
    own[1].wait()
    gather_a.start()
    for z in place.others:
        small_copy(z).start()
    small[place.z] = local_small[...]
    own_start = pl.multiple_of(place.z * share, share)
    bias[...] = segment_bias(*segment_rows(segment_ids, own_start, share, row_start, length))
    load_input.wait()

    saves = []

    def save(source, target):
        copy = pltpu.make_async_copy(source, target, save_sem.at[len(saves)])
        copy.start()
        saves.append(copy)

    def shard_saves(at, z):
        pairs = [
            (weights.at[1, z], out_w.at[1, z]),
            (weights.at[2, z], out_w.at[2, z]),
            (activation.at[z], out_activation.at[z]),
            (slope.at[z], out_slope.at[z]),
        ]
        return [
            pltpu.make_async_copy(source, target, shard_sem.at[index, at])
            for index, (source, target) in enumerate(pairs)
        ]

    shards = dict(zip("nmf", place.others))
    stages = {"F": "first", "S": "second", "T": "third", "L": "last"}
    matrices = dict(zip("abc", gathers))
    at_end = (place.z == 0) | (place.z == n_tensor - 1)

    def serve(slot, there=True):
        for inside, plan in enumerate(FORWARD_PLAN):
            steps = plan.get(slot, ())
            if not steps:
                continue

            def run(steps=steps):
                for stage, matrix, shard in steps:
                    getattr(matrices[matrix], stages[stage])(shards[shard])

            pl.when(jnp.logical_and(at_end != bool(inside), there))(run)

    def start_b():
        own[2].wait()
        gather_b.start()

    def start_c():
        own[3].wait()
        gather_c.start()

    def attend(turn, z):
        q_rows, k_rows, v_rows = (
            jnp.concatenate([weights[0, z, pl.ds((3 * head + kind) * size, size)] for head in range(heads)], axis=0)
            for kind in range(3)
        )
        q_bias, v_bias = small[z, 0:1, :group_rows], small[z, 1:2, :group_rows]
        x_row = row_input[...]
        q = (dot_nt(row_input[in_row], q_rows) + q_bias).astype(LOW) * scale
        k = dot_nt(x_row, k_rows).astype(LOW)
        v = (dot_nt(x_row, v_rows) + v_bias).astype(LOW)
        q_all[z], k_all[z], v_all[z] = q, k, v
        for head in range(heads):
            part = slice(head * size, (head + 1) * size)
            queries[head], keys[head], values[head] = q[:, part], k[:, part], v[:, part]

        def one_head(head, carry):
            chunk = share // 2
            for part in range(2):
                rows = pl.ds(part * chunk, chunk)
                scores = dot_nt(queries[head, rows], keys[head]) + bias[rows]
                top = jnp.max(scores, axis=-1, keepdims=True)
                raised = jnp.exp(scores - top)
                total = jnp.sum(raised, axis=-1, keepdims=True)
                summed = dot_nn(raised.astype(LOW), values[head])
                mixed[head, rows] = (summed / total).astype(LOW)
                totals[z, head, rows] = top + jnp.log(total)
                for index in range(heads):
                    serve(f"{turn}.{2 * index + part}", head == index)
                    if (turn, index, part) == (1, 0, 1):
                        pl.when(head == index)(start_c)
            return carry

        lax.fori_loop(0, heads, one_head, 0)
        attended[z] = jnp.concatenate([mixed[head] for head in range(heads)], axis=-1)
        save(weights.at[0, z], out_w.at[0, z])
        save(q_all.at[z], out_q.at[z])
        save(k_all.at[z], out_k.at[z])
        save(v_all.at[z], out_v.at[z])
        save(totals.at[z], out_totals.at[z])
        save(attended.at[z], out_attended.at[z])

    attend(0, place.z)
    start_b()
    serve("need.1")
    for z in place.others:
        small_arrival(z).wait_recv()
    attend(1, near)
    serve("need.2")
    attend(2, middle)
    serve("need.3")
    attend(3, far)

    first_sum = row_input[in_row].astype(HIGH) + as_row(out_bias)
    for z in range(n_tensor):
        first_sum = first_sum + dot_nn(attended[z], weights[0, z, 3 * group_rows :])
    normed, spread = norm_forward(first_sum)
    xhat[...] = normed
    inverse[...] = spread
    hidden = normed * as_row(norm1_gain) + as_row(norm1_bias)
    hidden_low[...] = hidden.astype(LOW)
    second_sum[...] = hidden + as_row(down_bias)

    order = [place.z] + place.others

    def one_shard(at, carry):
        z = place.pick(at, order)

        for index in range(n_tensor):
            serve(f"ffn.{index}", at == index)
        raw = dot_nn(hidden_low[...], weights[1, z]) + small[z, 2:3]
        value, rise = gelu_parts(raw)
        activation[z] = value.astype(LOW)
        slope[z] = rise.astype(LOW)
        second_sum[...] += dot_nn(activation[z], weights[2, z])
        for copy in shard_saves(at, z):
            copy.start()
        return carry

    lax.fori_loop(0, n_tensor, one_shard, 0)
    for z in place.others:
        small_copy(z).wait_send()
    for gather in gathers:
        gather.finish()
    for copy in saves:
        copy.wait()
    for at in range(n_tensor):
        for copy in shard_saves(at, order[at]):
            copy.wait()


class Reduce:
    def __init__(self, place, grads, lands, pieces, send, recv, wide, group, block):
        matrix, base, size = block
        self.place, self.send, self.recv, self.group = place, send, recv, group
        self.half, self.quarter, self.side = size // 2, size // 4, grads.shape[3] // 2

        def rows(ref, parts):
            return ref.at[matrix, :, pl.ds(base // parts, size // parts)]

        core_land, first_land, second_land, far_land = lands
        self.grads, self.core_land = rows(grads, 1), rows(core_land, 1)
        self.first_land, self.second_land, self.far_land = (
            rows(first_land, 2),
            rows(second_land, 4),
            rows(far_land, 4),
        )
        self.piece = pieces.at[matrix, pl.ds(base // 4, size // 4)]
        self.wide_flips, wide_out, wide_land, self.wide_send, self.wide_recv = wide
        self.wide_out, self.wide_land = rows(wide_out, 4), rows(wide_land, 4)

    def columns(self, side):
        return pl.ds(pl.multiple_of(side * self.side, 128), self.side)

    def axes(self, z):
        p = self.place
        odd = lax.rem(z + self.group, 2)
        ahead, behind = odd * p.b + (1 - odd) * p.a, odd * p.a + (1 - odd) * p.b
        to_first = odd * p.to_b[0] + (1 - odd) * p.to_a[0]
        to_second = odd * p.to_a[0] + (1 - odd) * p.to_b[0]
        return ahead, behind, (to_first, p.z), (to_second, p.z)

    def rows(self, start, size):
        return pl.ds(pl.multiple_of(start, 16), size)

    def copy(self, z, slot, source, target_ref, target):
        send, recv = self.send.at[self.group, z, slot], self.recv.at[self.group, z, slot]
        return remote(source, target_ref, send, recv, target)

    def core_copy(self, z):
        p = self.place
        source = self.grads.at[z, :, self.columns(1 - p.core)]
        return self.copy(z, 0, source, self.core_land.at[z], p.to_core)

    def first_copy(self, z):
        ahead, _, target, _ = self.axes(z)
        source = self.core_land.at[z, self.rows((1 - ahead) * self.half, self.half)]
        return self.copy(z, 1, source, self.first_land.at[z], target)

    def second_copy(self, z):
        ahead, behind, _, target = self.axes(z)
        start = ahead * self.half + (1 - behind) * self.quarter
        source = self.core_land.at[z, self.rows(start, self.quarter)]
        return self.copy(z, 2, source, self.second_land.at[z], target)

    def kept(self, z):
        ahead, behind, _, _ = self.axes(z)
        return self.rows(ahead * self.half + behind * self.quarter, self.quarter)

    def far_copy(self, z):
        p, group = self.place, self.group
        source = self.core_land.at[z, self.kept(z)]
        send, recv = self.send.at[group, z, 3], self.recv.at[group, p.z, 3]
        return remote(source, self.far_land.at[p.z], send, recv, (p.dp, z))

    def far_arrival(self, z):
        p, group = self.place, self.group
        land = self.far_land.at[z]
        return remote(land, land, self.send.at[group, z, 3], self.recv.at[group, z, 3], (p.dp, z))

    def wide_copy(self, at):
        group = self.group
        sems = self.wide_send.at[group, at], self.wide_recv.at[group, at]
        target = (self.wide_flips[at], self.place.z)
        return remote(self.wide_out.at[at], self.wide_land.at[at], *sems, target)

    def start(self, z):
        self.core_copy(z).start()

    def add(self, target, rows, other):
        target[rows] = (target[rows].astype(HIGH) + other.astype(HIGH)).astype(LOW)

    def first(self, z):
        p = self.place
        self.core_copy(z).wait_recv()
        mine = self.grads[z, :, self.columns(p.core)]
        land = self.core_land.at[z]
        self.add(land, slice(None), mine)
        self.first_copy(z).start()

    def second(self, z):
        ahead, _, _, _ = self.axes(z)
        self.first_copy(z).wait_recv()
        land = self.core_land.at[z]
        self.add(land, self.rows(ahead * self.half, self.half), self.first_land[z])
        self.second_copy(z).start()

    def third(self, z):
        self.second_copy(z).wait_recv()
        land = self.core_land.at[z]
        self.add(land, self.kept(z), self.second_land[z])
        pl.when(z != self.place.z)(self.far_copy(z).start)

    def fourth(self):
        p = self.place
        total = self.core_land[p.z, self.kept(p.z)].astype(HIGH)
        for z in p.others:
            self.far_arrival(z).wait_recv()
            total = total + self.far_land[z].astype(HIGH)
        for at in range(len(self.wide_flips)):
            self.wide_out[at] = total.astype(LOW)
            copy = self.wide_copy(at)
            copy.start()
            copy.wait_recv()
            total = self.wide_out[at].astype(HIGH) + self.wide_land[at].astype(HIGH)
        self.piece[...] = total.astype(LOW)

    def finish(self):
        p = self.place
        for z in [p.z] + p.others:
            self.core_copy(z).wait_send()
            self.first_copy(z).wait_send()
            self.second_copy(z).wait_send()
        for z in p.others:
            self.far_copy(z).wait_send()
        for at in range(len(self.wide_flips)):
            self.wide_copy(at).wait_send()


class Return(Spread):
    def __init__(self, place, whole, pieces, send, recv, keep_sem, group, block):
        super().__init__(place, whole, send, recv, group, block)
        self.mine = pieces.at[self.matrix, pl.ds(self.base // 4, self.quarter)]
        p = place
        self.keep = pltpu.make_async_copy(self.mine, self.piece(0, p.a, p.b, p.core), keep_sem.at[group])

    def hand_out(self, z):
        super().hand_out(z)
        self.keep.start()

    def sent(self, z):
        super().sent(z)
        self.keep.wait()

    def odd(self, z):
        return lax.rem(self.place.z + self.group, 2)


class Several:
    def __init__(self, parts):
        self.parts = parts

    def __getattr__(self, name):
        def call(*arguments):
            for part in self.parts:
                getattr(part, name)(*arguments)

        return call


def backward_kernel(
    n_tensor,
    heads,
    scale,
    layer_input,
    segment_ids,
    norm1_gain,
    norm2_gain,
    norm2_bias,
    in_cotangent,
    in_w,
    in_q,
    in_k,
    in_v,
    in_totals,
    in_attended,
    in_activation,
    in_slope,
    in_hidden,
    in_xhat,
    in_inverse,
    in_second,
    out_layer,
    out_partial,
    out_landed,
    out_summed,
    out_sums,
    weights,
    core_land,
    first_land,
    second_land,
    far_land,
    pieces,
    activation,
    slope,
    row_input,
    bias,
    q_all,
    k_all,
    v_all,
    totals,
    attended,
    queries,
    keys,
    values,
    grad_mixed,
    grad_k,
    grad_v,
    inverse,
    live_rows,
    terms,
    hidden_low,
    grad_low,
    spare,
    landed,
    sums,
    sums_land,
    sums_far,
    send,
    recv,
    final_send,
    final_recv,
    wide_out,
    wide_land,
    wide_send,
    wide_recv,
    load_sem,
    weight_sem,
    stream_sem,
    term_send,
    term_recv,
    sums_send,
    sums_recv,
    save_sem,
    keep_sem,
):
    place = Place(n_tensor)
    share, length = hidden_low.shape[0], row_input.shape[0]
    shares_per_row = length // share
    group_rows = q_all.shape[2]
    size = group_rows // heads
    my_share = lax.rem(place.z, shares_per_row)
    in_row = pl.ds(pl.multiple_of(my_share * share, share), share)
    row_start = pl.multiple_of(place.z // shares_per_row * length, length)
    order = list(reversed(place.others)) + [place.z]
    bits = sums_land.shape[0]
    flips = [place.dp + (1 << bit) - (2 << bit) * lax.rem(place.dp // (1 << bit), 2) for bit in range(bits)]

    accum, xhat = terms.at[0], terms.at[1]

    def load(source, target, at):
        copy = pltpu.make_async_copy(source, target, load_sem.at[at])
        copy.start()
        return copy

    def weight_load(group, z):
        return pltpu.make_async_copy(in_w.at[group, z], weights.at[group, z], weight_sem.at[group, z])

    def stream(at, sources, first_sem):
        z, slot = place.pick(at, order), lax.rem(at, 2)
        return [
            pltpu.make_async_copy(source.at[z], target.at[slot], stream_sem.at[first_sem + index, slot])
            for index, (source, target) in enumerate(sources)
        ]

    ffn_streams = [(in_activation, activation), (in_slope, slope)]
    head_streams = [
        (in_q, q_all),
        (in_k, k_all),
        (in_v, v_all),
        (in_totals, totals),
        (in_attended, attended),
    ]

    early = [
        load(source, target, at)
        for at, (source, target) in enumerate(
            [(in_second, accum), (in_cotangent, spare.at[0]), (in_xhat, xhat), (in_inverse, inverse), (in_hidden, hidden_low)]
        )
    ]
    for copy in stream(0, ffn_streams, 0):
        copy.start()
    for z in order:
        weight_load(2, z).start()
        weight_load(1, z).start()
    late = load(layer_input.at[pl.ds(row_start, length)], row_input, 5)
    for z in order:
        weight_load(0, z).start()
    for copy in stream(0, head_streams, 2):
        copy.start()
    meet([(flip, place.z) for flip in flips] + [(place.dp, z) for z in place.others])
    lands = (core_land, first_land, second_land, far_land)
    wide = (flips[3:], wide_out, wide_land, wide_send, wide_recv)
    width = row_input.shape[1]
    blocks = [(0, 0, width // 2), (0, width // 2, width // 2), (1, 0, width), (2, 0, width)]
    reduces = [
        Reduce(place, weights, lands, pieces, send, recv, wide, group, block)
        for group, block in enumerate(blocks)
    ]
    returns = [
        Return(place, out_summed, pieces, final_send, final_recv, keep_sem, group, block)
        for group, block in enumerate(blocks)
    ]
    reduce_a, reduce_b, reduce_c = Several(reduces[:2]), reduces[2], reduces[3]
    return_a, return_b, return_c = Several(returns[:2]), returns[2], returns[3]
    sums[0] = jnp.zeros(sums.shape[1:], HIGH)
    own_start = pl.multiple_of(place.z * share, share)
    own_segments, row_segments = segment_rows(segment_ids, own_start, share, row_start, length)
    bias[...] = segment_bias(own_segments, row_segments)
    live_rows[...] = (own_segments >= 0).astype(HIGH)
    gain_first, gain_second, shift_second = as_row(norm1_gain), as_row(norm2_gain), as_row(norm2_bias)

    for copy in early:
        copy.wait()
    band = min(128, share)

    def second_norm(at, carry):
        rows = pl.ds(pl.multiple_of(at * band, band), band)
        normed, spread = norm_forward(accum[rows])
        cotangent = spare[0, rows].astype(HIGH) * live_rows[rows]
        spare[0, rows] = (normed * gain_second + shift_second).astype(LOW)
        grad_second = norm_backward(normed, spread, cotangent * gain_second)
        sums[0, 0, 6:7] += column_sum(cotangent * normed)
        sums[0, 0, 7:8] += column_sum(cotangent)
        sums[0, 0, 5:6] += column_sum(grad_second)
        grad_low[rows] = grad_second.astype(LOW)
        accum[rows] = grad_second
        return carry

    lax.fori_loop(0, share // band, second_norm, 0)
    save_layer = pltpu.make_async_copy(spare.at[0], out_layer, save_sem.at[0])
    save_layer.start()

    def feed_forward(at, carry):
        z, slot = place.pick(at, order), lax.rem(at, 2)
        before = place.pick(at - 1, order)

        @pl.when(at + 1 < n_tensor)
        def _():
            for copy in stream(at + 1, ffn_streams, 0):
                copy.start()

        for copy in stream(at, ffn_streams, 0):
            copy.wait()
        weight_load(2, z).wait()
        low = grad_low[...]
        grad_up = (dot_nt(low, weights[2, z]) * slope[slot].astype(HIGH)).astype(LOW)
        weights[2, z] = dot_tn(activation[slot], low).astype(LOW)
        reduce_c.start(z)
        pl.when(at >= 1)(functools.partial(reduce_b.first, before))
        pl.when(at >= 3)(functools.partial(reduce_b.second, order[0]))
        weight_load(1, z).wait()
        accum[...] += dot_nt(grad_up, weights[1, z])
        weights[1, z] = dot_tn(hidden_low[...], grad_up).astype(LOW)
        reduce_b.start(z)
        sums[0, z, 1:2] = column_sum(grad_up.astype(HIGH))
        reduce_c.first(z)
        pl.when(at == 2)(functools.partial(reduce_c.second, order[0]))
        return carry

    lax.fori_loop(0, n_tensor, feed_forward, 0)

    def first_norm(at, carry):
        rows = pl.ds(pl.multiple_of(at * band, band), band)
        grad_hidden, normed = accum[rows], xhat[rows]
        grad_first = norm_backward(normed, inverse[rows], grad_hidden * gain_first)
        sums[0, 0, 2:3] += column_sum(grad_first)
        sums[0, 0, 3:4] += column_sum(grad_hidden * normed)
        sums[0, 0, 4:5] += column_sum(grad_hidden)
        accum[rows] = grad_first
        grad_low[rows] = grad_first.astype(LOW)
        return carry

    lax.fori_loop(0, share // band, first_norm, 0)
    for index in range(shares_per_row):
        terms[1 + index] = jnp.zeros(accum.shape, HIGH)
    reduce_b.first(order[-1])
    late.wait()

    def finish_c():
        reduce_c.fourth()
        return_c.hand_out(0)

    def finish_b():
        reduce_b.fourth()
        return_b.hand_out(0)

    term_copies = []
    for step in range(1, shares_per_row):
        partner = place.z - my_share + lax.rem(my_share + step, shares_per_row)
        sems = term_send.at[step - 1], term_recv.at[step - 1]
        term_copies.append(remote(spare.at[step - 1], landed.at[step - 1], *sems, (place.dp, partner)))

    def send_terms():
        save_layer.wait()
        for step in range(1, shares_per_row):
            spare[step - 1] = terms[1 + lax.rem(my_share + step, shares_per_row)].astype(LOW)
            term_copies[step - 1].start()

    def attend(at, carry):
        z, slot = place.pick(at, order), lax.rem(at, 2)
        after = place.pick(at + 1, order)
        before = place.pick(at - 1, order)

        @pl.when(at + 1 < n_tensor)
        def _():
            for copy in stream(at + 1, head_streams, 2):
                copy.start()

        for copy in stream(at, head_streams, 2):
            copy.wait()
        weight_load(0, z).wait()
        incoming = dot_nt(grad_low[...], weights[0, z, 3 * group_rows :]).astype(LOW)
        weights[0, z, 3 * group_rows :] = dot_tn(attended[slot], grad_low[...]).astype(LOW)
        for head in range(heads):
            part = slice(head * size, (head + 1) * size)
            queries[head], keys[head] = q_all[slot, :, part], k_all[slot, :, part]
            values[head], grad_mixed[head] = v_all[slot, :, part], incoming[:, part]
        pl.when(at >= 1)(functools.partial(reduce_a.first, before))

        def one_head(head, inner):
            k, v = keys[head], values[head]
            grad_kt = jnp.zeros((size, length), HIGH)
            grad_vt = jnp.zeros((size, length), HIGH)
            chunk = min(256, share)
            for start in range(0, share, chunk):
                rows = pl.ds(start, chunk)
                q, up = queries[head, rows], grad_mixed[head, rows]
                chance = jnp.exp(dot_nt(q, k) + bias[rows] - totals[slot, head, rows])
                change = chance * dot_nt(up, v)
                change = change - chance * jnp.sum(change, axis=-1, keepdims=True)
                change = change.astype(LOW)
                grad_kt = grad_kt + dot_nn(q.T, change)
                grad_vt = grad_vt + dot_nn(up.T, chance.astype(LOW))
                grad_mixed[head, rows] = (dot_nn(change, k) * scale).astype(LOW)
            grad_k[head] = grad_kt.astype(LOW)
            grad_v[head] = grad_vt.astype(LOW)

            @pl.when(head == 0)
            def _():
                reduce_c.third(z)
                pl.when(at + 1 < n_tensor)(functools.partial(reduce_c.second, after))

            @pl.when(head == 1)
            def _():
                reduce_b.third(z)
                pl.when(at == n_tensor - 1)(finish_c)
                pl.when(at >= 2)(functools.partial(reduce_a.third, place.pick(at - 2, order)))

            @pl.when(head == 2)
            def _():
                pl.when(at + 1 < n_tensor)(functools.partial(reduce_b.second, after))
                pl.when(at == n_tensor - 1)(finish_b)
                pl.when(at >= 1)(functools.partial(reduce_a.second, before))

            return inner

        lax.fori_loop(0, heads, one_head, 0)
        dq = jnp.concatenate([grad_mixed[head] for head in range(heads)], axis=-1)
        dk = grad_k[...].reshape(group_rows, length)
        dv = grad_v[...].reshape(group_rows, length)
        x_row = row_input[...]
        q_rows, k_rows, v_rows = (
            jnp.concatenate([weights[0, z, pl.ds((3 * head + kind) * size, size)] for head in range(heads)], axis=0)
            for kind in range(3)
        )
        for index in range(shares_per_row):
            tokens = slice(index * share, (index + 1) * share)
            terms[1 + index] += dot_tn(dk[:, tokens], k_rows) + dot_tn(dv[:, tokens], v_rows)
        pl.when(at == n_tensor - 1)(send_terms)
        accum[...] += dot_nn(dq, q_rows)
        for kind, (left, right) in enumerate(((dq.T, row_input[in_row]), (dk, x_row), (dv, x_row))):
            grad = dot_nn(left, right).astype(LOW)
            for head in range(heads):
                weights[0, z, pl.ds((3 * head + kind) * size, size)] = grad[head * size : (head + 1) * size]
        reduce_a.start(z)
        ones = jnp.ones((8, length), LOW)
        q_sums, v_sums = dot_nn(ones[:, :share], dq)[0:1], dot_nt(ones, dv)[0:1]
        for head in range(heads):
            part = slice(head * size, (head + 1) * size)
            pair = jnp.concatenate([q_sums[:, part], v_sums[:, part]], axis=1)
            sums[0, z, 0:1, 2 * head * size : 2 * (head + 1) * size] = pair
        return carry

    lax.fori_loop(0, n_tensor, attend, 0)

    accum[...] += terms[1 + my_share]
    save_partial = pltpu.make_async_copy(accum, out_partial, save_sem.at[1])
    save_partial.start()

    def sum_copy(bit):
        return remote(
            sums.at[bit], sums_land.at[bit], sums_send.at[bit], sums_recv.at[bit], (flips[bit], place.z)
        )

    def fold(bit):
        sum_copy(bit).wait_recv()
        sums[bit + 1] = sums[bit] + sums_land[bit]

    def far_sum(z):
        sems = sums_send.at[bits + z], sums_recv.at[bits + place.z]
        return remote(sums.at[bits, z], sums_far.at[place.z], *sems, (place.dp, z))

    def far_sum_arrival(z):
        sems = sums_send.at[bits + z], sums_recv.at[bits + z]
        return remote(sums.at[bits, z], sums_far.at[z], *sems, (place.dp, z))

    for z in range(1, n_tensor):
        sums[0, z, 2:8] = sums[0, 0, 2:8]
    sum_copy(0).start()
    reduce_a.first(order[3])
    reduce_a.third(order[2])
    fold(0)
    sum_copy(1).start()
    return_c.second(0)
    return_b.second(0)
    reduce_a.second(order[3])
    fold(1)
    sum_copy(2).start()
    return_c.third(0)
    return_b.third(0)
    reduce_a.third(order[3])
    reduce_a.fourth()
    return_a.hand_out(0)
    for bit in range(2, bits):
        fold(bit)
        if bit + 1 < bits:
            sum_copy(bit + 1).start()
    for z in place.others:
        far_sum(z).start()
    sums_far[place.z] = sums[bits, place.z]
    return_c.last(0)
    return_b.last(0)
    return_a.second(0)
    for copy in term_copies:
        copy.wait_recv()
    save_landed = pltpu.make_async_copy(landed, out_landed, save_sem.at[5])
    save_landed.start()
    return_a.third(0)
    for z in place.others:
        far_sum_arrival(z).wait_recv()
    total = sums_far[0]
    for z in range(1, n_tensor):
        total = total + sums_far[z]
    out_sums[...] = total
    return_a.last(0)
    save_partial.wait()
    save_landed.wait()
    for copy in term_copies:
        copy.wait_send()
    for bit in range(bits):
        sum_copy(bit).wait_send()
    for z in place.others:
        far_sum(z).wait_send()
    for reduce in reduces:
        reduce.finish()
    for part in returns:
        part.sent(0)


def finish_kernel(
    heads,
    in_layer,
    in_partial,
    in_landed,
    in_summed,
    sums,
    out_layer,
    out_input,
    out_qkv,
    qv_bias,
    out_out,
    out_bias,
    gain_first,
    shift_first,
    out_up,
    up_bias,
    out_down,
    down_bias,
    gain_second,
    shift_second,
    layer,
    partial,
    landed,
    summed,
    qkv,
    rest,
    matrices,
    load_sem,
    save_sem,
):
    size = qkv.shape[1]
    pairs = [(in_summed.at[2, 0], summed.at[2]), (in_summed.at[1, 0], summed.at[1]), (in_partial, partial)]
    pairs += [(in_landed, landed), (in_summed.at[0, 0], summed.at[0]), (in_layer, layer)]
    loads = [
        pltpu.make_async_copy(source, target, load_sem.at[at]) for at, (source, target) in enumerate(pairs)
    ]
    for copy in loads:
        copy.start()
    for at, vector in enumerate(
        [up_bias, out_bias, gain_first, shift_first, down_bias, gain_second, shift_second]
    ):
        vector[...] = sums[1 + at : 2 + at].reshape(vector.shape)
    for head in range(heads):
        width = qv_bias.shape[1]
        qv_bias[head : head + 1] = sums[0:1, head * width : (head + 1) * width]
    saves = []

    def save(source, target):
        copy = pltpu.make_async_copy(source, target, save_sem.at[len(saves)])
        copy.start()
        saves.append(copy)

    for at, target in ((2, out_down), (1, out_up)):
        loads[2 - at].wait()
        matrices[at - 1] = summed[at].astype(HIGH)
        save(matrices.at[at - 1], target)
    loads[2].wait()
    loads[3].wait()
    for step in range(landed.shape[0]):
        partial[...] += landed[step].astype(HIGH)
    save(partial, out_input)
    loads[4].wait()
    rest[...] = summed[0, heads * size :].astype(HIGH)
    save(rest, out_out)
    for head in range(heads):
        qkv[head] = summed[0, head * size : (head + 1) * size].astype(HIGH)
    save(qkv, out_qkv)
    loads[5].wait()
    save(layer, out_layer)
    for copy in saves:
        copy.wait()


def on_device(
    layer_input,
    segment_ids,
    w_qkv,
    qv_bias,
    w_out,
    out_bias,
    norm1_gain,
    norm1_bias,
    w_up,
    up_bias,
    w_down,
    down_bias,
    norm2_gain,
    norm2_bias,
    out_cotangent,
):
    n_tensor = lax.axis_size("tensor")
    place = lax.axis_index("tensor")
    n_dp = lax.axis_size("dp")
    bits = n_dp.bit_length() - 1
    tokens, width = layer_input.shape
    share = tokens // n_tensor
    heads = qv_bias.shape[0]
    head_dim = qv_bias.shape[1] // 2
    score_scale = float(head_dim) ** (-0.5)
    shares_per_row = SEQ // share
    group_rows = heads * head_dim

    local_qkv = w_qkv.transpose(1, 2, 0).reshape(3 * group_rows, width)
    local_small = jnp.concatenate(
        [
            jnp.pad(qv_bias[:, :head_dim].reshape(1, -1), ((0, 0), (0, width - group_rows))),
            jnp.pad(qv_bias[:, head_dim:].reshape(1, -1), ((0, 0), (0, width - group_rows))),
            up_bias.reshape(1, -1),
            jnp.zeros((5, width), LOW),
        ]
    ).astype(HIGH)

    vmem = pl.BlockSpec(memory_space=pltpu.VMEM)
    anywhere = pl.BlockSpec(memory_space=pl.ANY)

    def low(*shape):
        return jax.ShapeDtypeStruct(shape, LOW)

    def high(*shape):
        return jax.ShapeDtypeStruct(shape, HIGH)

    def low_scratch(*shape):
        return pltpu.VMEM(shape, LOW)

    def high_scratch(*shape):
        return pltpu.VMEM(shape, HIGH)

    dma = pltpu.SemaphoreType.DMA
    whole = (3, n_tensor, width, width)
    (w, q, k, v, totals, attended, activation, slope, small, hidden, xhat, inverse, second_sum) = pl.pallas_call(
        functools.partial(forward_kernel, n_tensor, heads, score_scale),
        out_shape=(
            low(*whole),
            low(n_tensor, share, group_rows),
            low(n_tensor, SEQ, group_rows),
            low(n_tensor, SEQ, group_rows),
            high(n_tensor, heads, share, 1),
            low(n_tensor, share, group_rows),
            low(n_tensor, share, width),
            low(n_tensor, share, width),
            high(n_tensor, 8, width),
            low(share, width),
            high(share, width),
            high(share, 1),
            high(share, width),
        ),
        in_specs=[anywhere, vmem] + [anywhere] * 4 + [vmem] * 5,
        out_specs=(anywhere,) * 8 + (vmem,) * 5,
        scratch_shapes=[
            low_scratch(*whole),
            low_scratch(SEQ, width),
            high_scratch(share, SEQ),
            low_scratch(n_tensor, share, group_rows),
            low_scratch(n_tensor, SEQ, group_rows),
            low_scratch(n_tensor, SEQ, group_rows),
            high_scratch(n_tensor, heads, share, 1),
            low_scratch(n_tensor, share, group_rows),
            low_scratch(n_tensor, share, width),
            low_scratch(n_tensor, share, width),
            low_scratch(heads, share, head_dim),
            low_scratch(heads, SEQ, head_dim),
            low_scratch(heads, SEQ, head_dim),
            low_scratch(heads, share, head_dim),
            dma((3, n_tensor, 9)),
            dma((3, n_tensor, 8)),
            dma((n_tensor,)),
            dma((n_tensor,)),
            dma((5,)),
            dma((24,)),
            dma((4, n_tensor)),
        ],
        compiler_params=pltpu.CompilerParams(
            collective_id=0, has_side_effects=True, vmem_limit_bytes=VMEM_LIMIT
        ),
        name="forward",
    )(
        layer_input,
        segment_ids,
        local_qkv,
        w_out,
        w_up,
        w_down,
        local_small,
        out_bias,
        norm1_gain,
        norm1_bias,
        down_bias,
    )

    half, side = width // 2, width // 2
    quarter = width // 4
    wide = max(bits - 3, 1)
    layer_output, partial, landed, summed, sums = pl.pallas_call(
        functools.partial(backward_kernel, n_tensor, heads, score_scale),
        out_shape=(
            low(share, width),
            high(share, width),
            low(shares_per_row - 1, share, width),
            low(3, 1, width, width),
            high(8, width),
        ),
        in_specs=[anywhere] + [vmem] * 4 + [anywhere] * 13,
        out_specs=(anywhere,) * 4 + (vmem,),
        scratch_shapes=[
            low_scratch(*whole),
            low_scratch(3, n_tensor, width, side),
            low_scratch(3, n_tensor, half, side),
            low_scratch(3, n_tensor, quarter, side),
            low_scratch(3, n_tensor, quarter, side),
            low_scratch(3, quarter, side),
            low_scratch(2, share, width),
            low_scratch(2, share, width),
            low_scratch(SEQ, width),
            high_scratch(share, SEQ),
            low_scratch(2, share, group_rows),
            low_scratch(2, SEQ, group_rows),
            low_scratch(2, SEQ, group_rows),
            high_scratch(2, heads, share, 1),
            low_scratch(2, share, group_rows),
            low_scratch(heads, share, head_dim),
            low_scratch(heads, SEQ, head_dim),
            low_scratch(heads, SEQ, head_dim),
            low_scratch(heads, share, head_dim),
            low_scratch(heads, head_dim, SEQ),
            low_scratch(heads, head_dim, SEQ),
            high_scratch(share, 1),
            high_scratch(share, 1),
            high_scratch(1 + shares_per_row, share, width),
            low_scratch(share, width),
            low_scratch(share, width),
            low_scratch(shares_per_row - 1, share, width),
            low_scratch(shares_per_row - 1, share, width),
            high_scratch(bits + 1, n_tensor, 8, width),
            high_scratch(bits, n_tensor, 8, width),
            high_scratch(n_tensor, 8, width),
            dma((4, n_tensor, 4)),
            dma((4, n_tensor, 4)),
            dma((4, 1, 9)),
            dma((4, 1, 8)),
            low_scratch(3, wide, quarter, side),
            low_scratch(3, wide, quarter, side),
            dma((4, wide)),
            dma((4, wide)),
            dma((8,)),
            dma((3, n_tensor)),
            dma((7, 2)),
            dma((shares_per_row - 1,)),
            dma((shares_per_row - 1,)),
            dma((bits + n_tensor,)),
            dma((bits + n_tensor,)),
            dma((6,)),
            dma((4,)),
        ],
        compiler_params=pltpu.CompilerParams(
            collective_id=1, has_side_effects=True, vmem_limit_bytes=VMEM_LIMIT
        ),
        name="backward",
    )(
        layer_input,
        segment_ids,
        norm1_gain,
        norm2_gain,
        norm2_bias,
        out_cotangent,
        w,
        q,
        k,
        v,
        totals,
        attended,
        activation,
        slope,
        hidden,
        xhat,
        inverse,
        second_sum,
    )

    vector = high(width)
    matrix = high(width, width)
    layer_output, input_grad, grad_qkv, *rest = pl.pallas_call(
        functools.partial(finish_kernel, heads),
        out_shape=(
            low(share, width),
            high(share, width),
            high(heads, 3 * head_dim, width),
            high(heads, 2 * head_dim),
            high(group_rows, width),
            vector,
            vector,
            vector,
            matrix,
            vector,
            matrix,
            vector,
            vector,
            vector,
        ),
        in_specs=[anywhere] * 4 + [vmem],
        out_specs=(anywhere,) * 3 + (vmem, anywhere, vmem, vmem, vmem, anywhere, vmem, anywhere, vmem, vmem, vmem),
        scratch_shapes=[
            low_scratch(share, width),
            high_scratch(share, width),
            low_scratch(shares_per_row - 1, share, width),
            low_scratch(3, width, width),
            high_scratch(heads, 3 * head_dim, width),
            high_scratch(group_rows, width),
            high_scratch(2, width, width),
            dma((6,)),
            dma((6,)),
        ],
        compiler_params=pltpu.CompilerParams(vmem_limit_bytes=VMEM_LIMIT),
        name="finish",
    )(layer_output, partial, landed, summed, sums)
    return (layer_output, input_grad, grad_qkv.transpose(2, 0, 1), *rest)


def solution(mesh):
    return jax.shard_map(
        on_device,
        mesh=mesh,
        in_specs=(
            P("dp", None),
            P("dp"),
            P(None, "tensor", None),
            P("tensor", None),
            P("tensor", None),
            P(),
            P(),
            P(),
            P(None, "tensor"),
            P("tensor"),
            P("tensor", None),
            P(),
            P(),
            P(),
            P(("dp", "tensor"), None),
        ),
        out_specs=(
            P(("dp", "tensor"), None),
            P(("dp", "tensor"), None),
            P(None, "tensor", None),
            P("tensor", None),
            P("tensor", None),
            P(),
            P(),
            P(),
            P(None, "tensor"),
            P("tensor"),
            P("tensor", None),
            P(),
            P(),
            P(),
        ),
        check_vma=False,
    )
```

```python
import functools

import jax
import jax.numpy as jnp
from jax import lax
from jax.experimental import pallas as pl
from jax.experimental.pallas import tpu as pltpu
from jax.sharding import PartitionSpec as P

SEQ = 1024


EPSILON = 1e-06
MASKED = -1e30
LOW = jnp.bfloat16
HIGH = jnp.float32
MESH = pl.DeviceIdType.MESH
VMEM_LIMIT = 127 * 512 * 1024


def dot_nn(left, right):
    return lax.dot_general(left, right, (((1,), (0,)), ((), ())), preferred_element_type=HIGH)


def dot_nt(left, right):
    return lax.dot_general(left, right, (((1,), (1,)), ((), ())), preferred_element_type=HIGH)


def dot_tn(left, right):
    return lax.dot_general(left, right, (((0,), (0,)), ((), ())), preferred_element_type=HIGH)


def norm_forward(summed):
    mean = jnp.mean(summed, axis=-1, keepdims=True)
    centred = summed - mean
    spread = jnp.mean(centred * centred, axis=-1, keepdims=True)
    inverse = lax.rsqrt(spread + EPSILON)
    return centred * inverse, inverse


def norm_backward(xhat, inverse, scaled):
    return inverse * (
        scaled
        - jnp.mean(scaled, axis=-1, keepdims=True)
        - xhat * jnp.mean(scaled * xhat, axis=-1, keepdims=True)
    )


def gelu_parts(u):
    phi_cdf = 0.5 * (1.0 + lax.erf(u * (2.0**-0.5)))
    density = jnp.exp(-0.5 * u * u) * 0.3989422804014327
    return u * phi_cdf, phi_cdf + u * density


def column_sum(values):
    return jnp.sum(values, axis=0, keepdims=True)


def as_row(vector):
    return vector[...].astype(HIGH).reshape(1, -1)


def as_column(row):
    return jnp.broadcast_to(row, (8, row.shape[1])).T[:, :1]


def segment_rows(segment_ids, own_start, share, row_start, length):
    own = segment_ids[pl.ds(own_start, share)].astype(HIGH).reshape(1, share)
    return as_column(own), segment_ids[pl.ds(row_start, length)].astype(HIGH).reshape(1, length)


def segment_bias(own_segments, row_segments):
    return jnp.where(own_segments == row_segments, 0.0, MASKED)


class Place:
    def __init__(self, n_tensor):
        self.n_tensor = n_tensor
        self.z = lax.axis_index("tensor")
        self.dp = lax.axis_index("dp")
        self.core = lax.rem(self.dp, 2)
        self.a = lax.rem(self.dp // 2, 2)
        self.b = lax.rem(self.dp // 4, 2)
        self.to_core = (self.dp + 1 - 2 * self.core, self.z)
        self.to_a = (self.dp + 2 - 4 * self.a, self.z)
        self.to_b = (self.dp + 4 - 8 * self.b, self.z)
        self.others = [lax.rem(self.z + step, n_tensor) for step in range(1, n_tensor)]
        if n_tensor == 4:
            near = self.z + 1 - 2 * lax.rem(self.z, 2)
            upper = self.z // 2
            self.others = [near, 2 - upper, 3 - 3 * upper]

    def pick(self, at, order):
        chosen = order[0]
        for index in range(1, len(order)):
            chosen = jnp.where(at == index, order[index], chosen)
        return chosen


def greet(partners):
    barrier = pltpu.get_barrier_semaphore()
    for partner in partners:
        pl.semaphore_signal(barrier, inc=1, device_id=partner, device_id_type=MESH)


def meet(partners):
    pl.semaphore_wait(pltpu.get_barrier_semaphore(), len(partners))


def remote(src, dst, send, recv, target):
    return pltpu.make_async_remote_copy(
        src_ref=src,
        dst_ref=dst,
        send_sem=send,
        recv_sem=recv,
        device_id=target,
        device_id_type=MESH,
    )


class Spread:
    def __init__(self, place, whole, send, recv, group, block):
        self.place, self.whole, self.send, self.recv, self.group = place, whole, send, recv, group
        self.matrix, self.base, size = block
        self.mine = None
        self.quarter = size // 4
        self.half = whole.shape[3] // 2

    def odd(self, z):
        return lax.rem(z + self.group, 2)

    def piece(self, z, a, b, side):
        odd = self.odd(z)
        row = odd * (2 * b + a) + (1 - odd) * (2 * a + b)
        rows = pl.ds(pl.multiple_of(self.base + row * self.quarter, 16), self.quarter)
        return self.whole.at[self.matrix, z, rows, pl.ds(pl.multiple_of(side * self.half, 128), self.half)]

    def pass_on(self, z, slot, a, b, side, target):
        part = self.piece(z, a, b, side)
        send = self.send.at[self.group, z, slot]
        recv = self.recv.at[self.group, z, slot % 8]
        source = self.mine if self.mine is not None and slot in (1, 2, 4) else part
        return remote(source, part, send, recv, target)

    def turn(self, z):
        p = self.place
        odd = self.odd(z)
        a = p.a * odd + (1 - p.a) * (1 - odd)
        b = p.b * (1 - odd) + (1 - p.b) * odd
        target = odd * p.to_a[0] + (1 - odd) * p.to_b[0]
        return self.pass_on(z, 3, a, b, p.core, (target, p.z))

    def hand_out(self, z):
        p = self.place
        self.pass_on(z, 1, p.a, p.b, p.core, p.to_a).start()
        self.pass_on(z, 2, p.a, p.b, p.core, p.to_b).start()
        self.pass_on(z, 4, p.a, p.b, p.core, p.to_core).start()

    def second(self, z):
        p = self.place
        self.pass_on(z, 1, 1 - p.a, p.b, p.core, p.to_a).wait_recv()
        self.pass_on(z, 2, p.a, 1 - p.b, p.core, p.to_b).wait_recv()
        self.turn(z).start()
        self.pass_on(z, 5, 1 - p.a, p.b, p.core, p.to_core).start()
        self.pass_on(z, 6, p.a, 1 - p.b, p.core, p.to_core).start()

    def third(self, z):
        p = self.place
        self.pass_on(z, 3, 1 - p.a, 1 - p.b, p.core, p.to_a).wait_recv()
        self.pass_on(z, 7, 1 - p.a, 1 - p.b, p.core, p.to_core).start()

    def last(self, z):
        p = self.place
        side = 1 - p.core
        self.pass_on(z, 4, p.a, p.b, side, p.to_core).wait_recv()
        self.pass_on(z, 5, 1 - p.a, p.b, side, p.to_core).wait_recv()
        self.pass_on(z, 6, p.a, 1 - p.b, side, p.to_core).wait_recv()
        self.pass_on(z, 7, 1 - p.a, 1 - p.b, side, p.to_core).wait_recv()

    def sent(self, z):
        p = self.place
        self.pass_on(z, 1, p.a, p.b, p.core, p.to_a).wait_send()
        self.pass_on(z, 2, p.a, p.b, p.core, p.to_b).wait_send()
        self.turn(z).wait_send()
        self.pass_on(z, 4, p.a, p.b, p.core, p.to_core).wait_send()
        self.pass_on(z, 5, 1 - p.a, p.b, p.core, p.to_core).wait_send()
        self.pass_on(z, 6, p.a, 1 - p.b, p.core, p.to_core).wait_send()
        self.pass_on(z, 7, 1 - p.a, 1 - p.b, p.core, p.to_core).wait_send()


class Gather(Spread):
    def along(self, z):
        p = self.place
        part = self.piece(p.z, p.a, p.b, p.core)
        send, recv = self.send.at[self.group, z, 0], self.recv.at[self.group, p.z, 0]
        return remote(part, part, send, recv, (p.dp, z))

    def onward(self, z):
        p = self.place
        target = jnp.where(z < p.z, p.z + 1, p.z - 1)
        copy = self.pass_on(z, 8, p.a, p.b, p.core, (p.dp, target))
        return (target >= 0) & (target < p.n_tensor), copy

    def start(self):
        p = self.place
        for z in (p.z - 1, p.z + 1):
            pl.when((z >= 0) & (z < p.n_tensor))(self.along(z).start)

    def first(self, z):
        p = self.place
        self.pass_on(z, 0, p.a, p.b, p.core, p.to_core).wait_recv()
        there, copy = self.onward(z)
        pl.when(there)(copy.start)
        self.hand_out(z)

    def finish(self):
        p = self.place
        for z in (p.z - 1, p.z + 1):
            pl.when((z >= 0) & (z < p.n_tensor))(self.along(z).wait_send)
        for z in p.others:
            there, copy = self.onward(z)
            pl.when(there)(copy.wait_send)
            self.sent(z)


FORWARD_PLAN = (
    {
        4: (0,),
        19: (100, 1, 10, 200, 2, 300,),
        10: (101,),
        11: (11,),
        14: (110,),
        29: (12, 102, 201, 301,),
        20: (111,),
        21: (20,),
        23: (210,),
        39: (310, 202, 21, 112, 302,),
        30: (211,),
        31: (22,),
        33: (311,),
        34: (120,),
        40: (121, 212,),
        41: (312, 122, 220, 221, 320,),
        42: (222, 321,),
        43: (322,),
    },
    {
        4: (0, 1,),
        19: (2, 100, 10, 11, 101, 12, 102, 200, 300,),
        10: (110,),
        12: (20,),
        13: (111,),
        29: (202, 201, 21, 302, 301,),
        20: (22, 112, 210,),
        23: (120,),
        24: (310,),
        30: (211,),
        33: (311,),
        35: (121,),
        40: (122, 212,),
        41: (220, 312, 320,),
        42: (221, 222, 321,),
        43: (322,),
    },
)


def in_bands(start, count, work):
    band = 96

    def one(at, carry):
        offset = pl.multiple_of(at * band, 16)
        work(pl.ds(pl.multiple_of(start + offset, 16), band), pl.ds(offset, band))
        return carry

    lax.fori_loop(0, count // band, one, 0)


class Reduce:
    def __init__(self, place, grads, lands, pieces, send, recv, wide, group, block, near_land=None):
        matrix, base, size = block
        self.near_land = near_land
        self.near = place.others[0]
        self.far = place.others if near_land is None else place.others[1:]
        self.place, self.send, self.recv, self.group = place, send, recv, group
        self.half, self.quarter, self.side = size // 2, size // 4, grads.shape[3] // 2

        def rows(ref, parts):
            return ref.at[matrix, :, pl.ds(base // parts, size // parts)]

        core_land, first_land, second_land, far_land = lands
        self.grads = rows(grads, 1)
        self.core_land = core_land.at[max(matrix - 1, 0)]
        self.first_land, self.second_land, self.far_land = (
            rows(first_land, 2),
            rows(second_land, 4),
            rows(far_land, 4),
        )
        self.piece = pieces.at[matrix, pl.ds(base // 4, size // 4)]
        self.wide_flips, wide_out, wide_land, self.wide_send, self.wide_recv = wide
        if self.wide_flips:
            self.wide_out, self.wide_land = rows(wide_out, 4), rows(wide_land, 4)

    def columns(self, side):
        return pl.ds(pl.multiple_of(side * self.side, 128), self.side)

    def axes(self, z):
        p = self.place
        odd = lax.rem(z + self.group, 2)
        ahead, behind = odd * p.b + (1 - odd) * p.a, odd * p.a + (1 - odd) * p.b
        to_first = odd * p.to_b[0] + (1 - odd) * p.to_a[0]
        to_second = odd * p.to_a[0] + (1 - odd) * p.to_b[0]
        return ahead, behind, (to_first, p.z), (to_second, p.z)

    def rows(self, start, size):
        return pl.ds(pl.multiple_of(start, 16), size)

    def copy(self, z, slot, source, target_ref, target):
        send, recv = self.send.at[self.group, z, slot], self.recv.at[self.group, z, slot]
        return remote(source, target_ref, send, recv, target)

    def core_copy(self, z):
        p = self.place
        source = self.grads.at[z, :, self.columns(1 - p.core)]
        return self.copy(z, 0, source, self.core_land.at[z], p.to_core)

    def first_copy(self, z):
        ahead, _, target, _ = self.axes(z)
        source = self.core_land.at[z, self.rows((1 - ahead) * self.half, self.half)]
        return self.copy(z, 1, source, self.first_land.at[z], target)

    def second_copy(self, z):
        ahead, behind, _, target = self.axes(z)
        start = ahead * self.half + (1 - behind) * self.quarter
        source = self.core_land.at[z, self.rows(start, self.quarter)]
        return self.copy(z, 2, source, self.second_land.at[z], target)

    def kept_start(self, z):
        ahead, behind, _, _ = self.axes(z)
        return ahead * self.half + behind * self.quarter

    def kept(self, z):
        return self.rows(self.kept_start(z), self.quarter)

    def far_slot(self, source, target):
        return lax.rem(source - target + self.place.n_tensor, self.place.n_tensor) - 1

    def far_copy(self, z):
        p, group = self.place, self.group
        source = self.core_land.at[z, self.kept(z)]
        send, recv = self.send.at[group, z, 3], self.recv.at[group, p.z, 3]
        return remote(source, self.far_land.at[self.far_slot(p.z, z)], send, recv, (p.dp, z))

    def far_arrival(self, z):
        p, group = self.place, self.group
        land = self.far_land.at[self.far_slot(z, p.z)]
        return remote(land, land, self.send.at[group, z, 3], self.recv.at[group, z, 3], (p.dp, z))

    def wide_copy(self, at):
        group = self.group
        sems = self.wide_send.at[group, at], self.wide_recv.at[group, at]
        target = (self.wide_flips[at], self.place.z)
        return remote(self.wide_out.at[at], self.wide_land.at[at], *sems, target)

    def start(self, z):
        self.core_copy(z).start()

    def add(self, target, start, count, other):
        def work(rows, part):
            target[rows] = target[rows] + other[part]

        in_bands(start, count, work)

    def near_copy(self):
        p, group = self.place, self.group
        sems = self.send.at[group, self.near, 3], self.recv.at[group, p.z, 3]
        return remote(self.core_land.at[self.near], self.near_land, *sems, (p.dp, self.near))

    def near_arrival(self):
        p, group = self.place, self.group
        sems = self.send.at[group, self.near, 3], self.recv.at[group, self.near, 3]
        return remote(self.near_land, self.near_land, *sems, (p.dp, self.near))

    def first(self, z):
        p = self.place
        self.core_copy(z).wait_recv()
        mine = self.grads.at[z, :, self.columns(p.core)]
        land = self.core_land.at[z]
        self.add(land, 0, 2 * self.half, mine)
        if self.near_land is not None and z is self.near:
            self.near_copy().start()
            return
        if self.near_land is not None and z is p.z:
            self.near_arrival().wait_recv()
            self.add(land, 0, 2 * self.half, self.near_land)
        self.first_copy(z).start()

    def second(self, z):
        ahead, _, _, _ = self.axes(z)
        self.first_copy(z).wait_recv()
        land = self.core_land.at[z]
        self.add(land, ahead * self.half, self.half, self.first_land.at[z])
        self.second_copy(z).start()

    def third(self, z):
        self.second_copy(z).wait_recv()
        land = self.core_land.at[z]
        self.add(land, self.kept_start(z), self.quarter, self.second_land.at[z])
        if z is not self.place.z:
            self.far_copy(z).start()

    def fourth(self):
        p = self.place
        for z in self.far:
            self.far_arrival(z).wait_recv()

        def gather_up(rows, part):
            total = self.core_land[p.z, rows].astype(HIGH)
            for z in self.far:
                total = total + self.far_land[self.far_slot(z, p.z), part].astype(HIGH)
            self.piece[part] = total.astype(LOW)

        in_bands(self.kept_start(p.z), self.quarter, gather_up)
        for at in range(len(self.wide_flips)):
            copy = self.wide_copy(at)

            def set_out(rows, part, at=at):
                self.wide_out[at, part] = self.piece[part]

            def take_in(rows, part, at=at):
                self.piece[part] = self.wide_out[at, part] + self.wide_land[at, part]

            in_bands(0, self.quarter, set_out)
            copy.start()
            copy.wait_recv()
            in_bands(0, self.quarter, take_in)

    def finish(self):
        p = self.place
        for z in [p.z] + p.others:
            self.core_copy(z).wait_send()
        for z in [p.z] + self.far:
            self.first_copy(z).wait_send()
            self.second_copy(z).wait_send()
        for z in self.far:
            self.far_copy(z).wait_send()
        if self.near_land is not None:
            self.near_copy().wait_send()
        for at in range(len(self.wide_flips)):
            self.wide_copy(at).wait_send()


class Return(Spread):
    def __init__(self, place, whole, pieces, send, recv, keep_sem, group, block):
        super().__init__(place, whole, send, recv, group, block)
        self.mine = pieces.at[self.matrix, pl.ds(self.base // 4, self.quarter)]
        p = place
        self.keep = pltpu.make_async_copy(self.mine, self.piece(0, p.a, p.b, p.core), keep_sem.at[group])

    def hand_out(self, z):
        super().hand_out(z)
        self.keep.start()

    def sent(self, z):
        super().sent(z)
        self.keep.wait()

    def odd(self, z):
        return lax.rem(self.place.z + self.group, 2)


class Fold:
    def __init__(self, place, flips, stages, lands, far, send, recv):
        self.place, self.flips, self.bits = place, flips, len(flips)
        self.stages, self.lands, self.far, self.send, self.recv = stages, lands, far, send, recv

    def copy(self, bit):
        sems = self.send.at[bit], self.recv.at[bit]
        return remote(self.stages.at[bit], self.lands.at[bit], *sems, (self.flips[bit], self.place.z))

    def start(self):
        self.copy(0).start()

    def fold(self, bit):
        self.copy(bit).wait_recv()
        self.stages[bit + 1] = self.stages[bit] + self.lands[bit]
        if bit + 1 < self.bits:
            self.copy(bit + 1).start()
        else:
            for z in self.place.others:
                self.far_copy(z).start()
            self.far[self.place.z] = self.tile(self.place.z)[...]

    def tile(self, z):
        return self.stages.at[self.bits, z if self.stages.shape[1] > 1 else 0]

    def far_copy(self, z):
        p = self.place
        sems = self.send.at[self.bits + z], self.recv.at[self.bits + p.z]
        return remote(self.tile(z), self.far.at[p.z], *sems, (p.dp, z))

    def total(self):
        p = self.place
        for z in p.others:
            sems = self.send.at[self.bits + z], self.recv.at[self.bits + z]
            remote(self.tile(z), self.far.at[z], *sems, (p.dp, z)).wait_recv()
        total = self.far[0]
        for z in range(1, self.far.shape[0]):
            total = total + self.far[z]
        return total

    def finish(self):
        for bit in range(self.bits):
            self.copy(bit).wait_send()
        for z in self.place.others:
            self.far_copy(z).wait_send()


BACKWARD_PLAN = (
    {
        11: (30,),
        20: (20, 32,),
        21: (22,),
        30: (31,),
        31: (21,),
        50: (33,),
        106: (130,),
        103: (122,),
        107: (23, 132,),
        116: (131,),
        110: (0,),
        111: (10,),
        112: (121,),
        115: (133, 222,),
        126: (230,),
        121: (2, 12,),
        122: (123, 232,),
        125: (100, 231,),
        136: (110, 221,),
        131: (1, 11,),
        132: (102, 233,),
        134: (333, 223, 112, 323,),
        137: (210, 200,),
        200: (111, 101, 3, 202, 701, 13,),
        201: (212, 433, 423, 201, 211, 702,),
        202: (113, 103, 523, 533, 203, 213,),
        203: (303, 313, 623, 703, 633, 403, 413,),
        204: (503, 513, 603, 613,),
    },
    {
        11: (30,),
        20: (20, 32,),
        21: (22,),
        30: (31,),
        31: (21,),
        50: (33,),
        106: (130,),
        101: (132,),
        107: (23, 122, 121,),
        110: (0,),
        111: (10,),
        112: (131,),
        114: (133,),
        115: (232,),
        117: (230,),
        121: (2, 12, 222,),
        122: (123,),
        123: (100,),
        125: (221,),
        127: (231,),
        136: (110,),
        130: (112,),
        131: (1, 11, 233,),
        133: (223,),
        135: (102, 210,),
        137: (101, 200, 212,),
        200: (202, 333, 3, 13, 701, 111,),
        201: (201, 323, 433, 113, 103, 702,),
        202: (211, 423, 203, 303, 533, 213,),
        203: (633, 523, 313, 703, 403, 623, 413,),
        204: (503, 513, 603, 613,),
    },
)


def layer_kernel(
    n_tensor,
    heads,
    scale,
    layer_input,
    segment_ids,
    local_qkv,
    w_out,
    w_up,
    w_down,
    in_cotangent,
    local_small,
    out_bias,
    norm1_gain,
    norm1_bias,
    down_bias,
    norm2_gain,
    norm2_bias,
    out_layer,
    out_partial,
    out_landed,
    out_summed,
    out_sums,
    small,
    weights,
    core_land,
    first_land,
    second_land,
    far_land,
    near_land,
    pieces,
    activation,
    slope,
    row_input,
    bias,
    q_and_mixed,
    k_and_v,
    totals,
    head_totals,
    queries,
    keys,
    values,
    grad_mixed,
    grad_k,
    grad_v,
    inverse,
    live_rows,
    terms,
    hidden_low,
    grad_low,
    spare,
    sums,
    sums_land,
    sums_far,
    late_sums,
    late_land,
    late_far,
    wide_out,
    wide_land,
    gather_send,
    gather_recv,
    small_send,
    small_recv,
    copy_sem,
    send,
    recv,
    final_send,
    final_recv,
    wide_send,
    wide_recv,
    term_send,
    term_recv,
    sums_send,
    sums_recv,
    late_send,
    late_recv,
    save_sem,
    keep_sem,
):
    place = Place(n_tensor)
    share = hidden_low.shape[0]
    length, width = row_input.shape
    shares_per_row = length // share
    group_rows = k_and_v.shape[2] // 2
    size = group_rows // heads
    my_share = lax.rem(place.z, shares_per_row)
    in_row = pl.ds(pl.multiple_of(my_share * share, share), share)
    row_start = pl.multiple_of(place.z // shares_per_row * length, length)
    near, middle, far = place.others
    bits = sums_land.shape[0]
    flips = [place.dp + (1 << bit) - (2 << bit) * lax.rem(place.dp // (1 << bit), 2) for bit in range(bits)]

    accum, xhat = terms.at[0], terms.at[1]

    mine = weights.at[0, place.z]
    pairs = [
        (local_qkv, mine.at[pl.ds(0, 3 * group_rows)]),
        (w_out, mine.at[pl.ds(3 * group_rows, group_rows)]),
        (w_up, weights.at[1, place.z]),
        (w_down, weights.at[2, place.z]),
    ]
    own = [
        pltpu.make_async_copy(source, target, copy_sem.at[at]) for at, (source, target) in enumerate(pairs)
    ]
    load_input = pltpu.make_async_copy(
        layer_input.at[pl.ds(row_start, length)], row_input, copy_sem.at[4]
    )
    for copy in own:
        copy.start()
    load_input.start()
    load_cotangent = pltpu.make_async_copy(in_cotangent, spare.at[0], copy_sem.at[5])
    load_cotangent.start()
    partners = [(flip, place.z) for flip in flips] + [(place.dp, z) for z in place.others]
    greet(partners)
    meet(partners)
    gathers = [Gather(place, weights, gather_send, gather_recv, group, (group, 0, width)) for group in range(3)]
    gather_a, gather_b, gather_c = gathers

    def small_copy(z):
        sems = small_send.at[z], small_recv.at[place.z]
        return remote(local_small, small.at[place.z], *sems, (place.dp, z))

    def small_arrival(z):
        return remote(local_small, small.at[z], small_send.at[z], small_recv.at[z], (place.dp, z))

    own[0].wait()
    own[1].wait()
    gather_a.start()
    for z in place.others:
        small_copy(z).start()
    small[place.z] = local_small[...]
    own_start = pl.multiple_of(place.z * share, share)
    own_segments, row_segments = segment_rows(segment_ids, own_start, share, row_start, length)
    bias[...] = segment_bias(own_segments, row_segments)
    live_rows[...] = (own_segments >= 0).astype(HIGH)
    load_input.wait()

    at_end = (place.z == 0) | (place.z == n_tensor - 1)

    def pass_pieces(slot, there=True):
        for inside, plan in enumerate(FORWARD_PLAN):
            steps = plan.get(slot, ())
            if not steps:
                continue

            def run(steps=steps):
                for step in steps:
                    part = gathers[step // 10 % 10]
                    stage = (part.first, part.second, part.third, part.last)[step // 100]
                    stage(place.others[step % 10])

            pl.when(jnp.logical_and(at_end != bool(inside), there))(run)

    def start_b():
        own[2].wait()
        gather_b.start()

    def start_c():
        own[3].wait()
        gather_c.start()

    def attend_forward(turn, z):
        q_rows, k_rows, v_rows = (
            jnp.concatenate([weights[0, z, pl.ds((3 * head + kind) * size, size)] for head in range(heads)], axis=0)
            for kind in range(3)
        )
        q_bias, v_bias = small[z, 0:1, :group_rows], small[z, 1:2, :group_rows]
        x_row = row_input[...]
        q = (dot_nt(row_input[in_row], q_rows) + q_bias).astype(LOW) * scale
        k = dot_nt(x_row, k_rows).astype(LOW)
        v = (dot_nt(x_row, v_rows) + v_bias).astype(LOW)
        k_and_v[z] = jnp.concatenate([k, v], axis=1)
        for head in range(heads):
            part = slice(head * size, (head + 1) * size)
            queries[head], keys[head], values[head] = q[:, part], k[:, part], v[:, part]

        def one_head(head, carry):
            chunk = share // 2
            for part in range(2):
                rows = pl.ds(part * chunk, chunk)
                scores = dot_nt(queries[head, rows], keys[head]) + bias[rows]
                top = jnp.max(scores, axis=-1, keepdims=True)
                raised = jnp.exp(scores - top)
                total = jnp.sum(raised, axis=-1, keepdims=True)
                summed = dot_nn(raised.astype(LOW), values[head])
                grad_mixed[head, rows] = (summed / total).astype(LOW)
                head_totals[head, rows] = top + jnp.log(total)
                for index in range(heads):
                    pass_pieces(10 * turn + 2 * index + part, head == index)
                    if (turn, index, part) == (1, 0, 1):
                        pl.when(head == index)(start_c)
            return carry

        lax.fori_loop(0, heads, one_head, 0)
        columns = [queries[head] for head in range(heads)] + [grad_mixed[head] for head in range(heads)]
        q_and_mixed[z] = jnp.concatenate(columns, axis=-1)
        totals[z] = jnp.concatenate([head_totals[head] for head in range(heads)], axis=-1)

    attend_forward(0, place.z)
    start_b()
    pass_pieces(19)
    for z in place.others:
        small_arrival(z).wait_recv()
    attend_forward(1, near)
    pass_pieces(29)
    attend_forward(2, middle)
    pass_pieces(39)
    attend_forward(3, far)

    band = min(128, share)
    own_first = my_share * share
    out_shift, gain_first, shift_first = as_row(out_bias), as_row(norm1_gain), as_row(norm1_bias)
    down_shift = as_row(down_bias)

    def project_out(at, carry):
        rows = pl.ds(pl.multiple_of(at * band, band), band)
        own_rows = pl.ds(pl.multiple_of(own_first + at * band, band), band)
        first_sum = row_input[own_rows].astype(HIGH) + out_shift
        for z in range(n_tensor):
            first_sum = first_sum + dot_nn(q_and_mixed[z, rows, group_rows:], weights[0, z, 3 * group_rows :])
        normed, spread = norm_forward(first_sum)
        xhat[rows] = normed
        inverse[rows] = spread
        hidden = normed * gain_first + shift_first
        hidden_low[rows] = hidden.astype(LOW)
        accum[rows] = hidden + down_shift
        return carry

    lax.fori_loop(0, share // band, project_out, 0)

    def feed_forward(at, carry):
        z = place.pick(at, [place.z] + place.others)

        for index in range(n_tensor):
            pass_pieces(40 + index, at == index)
        pl.when(at == 1)(gather_a.finish)
        pl.when(at == 2)(gather_b.finish)
        raw = dot_nn(hidden_low[...], weights[1, z]) + small[z, 2:3]
        value, rise = gelu_parts(raw)
        activation[z] = value.astype(LOW)
        slope[z] = rise.astype(LOW)
        accum[...] += dot_nn(activation[z], weights[2, z])
        return carry

    lax.fori_loop(0, n_tensor, feed_forward, 0)
    gather_c.finish()

    order = [near, far, middle, place.z]
    lands = (core_land, first_land, second_land, far_land)
    wide = (flips[3:], wide_out, wide_land, wide_send, wide_recv)
    blocks = [(0, 0, width // 2), (0, width // 2, width // 2), (1, 0, width), (2, 0, width)]
    reduces = [
        Reduce(place, weights, lands, pieces, send, recv, wide, group, block, near_land if group == 2 else None)
        for group, block in enumerate(blocks)
    ]
    for half in range(2):
        side = pl.ds(half * width // 2, width // 2)
        reduces[half].core_land = activation.at[:, pl.ds(0, width // 2), side]
    returns = [
        Return(place, out_summed, pieces, final_send, final_recv, keep_sem, group, block)
        for group, block in enumerate(blocks)
    ]
    first_half, second_half, reduce_b, reduce_c = reduces
    fold = Fold(place, flips, sums, sums_land, sums_far, sums_send, sums_recv)
    late_fold = Fold(place, flips, late_sums, late_land, late_far, late_send, late_recv)
    sums[0] = jnp.zeros(sums.shape[1:], HIGH)
    late_sums[0] = jnp.zeros(late_sums.shape[1:], HIGH)

    shards = (near, middle, far, place.z)

    def finish_sum(reduce, spread):
        reduce.fourth()
        spread.hand_out(0)

    def take(step):
        stage, block, shard = step // 100, step // 10 % 10, step % 10
        if stage == 7:
            return next_term(shard)
        reduce, spread = reduces[block], returns[block]
        if stage < 3:
            return (reduce.first, reduce.second, reduce.third)[stage](shards[shard])
        if stage == 3:
            return finish_sum(reduce, spread)
        return (spread.second, spread.third, spread.last)[stage - 4](0)

    def serve(slot, there=True):
        for inside, plan in enumerate(BACKWARD_PLAN):
            steps = plan.get(slot, ())
            if not steps:
                continue

            def run(steps=steps):
                for step in steps:
                    take(step)

            pl.when(jnp.logical_and(at_end != bool(inside), there))(run)

    def serve_loop(at, slot):
        for index in range(n_tensor):
            serve(10 * index + slot, at == index)

    gain_second, shift_second = as_row(norm2_gain), as_row(norm2_bias)

    load_cotangent.wait()
    def second_norm(at, carry):
        rows = pl.ds(pl.multiple_of(at * band, band), band)
        normed, spread = norm_forward(accum[rows])
        cotangent = spare[0, rows].astype(HIGH) * live_rows[rows]
        spare[0, rows] = (normed * gain_second + shift_second).astype(LOW)
        grad_second = norm_backward(normed, spread, cotangent * gain_second)
        sums[0, 0, 6:7] += column_sum(cotangent * normed)
        sums[0, 0, 7:8] += column_sum(cotangent)
        sums[0, 0, 5:6] += column_sum(grad_second)
        grad_low[rows] = grad_second.astype(LOW)
        accum[rows] = grad_second
        return carry

    lax.fori_loop(0, share // band, second_norm, 0)
    save_layer = pltpu.make_async_copy(spare.at[0], out_layer, save_sem.at[0])
    save_layer.start()

    def feed_backward(at, carry):
        z = place.pick(at, order)
        low = grad_low[...]
        grad_up = (dot_nt(low, weights[2, z]) * slope[z].astype(HIGH)).astype(LOW)
        weights[2, z] = dot_tn(activation[z], low).astype(LOW)
        reduce_c.start(z)
        serve_loop(at, 0)
        accum[...] += dot_nt(grad_up, weights[1, z])
        weights[1, z] = dot_tn(hidden_low[...], grad_up).astype(LOW)
        reduce_b.start(z)
        sums[0, z, 1:2] = column_sum(grad_up.astype(HIGH))
        serve_loop(at, 1)
        return carry

    lax.fori_loop(0, n_tensor, feed_backward, 0)

    def first_norm(at, carry):
        rows = pl.ds(pl.multiple_of(at * band, band), band)
        grad_hidden, normed = accum[rows], xhat[rows]
        grad_first = norm_backward(normed, inverse[rows], grad_hidden * gain_first)
        sums[0, 0, 2:3] += column_sum(grad_first)
        sums[0, 0, 3:4] += column_sum(grad_hidden * normed)
        sums[0, 0, 4:5] += column_sum(grad_hidden)
        accum[rows] = grad_first
        grad_low[rows] = grad_first.astype(LOW)
        return carry

    lax.fori_loop(0, share // band, first_norm, 0)
    for step in range(1, shares_per_row):
        terms[step] = jnp.zeros(accum.shape, HIGH)
    for z in range(1, n_tensor):
        sums[0, z, 2:8] = sums[0, 0, 2:8]
    fold.start()
    serve(50)

    parts = 4
    part_rows = share // parts

    def term_copy(step, part):
        rows = pl.ds(part * part_rows, part_rows)
        partner = place.z - my_share + lax.rem(my_share + step, shares_per_row)
        sems = term_send.at[step - 1, part], term_recv.at[step - 1, part]
        return remote(spare.at[step - 1, rows], out_landed.at[step - 1, rows], *sems, (place.dp, partner))

    def fold_some(turn):
        for bit in range(bits):
            if min(bit, 2) == turn:
                fold.fold(bit)

    def send_terms():
        save_layer.wait()
        for step in range(1, shares_per_row):
            spare[step - 1] = terms[step].astype(LOW)
            term_copy(step, 0).start()

    def next_term(part):
        for step in range(1, shares_per_row):
            term_copy(step, part).start()

    def attend_backward(at, carry):
        z = place.pick(at, order)
        incoming = dot_nt(grad_low[...], weights[0, z, 3 * group_rows :]).astype(LOW)
        weights[0, z, 3 * group_rows :] = dot_tn(q_and_mixed[z, :, group_rows:], grad_low[...]).astype(LOW)
        for head in range(heads):
            part = slice(head * size, (head + 1) * size)
            queries[head], grad_mixed[head] = q_and_mixed[z, :, part], incoming[:, part]
            keys[head], values[head] = k_and_v[z, :, part], k_and_v[z, :, group_rows:][:, part]
            head_totals[head] = totals[z, :, head : head + 1]
        serve_loop(at, 106)

        def one_head(head, inner):
            k, v = keys[head], values[head]
            grad_kt = jnp.zeros((size, length), HIGH)
            grad_vt = jnp.zeros((size, length), HIGH)
            chunk = share // 2
            for part in range(2):
                rows = pl.ds(part * chunk, chunk)
                q, up = queries[head, rows], grad_mixed[head, rows]
                chance = jnp.exp(dot_nt(q, k) + bias[rows] - head_totals[head, rows])
                change = chance * dot_nt(up, v)
                change = change - chance * jnp.sum(change, axis=-1, keepdims=True)
                change = change.astype(LOW)
                grad_kt = grad_kt + dot_nn(q.T, change)
                grad_vt = grad_vt + dot_nn(up.T, chance.astype(LOW))
                grad_mixed[head, rows] = (dot_nn(change, k) * scale).astype(LOW)
                for index in range(heads):
                    for turn in range(n_tensor):
                        serve(100 + 10 * turn + 2 * index + part, (head == index) & (at == turn))
            grad_k[head] = grad_kt.astype(LOW)
            grad_v[head] = grad_vt.astype(LOW)
            for turn, bit in ((0, 0), (1, 1), (2, 2)):
                pl.when((head == heads - 1) & (at == turn))(functools.partial(fold_some, bit))
            return inner

        lax.fori_loop(0, heads, one_head, 0)
        dq = jnp.concatenate([grad_mixed[head] for head in range(heads)], axis=-1)
        dk = grad_k[...].reshape(group_rows, length)
        dv = grad_v[...].reshape(group_rows, length)
        x_row = row_input[...]
        q_rows, k_rows, v_rows = (
            jnp.concatenate([weights[0, z, pl.ds((3 * head + kind) * size, size)] for head in range(heads)], axis=0)
            for kind in range(3)
        )

        def share_term(step):
            first_token = lax.rem(my_share + step, shares_per_row) * share
            tokens = pl.ds(pl.multiple_of(first_token, share), share)
            grad_keys = grad_k[:, :, tokens].reshape(group_rows, share)
            grad_values = grad_v[:, :, tokens].reshape(group_rows, share)
            return dot_tn(grad_keys, k_rows) + dot_tn(grad_values, v_rows)

        for step in range(1, shares_per_row):
            terms[step] += share_term(step)
        pl.when(at == n_tensor - 1)(send_terms)
        accum[...] += share_term(0) + dot_nn(dq, q_rows)
        for kind, (left, right) in enumerate(((dq.T, row_input[in_row]), (dk, x_row), (dv, x_row))):
            grad = dot_nn(left, right).astype(LOW)
            for head in range(heads):
                weights[0, z, pl.ds((3 * head + kind) * size, size)] = grad[head * size : (head + 1) * size]
        first_half.start(z)
        second_half.start(z)
        ones = jnp.ones((8, length), LOW)
        q_sums, v_sums = dot_nn(ones[:, :share], dq)[0:1], dot_nt(ones, dv)[0:1]
        for head in range(heads):
            part = slice(head * size, (head + 1) * size)
            pair = jnp.concatenate([q_sums[:, part], v_sums[:, part]], axis=1)
            at_row = lax.broadcasted_iota(jnp.int32, (8, 2 * size), 0) == z
            late_sums[0, 0, :, 2 * head * size : 2 * (head + 1) * size] += jnp.where(at_row, pair, 0.0)
        serve_loop(at, 107)
        return carry

    lax.fori_loop(0, n_tensor, attend_backward, 0)

    def keep_row(values, z):
        out_sums[0:1] = values[z : z + 1]

    late_fold.start()
    save_partial = pltpu.make_async_copy(accum, out_partial, save_sem.at[1])
    save_partial.start()
    for bit in range(bits):
        if bit < 3:
            serve(200 + bit)
        late_fold.fold(bit)
    serve(203)
    for step in range(1, shares_per_row):
        for part in range(parts):
            term_copy(step, part).wait_send()
            term_copy(step, part).wait_recv()
    out_sums[...] = fold.total()
    late_total = late_fold.total()
    for z in range(n_tensor):
        pl.when(place.z == z)(functools.partial(keep_row, late_total, z))
    fold.finish()
    late_fold.finish()
    for reduce in reduces:
        reduce.finish()
    serve(204)
    for part in returns:
        part.sent(0)
    for z in place.others:
        small_copy(z).wait_send()
    save_partial.wait()


def finish_kernel(
    heads,
    in_layer,
    in_partial,
    in_landed,
    in_summed,
    sums,
    out_layer,
    out_input,
    out_qkv,
    qv_bias,
    out_out,
    out_bias,
    gain_first,
    shift_first,
    out_up,
    up_bias,
    out_down,
    down_bias,
    gain_second,
    shift_second,
    layer,
    partial,
    landed,
    summed,
    qkv,
    rest,
    matrices,
    load_sem,
    save_sem,
):
    size = qkv.shape[1]
    pairs = [(in_summed.at[2, 0], summed.at[2]), (in_summed.at[1, 0], summed.at[1]), (in_partial, partial)]
    pairs += [(in_landed, landed), (in_summed.at[0, 0], summed.at[0]), (in_layer, layer)]
    loads = [
        pltpu.make_async_copy(source, target, load_sem.at[at]) for at, (source, target) in enumerate(pairs)
    ]
    for copy in loads:
        copy.start()
    for at, vector in enumerate(
        [up_bias, out_bias, gain_first, shift_first, down_bias, gain_second, shift_second]
    ):
        vector[...] = sums[1 + at : 2 + at].reshape(vector.shape)
    for head in range(heads):
        width = qv_bias.shape[1]
        qv_bias[head : head + 1] = sums[0:1, head * width : (head + 1) * width]
    saves = []

    def save(source, target):
        copy = pltpu.make_async_copy(source, target, save_sem.at[len(saves)])
        copy.start()
        saves.append(copy)

    for at, target in ((2, out_down), (1, out_up)):
        loads[2 - at].wait()
        matrices[at - 1] = summed[at].astype(HIGH)
        save(matrices.at[at - 1], target)
    loads[2].wait()
    loads[3].wait()
    for step in range(landed.shape[0]):
        partial[...] += landed[step].astype(HIGH)
    save(partial, out_input)
    loads[4].wait()
    rest[...] = summed[0, heads * size :].astype(HIGH)
    save(rest, out_out)
    for head in range(heads):
        qkv[head] = summed[0, head * size : (head + 1) * size].astype(HIGH)
    save(qkv, out_qkv)
    loads[5].wait()
    save(layer, out_layer)
    for copy in saves:
        copy.wait()


def on_device(
    layer_input,
    segment_ids,
    w_qkv,
    qv_bias,
    w_out,
    out_bias,
    norm1_gain,
    norm1_bias,
    w_up,
    up_bias,
    w_down,
    down_bias,
    norm2_gain,
    norm2_bias,
    out_cotangent,
):
    n_tensor = lax.axis_size("tensor")
    place = lax.axis_index("tensor")
    n_dp = lax.axis_size("dp")
    bits = n_dp.bit_length() - 1
    tokens, width = layer_input.shape
    share = tokens // n_tensor
    heads = qv_bias.shape[0]
    head_dim = qv_bias.shape[1] // 2
    score_scale = float(head_dim) ** (-0.5)
    shares_per_row = SEQ // share
    group_rows = heads * head_dim

    local_qkv = w_qkv.transpose(1, 2, 0).reshape(3 * group_rows, width)
    local_small = jnp.concatenate(
        [
            jnp.pad(qv_bias[:, :head_dim].reshape(1, -1), ((0, 0), (0, width - group_rows))),
            jnp.pad(qv_bias[:, head_dim:].reshape(1, -1), ((0, 0), (0, width - group_rows))),
            up_bias.reshape(1, -1),
            jnp.zeros((5, width), LOW),
        ]
    ).astype(HIGH)

    vmem = pl.BlockSpec(memory_space=pltpu.VMEM)
    anywhere = pl.BlockSpec(memory_space=pl.ANY)

    def low(*shape):
        return jax.ShapeDtypeStruct(shape, LOW)

    def high(*shape):
        return jax.ShapeDtypeStruct(shape, HIGH)

    def low_scratch(*shape):
        return pltpu.VMEM(shape, LOW)

    def high_scratch(*shape):
        return pltpu.VMEM(shape, HIGH)

    dma = pltpu.SemaphoreType.DMA
    side, quarter = width // 2, width // 4
    wide = bits - 3
    wide_shape = (3, wide, quarter, side) if wide else (3, 1, 64, 128)
    layer_output, partial, landed, summed, sums = pl.pallas_call(
        functools.partial(layer_kernel, n_tensor, heads, score_scale),
        out_shape=(
            low(share, width),
            high(share, width),
            low(shares_per_row - 1, share, width),
            low(3, 1, width, width),
            high(8, width),
        ),
        in_specs=[anywhere, vmem] + [anywhere] * 5 + [vmem] * 7,
        out_specs=(anywhere,) * 4 + (vmem,),
        scratch_shapes=[
            high_scratch(n_tensor, 8, width),
            low_scratch(3, n_tensor, width, width),
            low_scratch(2, n_tensor, width, side),
            low_scratch(3, n_tensor, 2 * quarter, side),
            low_scratch(3, n_tensor, quarter, side),
            low_scratch(3, n_tensor - 1, quarter, side),
            low_scratch(width, side),
            low_scratch(3, quarter, side),
            low_scratch(n_tensor, share, width),
            low_scratch(n_tensor, share, width),
            low_scratch(SEQ, width),
            high_scratch(share, SEQ),
            low_scratch(n_tensor, share, 2 * group_rows),
            low_scratch(n_tensor, SEQ, 2 * group_rows),
            high_scratch(n_tensor, share, heads),
            high_scratch(heads, share, 1),
            low_scratch(heads, share, head_dim),
            low_scratch(heads, SEQ, head_dim),
            low_scratch(heads, SEQ, head_dim),
            low_scratch(heads, share, head_dim),
            low_scratch(heads, head_dim, SEQ),
            low_scratch(heads, head_dim, SEQ),
            high_scratch(share, 1),
            high_scratch(share, 1),
            high_scratch(shares_per_row, share, width),
            low_scratch(share, width),
            low_scratch(share, width),
            low_scratch(shares_per_row - 1, share, width),
            high_scratch(bits + 1, n_tensor, 8, width),
            high_scratch(bits, n_tensor, 8, width),
            high_scratch(n_tensor, 8, width),
            high_scratch(bits + 1, 1, 8, width),
            high_scratch(bits, 1, 8, width),
            high_scratch(n_tensor, 8, width),
            low_scratch(*wide_shape),
            low_scratch(*wide_shape),
            dma((3, n_tensor, 9)),
            dma((3, n_tensor, 8)),
            dma((n_tensor,)),
            dma((n_tensor,)),
            dma((6,)),
            dma((4, n_tensor, 4)),
            dma((4, n_tensor, 4)),
            dma((4, 1, 9)),
            dma((4, 1, 8)),
            dma((4, max(wide, 1))),
            dma((4, max(wide, 1))),
            dma((shares_per_row - 1, 4)),
            dma((shares_per_row - 1, 4)),
            dma((bits + n_tensor,)),
            dma((bits + n_tensor,)),
            dma((bits + n_tensor,)),
            dma((bits + n_tensor,)),
            dma((3,)),
            dma((4,)),
        ],
        compiler_params=pltpu.CompilerParams(
            collective_id=0, has_side_effects=True, vmem_limit_bytes=VMEM_LIMIT
        ),
        name="layer",
    )(
        layer_input,
        segment_ids,
        local_qkv,
        w_out,
        w_up,
        w_down,
        out_cotangent,
        local_small,
        out_bias,
        norm1_gain,
        norm1_bias,
        down_bias,
        norm2_gain,
        norm2_bias,
    )

    vector = high(width)
    matrix = high(width, width)
    layer_output, input_grad, grad_qkv, *rest = pl.pallas_call(
        functools.partial(finish_kernel, heads),
        out_shape=(
            low(share, width),
            high(share, width),
            high(heads, 3 * head_dim, width),
            high(heads, 2 * head_dim),
            high(group_rows, width),
            vector,
            vector,
            vector,
            matrix,
            vector,
            matrix,
            vector,
            vector,
            vector,
        ),
        in_specs=[anywhere] * 4 + [vmem],
        out_specs=(anywhere,) * 3 + (vmem, anywhere, vmem, vmem, vmem, anywhere, vmem, anywhere, vmem, vmem, vmem),
        scratch_shapes=[
            low_scratch(share, width),
            high_scratch(share, width),
            low_scratch(shares_per_row - 1, share, width),
            low_scratch(3, width, width),
            high_scratch(heads, 3 * head_dim, width),
            high_scratch(group_rows, width),
            high_scratch(2, width, width),
            dma((6,)),
            dma((6,)),
        ],
        compiler_params=pltpu.CompilerParams(vmem_limit_bytes=VMEM_LIMIT),
        name="finish",
    )(layer_output, partial, landed, summed, sums)
    return (layer_output, input_grad, grad_qkv.transpose(2, 0, 1), *rest)


def solution(mesh):
    return jax.shard_map(
        on_device,
        mesh=mesh,
        in_specs=(
            P("dp", None),
            P("dp"),
            P(None, "tensor", None),
            P("tensor", None),
            P("tensor", None),
            P(),
            P(),
            P(),
            P(None, "tensor"),
            P("tensor"),
            P("tensor", None),
            P(),
            P(),
            P(),
            P(("dp", "tensor"), None),
        ),
        out_specs=(
            P(("dp", "tensor"), None),
            P(("dp", "tensor"), None),
            P(None, "tensor", None),
            P("tensor", None),
            P("tensor", None),
            P(),
            P(),
            P(),
            P(None, "tensor"),
            P("tensor"),
            P("tensor", None),
            P(),
            P(),
            P(),
        ),
        check_vma=False,
    )
```

```python
import functools

import jax
import jax.numpy as jnp
from jax import lax
from jax.experimental import pallas as pl
from jax.experimental.pallas import tpu as pltpu
from jax.sharding import PartitionSpec as P

SEQ = 1024


EPSILON = 1e-06
MASKED = -1e30
LOW = jnp.bfloat16
HIGH = jnp.float32
MESH = pl.DeviceIdType.MESH
VMEM_LIMIT = 127 * 512 * 1024


def dot_nn(left, right):
    return lax.dot_general(left, right, (((1,), (0,)), ((), ())), preferred_element_type=HIGH)


def dot_nt(left, right):
    return lax.dot_general(left, right, (((1,), (1,)), ((), ())), preferred_element_type=HIGH)


def dot_tn(left, right):
    return lax.dot_general(left, right, (((0,), (0,)), ((), ())), preferred_element_type=HIGH)


def norm_forward(summed):
    mean = jnp.mean(summed, axis=-1, keepdims=True)
    centred = summed - mean
    spread = jnp.mean(centred * centred, axis=-1, keepdims=True)
    inverse = lax.rsqrt(spread + EPSILON)
    return centred * inverse, inverse


def norm_backward(xhat, inverse, scaled):
    return inverse * (
        scaled
        - jnp.mean(scaled, axis=-1, keepdims=True)
        - xhat * jnp.mean(scaled * xhat, axis=-1, keepdims=True)
    )


def gelu_parts(u):
    phi_cdf = 0.5 * (1.0 + lax.erf(u * (2.0**-0.5)))
    density = jnp.exp(-0.5 * u * u) * 0.3989422804014327
    return u * phi_cdf, phi_cdf + u * density


def column_sum(values):
    return jnp.sum(values, axis=0, keepdims=True)


def as_row(vector):
    return vector[...].astype(HIGH).reshape(1, -1)


def as_column(row):
    return jnp.broadcast_to(row, (8, row.shape[1])).T[:, :1]


def segment_rows(segment_ids, own_start, share, row_start, length):
    own = segment_ids[pl.ds(own_start, share)].astype(HIGH).reshape(1, share)
    return as_column(own), segment_ids[pl.ds(row_start, length)].astype(HIGH).reshape(1, length)


def segment_bias(own_segments, row_segments):
    return jnp.where(own_segments == row_segments, 0.0, MASKED)


class Place:
    def __init__(self, n_tensor):
        self.n_tensor = n_tensor
        self.z = lax.axis_index("tensor")
        self.dp = lax.axis_index("dp")
        self.core = lax.rem(self.dp, 2)
        self.a = lax.rem(self.dp // 2, 2)
        self.b = lax.rem(self.dp // 4, 2)
        self.to_core = (self.dp + 1 - 2 * self.core, self.z)
        self.to_a = (self.dp + 2 - 4 * self.a, self.z)
        self.to_b = (self.dp + 4 - 8 * self.b, self.z)
        self.others = [lax.rem(self.z + step, n_tensor) for step in range(1, n_tensor)]
        if n_tensor == 4:
            near = self.z + 1 - 2 * lax.rem(self.z, 2)
            upper = self.z // 2
            self.others = [near, 2 - upper, 3 - 3 * upper]

    def pick(self, at, order):
        chosen = order[0]
        for index in range(1, len(order)):
            chosen = jnp.where(at == index, order[index], chosen)
        return chosen


def greet(partners):
    barrier = pltpu.get_barrier_semaphore()
    for partner in partners:
        pl.semaphore_signal(barrier, inc=1, device_id=partner, device_id_type=MESH)


def meet(partners):
    pl.semaphore_wait(pltpu.get_barrier_semaphore(), len(partners))


def remote(src, dst, send, recv, target):
    return pltpu.make_async_remote_copy(
        src_ref=src,
        dst_ref=dst,
        send_sem=send,
        recv_sem=recv,
        device_id=target,
        device_id_type=MESH,
    )


class Spread:
    def __init__(self, place, whole, send, recv, group, block):
        self.place, self.whole, self.send, self.recv, self.group = place, whole, send, recv, group
        self.matrix, self.base, size = block
        self.mine = None
        self.quarter = size // 4
        self.half = whole.shape[3] // 2

    def odd(self, z):
        return lax.rem(z + self.group, 2)

    def piece(self, z, a, b, side):
        odd = self.odd(z)
        row = odd * (2 * b + a) + (1 - odd) * (2 * a + b)
        rows = pl.ds(pl.multiple_of(self.base + row * self.quarter, 16), self.quarter)
        return self.whole.at[self.matrix, z, rows, pl.ds(pl.multiple_of(side * self.half, 128), self.half)]

    def pass_on(self, z, slot, a, b, side, target):
        part = self.piece(z, a, b, side)
        send = self.send.at[self.group, z, slot]
        recv = self.recv.at[self.group, z, slot % 8]
        source = self.mine if self.mine is not None and slot in (1, 2, 4) else part
        return remote(source, part, send, recv, target)

    def turn(self, z):
        p = self.place
        odd = self.odd(z)
        a = p.a * odd + (1 - p.a) * (1 - odd)
        b = p.b * (1 - odd) + (1 - p.b) * odd
        target = odd * p.to_a[0] + (1 - odd) * p.to_b[0]
        return self.pass_on(z, 3, a, b, p.core, (target, p.z))

    def hand_out(self, z):
        p = self.place
        self.pass_on(z, 1, p.a, p.b, p.core, p.to_a).start()
        self.pass_on(z, 2, p.a, p.b, p.core, p.to_b).start()
        self.pass_on(z, 4, p.a, p.b, p.core, p.to_core).start()

    def second(self, z):
        p = self.place
        self.pass_on(z, 1, 1 - p.a, p.b, p.core, p.to_a).wait_recv()
        self.pass_on(z, 2, p.a, 1 - p.b, p.core, p.to_b).wait_recv()
        self.turn(z).start()
        self.pass_on(z, 5, 1 - p.a, p.b, p.core, p.to_core).start()
        self.pass_on(z, 6, p.a, 1 - p.b, p.core, p.to_core).start()

    def third(self, z):
        p = self.place
        self.pass_on(z, 3, 1 - p.a, 1 - p.b, p.core, p.to_a).wait_recv()
        self.pass_on(z, 7, 1 - p.a, 1 - p.b, p.core, p.to_core).start()

    def last(self, z):
        p = self.place
        side = 1 - p.core
        self.pass_on(z, 4, p.a, p.b, side, p.to_core).wait_recv()
        self.pass_on(z, 5, 1 - p.a, p.b, side, p.to_core).wait_recv()
        self.pass_on(z, 6, p.a, 1 - p.b, side, p.to_core).wait_recv()
        self.pass_on(z, 7, 1 - p.a, 1 - p.b, side, p.to_core).wait_recv()

    def sent(self, z):
        p = self.place
        self.pass_on(z, 1, p.a, p.b, p.core, p.to_a).wait_send()
        self.pass_on(z, 2, p.a, p.b, p.core, p.to_b).wait_send()
        self.turn(z).wait_send()
        self.pass_on(z, 4, p.a, p.b, p.core, p.to_core).wait_send()
        self.pass_on(z, 5, 1 - p.a, p.b, p.core, p.to_core).wait_send()
        self.pass_on(z, 6, p.a, 1 - p.b, p.core, p.to_core).wait_send()
        self.pass_on(z, 7, 1 - p.a, 1 - p.b, p.core, p.to_core).wait_send()


class Gather(Spread):
    def along(self, z):
        p = self.place
        part = self.piece(p.z, p.a, p.b, p.core)
        send, recv = self.send.at[self.group, z, 0], self.recv.at[self.group, p.z, 0]
        return remote(part, part, send, recv, (p.dp, z))

    def onward(self, z):
        p = self.place
        target = jnp.where(z < p.z, p.z + 1, p.z - 1)
        copy = self.pass_on(z, 8, p.a, p.b, p.core, (p.dp, target))
        return (target >= 0) & (target < p.n_tensor), copy

    def start(self):
        p = self.place
        for z in (p.z - 1, p.z + 1):
            pl.when((z >= 0) & (z < p.n_tensor))(self.along(z).start)

    def first(self, z):
        p = self.place
        self.pass_on(z, 0, p.a, p.b, p.core, p.to_core).wait_recv()
        there, copy = self.onward(z)
        pl.when(there)(copy.start)
        self.hand_out(z)

    def finish(self):
        p = self.place
        for z in (p.z - 1, p.z + 1):
            pl.when((z >= 0) & (z < p.n_tensor))(self.along(z).wait_send)
        for z in p.others:
            there, copy = self.onward(z)
            pl.when(there)(copy.wait_send)
            self.sent(z)


FORWARD_PLAN = (
    {
        4: (0,),
        19: (100, 1, 10, 200, 2, 300,),
        10: (101,),
        11: (11,),
        14: (110,),
        29: (12, 102, 201, 301,),
        20: (111,),
        21: (20,),
        23: (210,),
        39: (310, 202, 21, 112, 302,),
        30: (211,),
        31: (22,),
        33: (311,),
        34: (120,),
        40: (121, 212,),
        41: (312, 122,),
        46: (220, 221, 320,),
        47: (222, 321,),
        48: (322,),
    },
    {
        4: (0, 1,),
        19: (2, 100, 10, 11, 101, 12, 102, 200, 300,),
        10: (110,),
        12: (20,),
        13: (111,),
        29: (202, 201, 21, 302, 301,),
        20: (22, 112, 210,),
        23: (120,),
        24: (310,),
        30: (211,),
        33: (311,),
        35: (121,),
        40: (122, 212,),
        41: (220, 312,),
        46: (320,),
        47: (221, 222, 321,),
        48: (322,),
    },
)


def in_bands(start, count, work):
    band = 96

    def one(at, carry):
        offset = pl.multiple_of(at * band, 16)
        work(pl.ds(pl.multiple_of(start + offset, 16), band), pl.ds(offset, band))
        return carry

    lax.fori_loop(0, count // band, one, 0)


class Reduce:
    def __init__(self, place, grads, lands, pieces, send, recv, wide, group, block, near_land=None):
        matrix, base, size = block
        self.near_land = near_land
        self.near = place.others[0]
        self.far = place.others if near_land is None else place.others[1:]
        self.place, self.send, self.recv, self.group = place, send, recv, group
        self.half, self.quarter, self.side = size // 2, size // 4, grads.shape[3] // 2

        def rows(ref, parts):
            return ref.at[matrix, :, pl.ds(base // parts, size // parts)]

        core_land, first_land, second_land, far_land = lands
        self.grads = rows(grads, 1)
        self.core_land = core_land.at[max(matrix - 1, 0)]
        self.first_land, self.second_land, self.far_land = (
            rows(first_land, 2),
            rows(second_land, 4),
            rows(far_land, 4),
        )
        self.piece = pieces.at[matrix, pl.ds(base // 4, size // 4)]
        self.wide_flips, wide_out, wide_land, self.wide_send, self.wide_recv = wide
        if self.wide_flips:
            self.wide_out, self.wide_land = rows(wide_out, 4), rows(wide_land, 4)

    def columns(self, side):
        return pl.ds(pl.multiple_of(side * self.side, 128), self.side)

    def axes(self, z):
        p = self.place
        odd = lax.rem(z + self.group, 2)
        ahead, behind = odd * p.b + (1 - odd) * p.a, odd * p.a + (1 - odd) * p.b
        to_first = odd * p.to_b[0] + (1 - odd) * p.to_a[0]
        to_second = odd * p.to_a[0] + (1 - odd) * p.to_b[0]
        return ahead, behind, (to_first, p.z), (to_second, p.z)

    def rows(self, start, size):
        return pl.ds(pl.multiple_of(start, 16), size)

    def copy(self, z, slot, source, target_ref, target):
        send, recv = self.send.at[self.group, z, slot], self.recv.at[self.group, z, slot]
        return remote(source, target_ref, send, recv, target)

    def core_copy(self, z):
        p = self.place
        source = self.grads.at[z, :, self.columns(1 - p.core)]
        return self.copy(z, 0, source, self.core_land.at[z], p.to_core)

    def first_copy(self, z):
        ahead, _, target, _ = self.axes(z)
        source = self.core_land.at[z, self.rows((1 - ahead) * self.half, self.half)]
        return self.copy(z, 1, source, self.first_land.at[z], target)

    def second_copy(self, z):
        ahead, behind, _, target = self.axes(z)
        start = ahead * self.half + (1 - behind) * self.quarter
        source = self.core_land.at[z, self.rows(start, self.quarter)]
        return self.copy(z, 2, source, self.second_land.at[z], target)

    def kept_start(self, z):
        ahead, behind, _, _ = self.axes(z)
        return ahead * self.half + behind * self.quarter

    def kept(self, z):
        return self.rows(self.kept_start(z), self.quarter)

    def far_slot(self, source, target):
        return lax.rem(source - target + self.place.n_tensor, self.place.n_tensor) - 1

    def far_copy(self, z):
        p, group = self.place, self.group
        source = self.core_land.at[z, self.kept(z)]
        send, recv = self.send.at[group, z, 3], self.recv.at[group, p.z, 3]
        return remote(source, self.far_land.at[self.far_slot(p.z, z)], send, recv, (p.dp, z))

    def far_arrival(self, z):
        p, group = self.place, self.group
        land = self.far_land.at[self.far_slot(z, p.z)]
        return remote(land, land, self.send.at[group, z, 3], self.recv.at[group, z, 3], (p.dp, z))

    def wide_copy(self, at):
        group = self.group
        sems = self.wide_send.at[group, at], self.wide_recv.at[group, at]
        target = (self.wide_flips[at], self.place.z)
        return remote(self.wide_out.at[at], self.wide_land.at[at], *sems, target)

    def start(self, z):
        self.core_copy(z).start()

    def add(self, target, start, count, other):
        def work(rows, part):
            target[rows] = target[rows] + other[part]

        in_bands(start, count, work)

    def near_copy(self):
        p, group = self.place, self.group
        sems = self.send.at[group, self.near, 3], self.recv.at[group, p.z, 3]
        return remote(self.core_land.at[self.near], self.near_land, *sems, (p.dp, self.near))

    def near_arrival(self):
        p, group = self.place, self.group
        sems = self.send.at[group, self.near, 3], self.recv.at[group, self.near, 3]
        return remote(self.near_land, self.near_land, *sems, (p.dp, self.near))

    def first(self, z):
        p = self.place
        self.core_copy(z).wait_recv()
        mine = self.grads.at[z, :, self.columns(p.core)]
        land = self.core_land.at[z]
        self.add(land, 0, 2 * self.half, mine)
        if self.near_land is not None and z is self.near:
            self.near_copy().start()
            return
        if self.near_land is not None and z is p.z:
            self.near_arrival().wait_recv()
            self.add(land, 0, 2 * self.half, self.near_land)
        self.first_copy(z).start()

    def second(self, z):
        ahead, _, _, _ = self.axes(z)
        self.first_copy(z).wait_recv()
        land = self.core_land.at[z]
        self.add(land, ahead * self.half, self.half, self.first_land.at[z])
        self.second_copy(z).start()

    def third(self, z):
        self.second_copy(z).wait_recv()
        land = self.core_land.at[z]
        self.add(land, self.kept_start(z), self.quarter, self.second_land.at[z])
        if z is not self.place.z:
            self.far_copy(z).start()

    def fourth(self):
        p = self.place
        for z in self.far:
            self.far_arrival(z).wait_recv()

        def gather_up(rows, part):
            total = self.core_land[p.z, rows].astype(HIGH)
            for z in self.far:
                total = total + self.far_land[self.far_slot(z, p.z), part].astype(HIGH)
            self.piece[part] = total.astype(LOW)

        in_bands(self.kept_start(p.z), self.quarter, gather_up)
        for at in range(len(self.wide_flips)):
            copy = self.wide_copy(at)

            def set_out(rows, part, at=at):
                self.wide_out[at, part] = self.piece[part]

            def take_in(rows, part, at=at):
                self.piece[part] = self.wide_out[at, part] + self.wide_land[at, part]

            in_bands(0, self.quarter, set_out)
            copy.start()
            copy.wait_recv()
            in_bands(0, self.quarter, take_in)

    def finish(self):
        p = self.place
        for z in [p.z] + p.others:
            self.core_copy(z).wait_send()
        for z in [p.z] + self.far:
            self.first_copy(z).wait_send()
            self.second_copy(z).wait_send()
        for z in self.far:
            self.far_copy(z).wait_send()
        if self.near_land is not None:
            self.near_copy().wait_send()
        for at in range(len(self.wide_flips)):
            self.wide_copy(at).wait_send()


class Return(Spread):
    def __init__(self, place, whole, pieces, send, recv, keep_sem, group, block):
        super().__init__(place, whole, send, recv, group, block)
        self.mine = pieces.at[self.matrix, pl.ds(self.base // 4, self.quarter)]
        p = place
        self.keep = pltpu.make_async_copy(self.mine, self.piece(0, p.a, p.b, p.core), keep_sem.at[group])

    def hand_out(self, z):
        super().hand_out(z)
        self.keep.start()

    def sent(self, z):
        super().sent(z)
        self.keep.wait()

    def odd(self, z):
        return lax.rem(self.place.z + self.group, 2)


class Fold:
    def __init__(self, place, flips, stages, lands, far, send, recv):
        self.place, self.flips, self.bits = place, flips, len(flips)
        self.stages, self.lands, self.far, self.send, self.recv = stages, lands, far, send, recv

    def copy(self, bit):
        sems = self.send.at[bit], self.recv.at[bit]
        return remote(self.stages.at[bit], self.lands.at[bit], *sems, (self.flips[bit], self.place.z))

    def start(self):
        self.copy(0).start()

    def fold(self, bit):
        self.copy(bit).wait_recv()
        self.stages[bit + 1] = self.stages[bit] + self.lands[bit]
        if bit + 1 < self.bits:
            self.copy(bit + 1).start()
        else:
            for z in self.place.others:
                self.far_copy(z).start()
            self.far[self.place.z] = self.tile(self.place.z)[...]

    def tile(self, z):
        return self.stages.at[self.bits, z if self.stages.shape[1] > 1 else 0]

    def far_copy(self, z):
        p = self.place
        sems = self.send.at[self.bits + z], self.recv.at[self.bits + p.z]
        return remote(self.tile(z), self.far.at[p.z], *sems, (p.dp, z))

    def total(self):
        p = self.place
        for z in p.others:
            sems = self.send.at[self.bits + z], self.recv.at[self.bits + z]
            remote(self.tile(z), self.far.at[z], *sems, (p.dp, z)).wait_recv()
        total = self.far[0]
        for z in range(1, self.far.shape[0]):
            total = total + self.far[z]
        return total

    def finish(self):
        for bit in range(self.bits):
            self.copy(bit).wait_send()
        for z in self.place.others:
            self.far_copy(z).wait_send()


BACKWARD_PLAN = (
    {
        11: (32, 22,),
        20: (30,),
        21: (20,),
        30: (31,),
        31: (21,),
        50: (132, 122, 33,),
        104: (130, 131,),
        107: (232, 23,),
        116: (121,),
        110: (2, 12,),
        112: (222,),
        113: (133,),
        117: (231, 230, 221,),
        120: (0,),
        121: (123, 102, 10,),
        124: (112,),
        125: (100,),
        127: (233, 223, 202, 323, 333,),
        136: (212,),
        130: (1, 110, 11,),
        132: (200,),
        135: (423,),
        137: (210, 433,),
        200: (111, 3, 101, 13, 523,),
        201: (701, 533, 201, 623, 211,),
        202: (633, 113, 103, 702, 703,),
        203: (213, 313, 203, 303, 413, 403,),
        204: (513, 503, 613, 603,),
    },
    {
        11: (32, 22,),
        20: (30,),
        21: (20,),
        30: (31,),
        31: (21,),
        50: (132, 122, 33,),
        105: (130, 121,),
        107: (222, 23,),
        110: (131, 2, 12,),
        113: (232, 133,),
        117: (221, 230,),
        126: (231,),
        120: (0,),
        121: (123, 112, 10,),
        124: (102,),
        125: (100,),
        127: (233, 223,),
        136: (212, 202,),
        130: (1,),
        131: (110, 11, 323,),
        132: (200,),
        134: (333,),
        135: (101,),
        137: (210, 111,),
        200: (423, 701, 3, 13, 433,),
        201: (201, 211, 103, 523, 702,),
        202: (703, 623, 533, 113, 203,),
        203: (303, 633, 213, 313, 403, 413,),
        204: (503, 513, 603, 613,),
    },
)


def layer_kernel(
    n_tensor,
    heads,
    scale,
    layer_input,
    segment_ids,
    local_qkv,
    w_out,
    w_up,
    w_down,
    in_cotangent,
    qv_bias,
    up_bias,
    out_bias,
    norm1_gain,
    norm1_bias,
    down_bias,
    norm2_gain,
    norm2_bias,
    out_layer,
    out_partial,
    out_landed,
    out_summed,
    out_sums,
    local_small,
    small,
    weights,
    core_land,
    first_land,
    second_land,
    far_land,
    near_land,
    pieces,
    activation,
    slope,
    row_input,
    bias,
    q_and_mixed,
    k_and_v,
    totals,
    head_totals,
    queries,
    keys,
    values,
    grad_mixed,
    grad_k,
    grad_v,
    inverse,
    live_rows,
    terms,
    hidden_low,
    grad_low,
    spare,
    sums,
    sums_land,
    sums_far,
    late_sums,
    late_land,
    late_far,
    wide_out,
    wide_land,
    gather_send,
    gather_recv,
    small_send,
    small_recv,
    copy_sem,
    send,
    recv,
    final_send,
    final_recv,
    wide_send,
    wide_recv,
    term_send,
    term_recv,
    sums_send,
    sums_recv,
    late_send,
    late_recv,
    save_sem,
    keep_sem,
):
    place = Place(n_tensor)
    share = hidden_low.shape[0]
    length, width = row_input.shape
    shares_per_row = length // share
    group_rows = k_and_v.shape[2] // 2
    size = group_rows // heads
    my_share = lax.rem(place.z, shares_per_row)
    in_row = pl.ds(pl.multiple_of(my_share * share, share), share)
    row_start = pl.multiple_of(place.z // shares_per_row * length, length)
    near, middle, far = place.others
    bits = sums_land.shape[0]
    flips = [place.dp + (1 << bit) - (2 << bit) * lax.rem(place.dp // (1 << bit), 2) for bit in range(bits)]

    accum, xhat = terms.at[0], terms.at[1]

    mine = weights.at[0, place.z]
    pairs = [
        (local_qkv, mine.at[pl.ds(0, 3 * group_rows)]),
        (w_out, mine.at[pl.ds(3 * group_rows, group_rows)]),
        (w_up, weights.at[1, place.z]),
        (w_down, weights.at[2, place.z]),
    ]
    own = [
        pltpu.make_async_copy(source, target, copy_sem.at[at]) for at, (source, target) in enumerate(pairs)
    ]
    load_input = pltpu.make_async_copy(
        layer_input.at[pl.ds(row_start, length)], row_input, copy_sem.at[4]
    )
    for copy in own:
        copy.start()
    load_input.start()
    load_cotangent = pltpu.make_async_copy(in_cotangent, spare.at[0], copy_sem.at[5])
    load_cotangent.start()
    partners = [(flip, place.z) for flip in flips] + [(place.dp, z) for z in place.others]
    greet(partners)
    biases = qv_bias[...].astype(HIGH)
    local_small[...] = jnp.zeros(local_small.shape, HIGH)
    for row in range(2):
        parts = [biases[head : head + 1, row * size : (row + 1) * size] for head in range(heads)]
        local_small[row : row + 1, :group_rows] = jnp.concatenate(parts, axis=1)
    local_small[2:3] = as_row(up_bias)
    meet(partners)
    gathers = [Gather(place, weights, gather_send, gather_recv, group, (group, 0, width)) for group in range(3)]
    gather_a, gather_b, gather_c = gathers

    def small_copy(z):
        sems = small_send.at[z], small_recv.at[place.z]
        return remote(local_small, small.at[place.z], *sems, (place.dp, z))

    def small_arrival(z):
        return remote(local_small, small.at[z], small_send.at[z], small_recv.at[z], (place.dp, z))

    own[0].wait()
    own[1].wait()
    gather_a.start()
    for z in place.others:
        small_copy(z).start()
    small[place.z] = local_small[...]
    own_start = pl.multiple_of(place.z * share, share)
    own_segments, row_segments = segment_rows(segment_ids, own_start, share, row_start, length)
    bias[...] = segment_bias(own_segments, row_segments)
    live_rows[...] = (own_segments >= 0).astype(HIGH)
    load_input.wait()

    at_end = (place.z == 0) | (place.z == n_tensor - 1)

    def pass_pieces(slot, there=True):
        for inside, plan in enumerate(FORWARD_PLAN):
            steps = plan.get(slot, ())
            if not steps:
                continue

            def run(steps=steps):
                for step in steps:
                    part = gathers[step // 10 % 10]
                    stage = (part.first, part.second, part.third, part.last)[step // 100]
                    stage(place.others[step % 10])

            pl.when(jnp.logical_and(at_end != bool(inside), there))(run)

    def start_b():
        own[2].wait()
        gather_b.start()

    def start_c():
        own[3].wait()
        gather_c.start()

    def attend_forward(turn, z):
        q_rows, k_rows, v_rows = (
            jnp.concatenate([weights[0, z, pl.ds((3 * head + kind) * size, size)] for head in range(heads)], axis=0)
            for kind in range(3)
        )
        q_bias, v_bias = small[z, 0:1, :group_rows], small[z, 1:2, :group_rows]
        x_row = row_input[...]
        q = (dot_nt(row_input[in_row], q_rows) + q_bias).astype(LOW) * scale
        k = dot_nt(x_row, k_rows).astype(LOW)
        v = (dot_nt(x_row, v_rows) + v_bias).astype(LOW)
        k_and_v[z] = jnp.concatenate([k, v], axis=1)
        for head in range(heads):
            part = slice(head * size, (head + 1) * size)
            queries[head], keys[head], values[head] = q[:, part], k[:, part], v[:, part]

        def one_head(head, carry):
            chunk = share // 2
            for part in range(2):
                rows = pl.ds(part * chunk, chunk)
                scores = dot_nt(queries[head, rows], keys[head]) + bias[rows]
                top = jnp.max(scores, axis=-1, keepdims=True)
                raised = jnp.exp(scores - top)
                total = jnp.sum(raised, axis=-1, keepdims=True)
                summed = dot_nn(raised.astype(LOW), values[head])
                grad_mixed[head, rows] = (summed / total).astype(LOW)
                head_totals[head, rows] = top + jnp.log(total)
                for index in range(heads):
                    pass_pieces(10 * turn + 2 * index + part, head == index)
                    if (turn, index, part) == (1, 0, 1):
                        pl.when(head == index)(start_c)
            return carry

        lax.fori_loop(0, heads, one_head, 0)
        columns = [queries[head] for head in range(heads)] + [grad_mixed[head] for head in range(heads)]
        q_and_mixed[z] = jnp.concatenate(columns, axis=-1)
        totals[z] = jnp.concatenate([head_totals[head] for head in range(heads)], axis=-1)

    attend_forward(0, place.z)
    start_b()
    pass_pieces(19)
    for z in place.others:
        small_arrival(z).wait_recv()
    attend_forward(1, near)
    pass_pieces(29)
    attend_forward(2, middle)
    pass_pieces(39)
    attend_forward(3, far)

    band = min(128, share)
    own_first = my_share * share
    out_shift, gain_first, shift_first = as_row(out_bias), as_row(norm1_gain), as_row(norm1_bias)
    down_shift = as_row(down_bias)

    def project_out(at, carry):
        rows = pl.ds(pl.multiple_of(at * band, band), band)
        own_rows = pl.ds(pl.multiple_of(own_first + at * band, band), band)
        first_sum = row_input[own_rows].astype(HIGH) + out_shift
        for z in range(n_tensor):
            first_sum = first_sum + dot_nn(q_and_mixed[z, rows, group_rows:], weights[0, z, 3 * group_rows :])
        normed, spread = norm_forward(first_sum)
        xhat[rows] = normed
        inverse[rows] = spread
        hidden = normed * gain_first + shift_first
        hidden_low[rows] = hidden.astype(LOW)
        accum[rows] = hidden + down_shift
        return carry

    lax.fori_loop(0, share // band, project_out, 0)

    def feed_forward(at, carry):
        z = place.pick(at, [place.z] + place.others)

        for index in range(n_tensor):
            pass_pieces(40 + index, at == index)
        pl.when(at == 1)(gather_a.finish)
        pl.when(at == 2)(gather_b.finish)
        raw = dot_nn(hidden_low[...], weights[1, z]) + small[z, 2:3]
        value, rise = gelu_parts(raw)
        activation[z] = value.astype(LOW)
        slope[z] = rise.astype(LOW)
        for index in range(n_tensor):
            pass_pieces(45 + index, at == index)
        accum[...] += dot_nn(activation[z], weights[2, z])
        return carry

    lax.fori_loop(0, n_tensor, feed_forward, 0)
    gather_c.finish()

    order = [far, near, middle, place.z]
    lands = (core_land, first_land, second_land, far_land)
    wide = (flips[3:], wide_out, wide_land, wide_send, wide_recv)
    blocks = [(0, 0, width // 2), (0, width // 2, width // 2), (1, 0, width), (2, 0, width)]
    reduces = [
        Reduce(place, weights, lands, pieces, send, recv, wide, group, block, near_land if group == 2 else None)
        for group, block in enumerate(blocks)
    ]
    for half in range(2):
        side = pl.ds(half * width // 2, width // 2)
        reduces[half].core_land = activation.at[:, pl.ds(0, width // 2), side]
    returns = [
        Return(place, out_summed, pieces, final_send, final_recv, keep_sem, group, block)
        for group, block in enumerate(blocks)
    ]
    first_half, second_half, reduce_b, reduce_c = reduces
    fold = Fold(place, flips, sums, sums_land, sums_far, sums_send, sums_recv)
    late_fold = Fold(place, flips, late_sums, late_land, late_far, late_send, late_recv)
    sums[0] = jnp.zeros(sums.shape[1:], HIGH)
    late_sums[0] = jnp.zeros(late_sums.shape[1:], HIGH)

    shards = (near, middle, far, place.z)

    def finish_sum(reduce, spread):
        reduce.fourth()
        spread.hand_out(0)

    def take(step):
        stage, block, shard = step // 100, step // 10 % 10, step % 10
        if stage == 7:
            return next_term(shard)
        reduce, spread = reduces[block], returns[block]
        if stage < 3:
            return (reduce.first, reduce.second, reduce.third)[stage](shards[shard])
        if stage == 3:
            return finish_sum(reduce, spread)
        return (spread.second, spread.third, spread.last)[stage - 4](0)

    def serve(slot, there=True):
        for inside, plan in enumerate(BACKWARD_PLAN):
            steps = plan.get(slot, ())
            if not steps:
                continue

            def run(steps=steps):
                for step in steps:
                    take(step)

            pl.when(jnp.logical_and(at_end != bool(inside), there))(run)

    def serve_loop(at, slot):
        for index in range(n_tensor):
            serve(10 * index + slot, at == index)

    gain_second, shift_second = as_row(norm2_gain), as_row(norm2_bias)

    load_cotangent.wait()
    def second_norm(at, carry):
        rows = pl.ds(pl.multiple_of(at * band, band), band)
        normed, spread = norm_forward(accum[rows])
        cotangent = spare[0, rows].astype(HIGH) * live_rows[rows]
        spare[0, rows] = (normed * gain_second + shift_second).astype(LOW)
        grad_second = norm_backward(normed, spread, cotangent * gain_second)
        sums[0, 0, 6:7] += column_sum(cotangent * normed)
        sums[0, 0, 7:8] += column_sum(cotangent)
        sums[0, 0, 5:6] += column_sum(grad_second)
        grad_low[rows] = grad_second.astype(LOW)
        accum[rows] = grad_second
        return carry

    lax.fori_loop(0, share // band, second_norm, 0)
    save_layer = pltpu.make_async_copy(spare.at[0], out_layer, save_sem.at[0])
    save_layer.start()

    def feed_backward(at, carry):
        z = place.pick(at, order)
        low = grad_low[...]
        grad_up = (dot_nt(low, weights[2, z]) * slope[z].astype(HIGH)).astype(LOW)
        weights[2, z] = dot_tn(activation[z], low).astype(LOW)
        reduce_c.start(z)
        serve_loop(at, 0)
        accum[...] += dot_nt(grad_up, weights[1, z])
        weights[1, z] = dot_tn(hidden_low[...], grad_up).astype(LOW)
        reduce_b.start(z)
        sums[0, z, 1:2] = column_sum(grad_up.astype(HIGH))
        serve_loop(at, 1)
        return carry

    lax.fori_loop(0, n_tensor, feed_backward, 0)

    def first_norm(at, carry):
        rows = pl.ds(pl.multiple_of(at * band, band), band)
        grad_hidden, normed = accum[rows], xhat[rows]
        grad_first = norm_backward(normed, inverse[rows], grad_hidden * gain_first)
        sums[0, 0, 2:3] += column_sum(grad_first)
        sums[0, 0, 3:4] += column_sum(grad_hidden * normed)
        sums[0, 0, 4:5] += column_sum(grad_hidden)
        accum[rows] = grad_first
        grad_low[rows] = grad_first.astype(LOW)
        return carry

    lax.fori_loop(0, share // band, first_norm, 0)
    for step in range(1, shares_per_row):
        terms[step] = jnp.zeros(accum.shape, HIGH)
    for z in range(1, n_tensor):
        sums[0, z, 2:8] = sums[0, 0, 2:8]
    fold.start()
    serve(50)

    parts = 4
    part_rows = share // parts

    def term_copy(step, part):
        rows = pl.ds(part * part_rows, part_rows)
        partner = place.z - my_share + lax.rem(my_share + step, shares_per_row)
        sems = term_send.at[step - 1, part], term_recv.at[step - 1, part]
        return remote(spare.at[step - 1, rows], out_landed.at[step - 1, rows], *sems, (place.dp, partner))

    def fold_some(turn):
        for bit in range(bits):
            if min(bit, 2) == turn:
                fold.fold(bit)

    def send_terms():
        save_layer.wait()
        for step in range(1, shares_per_row):
            spare[step - 1] = terms[step].astype(LOW)
            term_copy(step, 0).start()

    def next_term(part):
        for step in range(1, shares_per_row):
            term_copy(step, part).start()

    def attend_backward(at, carry):
        z = place.pick(at, order)
        incoming = dot_nt(grad_low[...], weights[0, z, 3 * group_rows :]).astype(LOW)
        weights[0, z, 3 * group_rows :] = dot_tn(q_and_mixed[z, :, group_rows:], grad_low[...]).astype(LOW)
        for head in range(heads):
            part = slice(head * size, (head + 1) * size)
            queries[head], grad_mixed[head] = q_and_mixed[z, :, part], incoming[:, part]
            keys[head], values[head] = k_and_v[z, :, part], k_and_v[z, :, group_rows:][:, part]
            head_totals[head] = totals[z, :, head : head + 1]
        serve_loop(at, 106)

        def one_head(head, inner):
            k, v = keys[head], values[head]
            grad_kt = jnp.zeros((size, length), HIGH)
            grad_vt = jnp.zeros((size, length), HIGH)
            chunk = share // 2
            for part in range(2):
                rows = pl.ds(part * chunk, chunk)
                q, up = queries[head, rows], grad_mixed[head, rows]
                chance = jnp.exp(dot_nt(q, k) + bias[rows] - head_totals[head, rows])
                change = chance * dot_nt(up, v)
                change = change - chance * jnp.sum(change, axis=-1, keepdims=True)
                change = change.astype(LOW)
                grad_kt = grad_kt + dot_nn(q.T, change)
                grad_vt = grad_vt + dot_nn(up.T, chance.astype(LOW))
                grad_mixed[head, rows] = (dot_nn(change, k) * scale).astype(LOW)
                for index in range(heads):
                    for turn in range(n_tensor):
                        serve(100 + 10 * turn + 2 * index + part, (head == index) & (at == turn))
            grad_k[head] = grad_kt.astype(LOW)
            grad_v[head] = grad_vt.astype(LOW)
            for turn, bit in ((0, 0), (1, 1), (2, 2)):
                pl.when((head == heads - 1) & (at == turn))(functools.partial(fold_some, bit))
            return inner

        lax.fori_loop(0, heads, one_head, 0)
        dq = jnp.concatenate([grad_mixed[head] for head in range(heads)], axis=-1)
        dk = grad_k[...].reshape(group_rows, length)
        dv = grad_v[...].reshape(group_rows, length)
        x_row = row_input[...]
        q_rows, k_rows, v_rows = (
            jnp.concatenate([weights[0, z, pl.ds((3 * head + kind) * size, size)] for head in range(heads)], axis=0)
            for kind in range(3)
        )

        def share_term(step):
            first_token = lax.rem(my_share + step, shares_per_row) * share
            tokens = pl.ds(pl.multiple_of(first_token, share), share)
            grad_keys = grad_k[:, :, tokens].reshape(group_rows, share)
            grad_values = grad_v[:, :, tokens].reshape(group_rows, share)
            return dot_tn(grad_keys, k_rows) + dot_tn(grad_values, v_rows)

        for step in range(1, shares_per_row):
            terms[step] += share_term(step)
        pl.when(at == n_tensor - 1)(send_terms)
        accum[...] += share_term(0) + dot_nn(dq, q_rows)
        for kind, (left, right) in enumerate(((dq.T, row_input[in_row]), (dk, x_row), (dv, x_row))):
            grad = dot_nn(left, right).astype(LOW)
            for head in range(heads):
                weights[0, z, pl.ds((3 * head + kind) * size, size)] = grad[head * size : (head + 1) * size]
        first_half.start(z)
        second_half.start(z)
        ones = jnp.ones((8, length), LOW)
        q_sums, v_sums = dot_nn(ones[:, :share], dq)[0:1], dot_nt(ones, dv)[0:1]
        for head in range(heads):
            part = slice(head * size, (head + 1) * size)
            pair = jnp.concatenate([q_sums[:, part], v_sums[:, part]], axis=1)
            at_row = lax.broadcasted_iota(jnp.int32, (8, 2 * size), 0) == z
            late_sums[0, 0, :, 2 * head * size : 2 * (head + 1) * size] += jnp.where(at_row, pair, 0.0)
        serve_loop(at, 107)
        return carry

    lax.fori_loop(0, n_tensor, attend_backward, 0)

    def keep_row(values, z):
        out_sums[0:1] = values[z : z + 1]

    late_fold.start()
    save_partial = pltpu.make_async_copy(accum, out_partial, save_sem.at[1])
    save_partial.start()
    for bit in range(bits):
        if bit < 3:
            serve(200 + bit)
        late_fold.fold(bit)
    serve(203)
    for step in range(1, shares_per_row):
        for part in range(parts):
            term_copy(step, part).wait_send()
            term_copy(step, part).wait_recv()
    out_sums[...] = fold.total()
    late_total = late_fold.total()
    for z in range(n_tensor):
        pl.when(place.z == z)(functools.partial(keep_row, late_total, z))
    fold.finish()
    late_fold.finish()
    for reduce in reduces:
        reduce.finish()
    serve(204)
    for part in returns:
        part.sent(0)
    for z in place.others:
        small_copy(z).wait_send()
    save_partial.wait()


def finish_kernel(
    heads,
    in_layer,
    in_partial,
    in_landed,
    in_summed,
    sums,
    out_layer,
    out_input,
    out_qkv,
    qv_bias,
    out_out,
    out_bias,
    gain_first,
    shift_first,
    out_up,
    up_bias,
    out_down,
    down_bias,
    gain_second,
    shift_second,
    layer,
    partial,
    landed,
    summed,
    qkv,
    rest,
    matrices,
    load_sem,
    save_sem,
):
    size = qkv.shape[1]
    pairs = [(in_summed.at[2, 0], summed.at[2]), (in_summed.at[1, 0], summed.at[1]), (in_partial, partial)]
    pairs += [(in_landed, landed), (in_summed.at[0, 0], summed.at[0]), (in_layer, layer)]
    loads = [
        pltpu.make_async_copy(source, target, load_sem.at[at]) for at, (source, target) in enumerate(pairs)
    ]
    for copy in loads:
        copy.start()
    for at, vector in enumerate(
        [up_bias, out_bias, gain_first, shift_first, down_bias, gain_second, shift_second]
    ):
        vector[...] = sums[1 + at : 2 + at].reshape(vector.shape)
    for head in range(heads):
        width = qv_bias.shape[1]
        qv_bias[head : head + 1] = sums[0:1, head * width : (head + 1) * width]
    saves = []

    def save(source, target):
        copy = pltpu.make_async_copy(source, target, save_sem.at[len(saves)])
        copy.start()
        saves.append(copy)

    for at, target in ((2, out_down), (1, out_up)):
        loads[2 - at].wait()
        matrices[at - 1] = summed[at].astype(HIGH)
        save(matrices.at[at - 1], target)
    loads[2].wait()
    loads[3].wait()
    for step in range(landed.shape[0]):
        partial[...] += landed[step].astype(HIGH)
    save(partial, out_input)
    loads[4].wait()
    rest[...] = summed[0, heads * size :].astype(HIGH)
    save(rest, out_out)
    for head in range(heads):
        qkv[head] = summed[0, head * size : (head + 1) * size].astype(HIGH)
    save(qkv, out_qkv)
    loads[5].wait()
    save(layer, out_layer)
    for copy in saves:
        copy.wait()


def on_device(
    layer_input,
    segment_ids,
    w_qkv,
    qv_bias,
    w_out,
    out_bias,
    norm1_gain,
    norm1_bias,
    w_up,
    up_bias,
    w_down,
    down_bias,
    norm2_gain,
    norm2_bias,
    out_cotangent,
):
    n_tensor = lax.axis_size("tensor")
    place = lax.axis_index("tensor")
    n_dp = lax.axis_size("dp")
    bits = n_dp.bit_length() - 1
    tokens, width = layer_input.shape
    share = tokens // n_tensor
    heads = qv_bias.shape[0]
    head_dim = qv_bias.shape[1] // 2
    score_scale = float(head_dim) ** (-0.5)
    shares_per_row = SEQ // share
    group_rows = heads * head_dim

    local_qkv = w_qkv.transpose(1, 2, 0).reshape(3 * group_rows, width)
    vmem = pl.BlockSpec(memory_space=pltpu.VMEM)
    anywhere = pl.BlockSpec(memory_space=pl.ANY)

    def low(*shape):
        return jax.ShapeDtypeStruct(shape, LOW)

    def high(*shape):
        return jax.ShapeDtypeStruct(shape, HIGH)

    def low_scratch(*shape):
        return pltpu.VMEM(shape, LOW)

    def high_scratch(*shape):
        return pltpu.VMEM(shape, HIGH)

    dma = pltpu.SemaphoreType.DMA
    side, quarter = width // 2, width // 4
    wide = bits - 3
    wide_shape = (3, wide, quarter, side) if wide else (3, 1, 64, 128)
    layer_output, partial, landed, summed, sums = pl.pallas_call(
        functools.partial(layer_kernel, n_tensor, heads, score_scale),
        out_shape=(
            low(share, width),
            high(share, width),
            low(shares_per_row - 1, share, width),
            low(3, 1, width, width),
            high(8, width),
        ),
        in_specs=[anywhere, vmem] + [anywhere] * 5 + [vmem] * 8,
        out_specs=(anywhere,) * 4 + (vmem,),
        scratch_shapes=[
            high_scratch(8, width),
            high_scratch(n_tensor, 8, width),
            low_scratch(3, n_tensor, width, width),
            low_scratch(2, n_tensor, width, side),
            low_scratch(3, n_tensor, 2 * quarter, side),
            low_scratch(3, n_tensor, quarter, side),
            low_scratch(3, n_tensor - 1, quarter, side),
            low_scratch(width, side),
            low_scratch(3, quarter, side),
            low_scratch(n_tensor, share, width),
            low_scratch(n_tensor, share, width),
            low_scratch(SEQ, width),
            high_scratch(share, SEQ),
            low_scratch(n_tensor, share, 2 * group_rows),
            low_scratch(n_tensor, SEQ, 2 * group_rows),
            high_scratch(n_tensor, share, heads),
            high_scratch(heads, share, 1),
            low_scratch(heads, share, head_dim),
            low_scratch(heads, SEQ, head_dim),
            low_scratch(heads, SEQ, head_dim),
            low_scratch(heads, share, head_dim),
            low_scratch(heads, head_dim, SEQ),
            low_scratch(heads, head_dim, SEQ),
            high_scratch(share, 1),
            high_scratch(share, 1),
            high_scratch(shares_per_row, share, width),
            low_scratch(share, width),
            low_scratch(share, width),
            low_scratch(shares_per_row - 1, share, width),
            high_scratch(bits + 1, n_tensor, 8, width),
            high_scratch(bits, n_tensor, 8, width),
            high_scratch(n_tensor, 8, width),
            high_scratch(bits + 1, 1, 8, width),
            high_scratch(bits, 1, 8, width),
            high_scratch(n_tensor, 8, width),
            low_scratch(*wide_shape),
            low_scratch(*wide_shape),
            dma((3, n_tensor, 9)),
            dma((3, n_tensor, 8)),
            dma((n_tensor,)),
            dma((n_tensor,)),
            dma((6,)),
            dma((4, n_tensor, 4)),
            dma((4, n_tensor, 4)),
            dma((4, 1, 9)),
            dma((4, 1, 8)),
            dma((4, max(wide, 1))),
            dma((4, max(wide, 1))),
            dma((shares_per_row - 1, 4)),
            dma((shares_per_row - 1, 4)),
            dma((bits + n_tensor,)),
            dma((bits + n_tensor,)),
            dma((bits + n_tensor,)),
            dma((bits + n_tensor,)),
            dma((3,)),
            dma((4,)),
        ],
        compiler_params=pltpu.CompilerParams(
            collective_id=0, has_side_effects=True, vmem_limit_bytes=VMEM_LIMIT
        ),
        name="layer",
    )(
        layer_input,
        segment_ids,
        local_qkv,
        w_out,
        w_up,
        w_down,
        out_cotangent,
        qv_bias,
        up_bias,
        out_bias,
        norm1_gain,
        norm1_bias,
        down_bias,
        norm2_gain,
        norm2_bias,
    )

    vector = high(width)
    matrix = high(width, width)
    layer_output, input_grad, grad_qkv, *rest = pl.pallas_call(
        functools.partial(finish_kernel, heads),
        out_shape=(
            low(share, width),
            high(share, width),
            high(heads, 3 * head_dim, width),
            high(heads, 2 * head_dim),
            high(group_rows, width),
            vector,
            vector,
            vector,
            matrix,
            vector,
            matrix,
            vector,
            vector,
            vector,
        ),
        in_specs=[anywhere] * 4 + [vmem],
        out_specs=(anywhere,) * 3 + (vmem, anywhere, vmem, vmem, vmem, anywhere, vmem, anywhere, vmem, vmem, vmem),
        scratch_shapes=[
            low_scratch(share, width),
            high_scratch(share, width),
            low_scratch(shares_per_row - 1, share, width),
            low_scratch(3, width, width),
            high_scratch(heads, 3 * head_dim, width),
            high_scratch(group_rows, width),
            high_scratch(2, width, width),
            dma((6,)),
            dma((6,)),
        ],
        compiler_params=pltpu.CompilerParams(vmem_limit_bytes=VMEM_LIMIT),
        name="finish",
    )(layer_output, partial, landed, summed, sums)
    return (layer_output, input_grad, grad_qkv.transpose(2, 0, 1), *rest)


def solution(mesh):
    return jax.shard_map(
        on_device,
        mesh=mesh,
        in_specs=(
            P("dp", None),
            P("dp"),
            P(None, "tensor", None),
            P("tensor", None),
            P("tensor", None),
            P(),
            P(),
            P(),
            P(None, "tensor"),
            P("tensor"),
            P("tensor", None),
            P(),
            P(),
            P(),
            P(("dp", "tensor"), None),
        ),
        out_specs=(
            P(("dp", "tensor"), None),
            P(("dp", "tensor"), None),
            P(None, "tensor", None),
            P("tensor", None),
            P("tensor", None),
            P(),
            P(),
            P(),
            P(None, "tensor"),
            P("tensor"),
            P("tensor", None),
            P(),
            P(),
            P(),
        ),
        check_vma=False,
    )
```

```python
import functools

import jax
import jax.numpy as jnp
from jax import lax
from jax.experimental import pallas as pl
from jax.experimental.pallas import tpu as pltpu
from jax.sharding import PartitionSpec as P

SEQ = 1024


EPSILON = 1e-06
MASKED = -1e30
LOW = jnp.bfloat16
HIGH = jnp.float32
MESH = pl.DeviceIdType.MESH
VMEM_LIMIT = 127 * 512 * 1024


def dot_nn(left, right):
    return lax.dot_general(left, right, (((1,), (0,)), ((), ())), preferred_element_type=HIGH)


def dot_nt(left, right):
    return lax.dot_general(left, right, (((1,), (1,)), ((), ())), preferred_element_type=HIGH)


def dot_tn(left, right):
    return lax.dot_general(left, right, (((0,), (0,)), ((), ())), preferred_element_type=HIGH)


def norm_forward(summed):
    mean = jnp.mean(summed, axis=-1, keepdims=True)
    centred = summed - mean
    spread = jnp.mean(centred * centred, axis=-1, keepdims=True)
    inverse = lax.rsqrt(spread + EPSILON)
    return centred * inverse, inverse


def norm_backward(xhat, inverse, scaled):
    return inverse * (
        scaled
        - jnp.mean(scaled, axis=-1, keepdims=True)
        - xhat * jnp.mean(scaled * xhat, axis=-1, keepdims=True)
    )


def gelu_parts(u):
    phi_cdf = 0.5 * (1.0 + lax.erf(u * (2.0**-0.5)))
    density = jnp.exp(-0.5 * u * u) * 0.3989422804014327
    return u * phi_cdf, phi_cdf + u * density


def column_sum(values):
    return jnp.sum(values, axis=0, keepdims=True)


def as_row(vector):
    return vector[...].astype(HIGH).reshape(1, -1)


def as_column(row):
    return jnp.broadcast_to(row, (8, row.shape[1])).T[:, :1]


def segment_rows(segment_ids, own_start, share, row_start, length):
    own = segment_ids[pl.ds(own_start, share)].astype(HIGH).reshape(1, share)
    return as_column(own), segment_ids[pl.ds(row_start, length)].astype(HIGH).reshape(1, length)


def segment_bias(own_segments, row_segments):
    return jnp.where(own_segments == row_segments, 0.0, MASKED)


class Place:
    def __init__(self, n_tensor):
        self.n_tensor = n_tensor
        self.z = lax.axis_index("tensor")
        self.dp = lax.axis_index("dp")
        self.core = lax.rem(self.dp, 2)
        self.a = lax.rem(self.dp // 2, 2)
        self.b = lax.rem(self.dp // 4, 2)
        self.to_core = (self.dp + 1 - 2 * self.core, self.z)
        self.to_a = (self.dp + 2 - 4 * self.a, self.z)
        self.to_b = (self.dp + 4 - 8 * self.b, self.z)
        self.others = [lax.rem(self.z + step, n_tensor) for step in range(1, n_tensor)]
        if n_tensor == 4:
            near = self.z + 1 - 2 * lax.rem(self.z, 2)
            upper = self.z // 2
            self.others = [near, 2 - upper, 3 - 3 * upper]

    def pick(self, at, order):
        chosen = order[0]
        for index in range(1, len(order)):
            chosen = jnp.where(at == index, order[index], chosen)
        return chosen


def greet(partners):
    barrier = pltpu.get_barrier_semaphore()
    for partner in partners:
        pl.semaphore_signal(barrier, inc=1, device_id=partner, device_id_type=MESH)


def meet(partners):
    pl.semaphore_wait(pltpu.get_barrier_semaphore(), len(partners))


def remote(src, dst, send, recv, target):
    return pltpu.make_async_remote_copy(
        src_ref=src,
        dst_ref=dst,
        send_sem=send,
        recv_sem=recv,
        device_id=target,
        device_id_type=MESH,
    )


class Spread:
    def __init__(self, place, whole, send, recv, group, block):
        self.place, self.whole, self.send, self.recv, self.group = place, whole, send, recv, group
        self.matrix, self.base, size = block
        self.mine = None
        self.quarter = size // 4
        self.half = whole.shape[3] // 2

    def odd(self, z):
        return lax.rem(z + self.group, 2)

    def piece(self, z, a, b, side):
        odd = self.odd(z)
        row = odd * (2 * b + a) + (1 - odd) * (2 * a + b)
        rows = pl.ds(pl.multiple_of(self.base + row * self.quarter, 16), self.quarter)
        return self.whole.at[self.matrix, z, rows, pl.ds(pl.multiple_of(side * self.half, 128), self.half)]

    def pass_on(self, z, slot, a, b, side, target):
        part = self.piece(z, a, b, side)
        send = self.send.at[self.group, z, slot]
        recv = self.recv.at[self.group, z, slot % 8]
        source = self.mine if self.mine is not None and slot in (1, 2, 4) else part
        return remote(source, part, send, recv, target)

    def turn(self, z):
        p = self.place
        odd = self.odd(z)
        a = p.a * odd + (1 - p.a) * (1 - odd)
        b = p.b * (1 - odd) + (1 - p.b) * odd
        target = odd * p.to_a[0] + (1 - odd) * p.to_b[0]
        return self.pass_on(z, 3, a, b, p.core, (target, p.z))

    def hand_out(self, z):
        p = self.place
        self.pass_on(z, 1, p.a, p.b, p.core, p.to_a).start()
        self.pass_on(z, 2, p.a, p.b, p.core, p.to_b).start()
        self.pass_on(z, 4, p.a, p.b, p.core, p.to_core).start()

    def second(self, z):
        p = self.place
        self.pass_on(z, 1, 1 - p.a, p.b, p.core, p.to_a).wait_recv()
        self.pass_on(z, 2, p.a, 1 - p.b, p.core, p.to_b).wait_recv()
        self.turn(z).start()
        self.pass_on(z, 5, 1 - p.a, p.b, p.core, p.to_core).start()
        self.pass_on(z, 6, p.a, 1 - p.b, p.core, p.to_core).start()

    def third(self, z):
        p = self.place
        self.pass_on(z, 3, 1 - p.a, 1 - p.b, p.core, p.to_a).wait_recv()
        self.pass_on(z, 7, 1 - p.a, 1 - p.b, p.core, p.to_core).start()

    def last(self, z):
        p = self.place
        side = 1 - p.core
        self.pass_on(z, 4, p.a, p.b, side, p.to_core).wait_recv()
        self.pass_on(z, 5, 1 - p.a, p.b, side, p.to_core).wait_recv()
        self.pass_on(z, 6, p.a, 1 - p.b, side, p.to_core).wait_recv()
        self.pass_on(z, 7, 1 - p.a, 1 - p.b, side, p.to_core).wait_recv()

    def sent(self, z):
        p = self.place
        self.pass_on(z, 1, p.a, p.b, p.core, p.to_a).wait_send()
        self.pass_on(z, 2, p.a, p.b, p.core, p.to_b).wait_send()
        self.turn(z).wait_send()
        self.pass_on(z, 4, p.a, p.b, p.core, p.to_core).wait_send()
        self.pass_on(z, 5, 1 - p.a, p.b, p.core, p.to_core).wait_send()
        self.pass_on(z, 6, p.a, 1 - p.b, p.core, p.to_core).wait_send()
        self.pass_on(z, 7, 1 - p.a, 1 - p.b, p.core, p.to_core).wait_send()


class Gather(Spread):
    def along(self, z):
        p = self.place
        part = self.piece(p.z, p.a, p.b, p.core)
        send, recv = self.send.at[self.group, z, 0], self.recv.at[self.group, p.z, 0]
        return remote(part, part, send, recv, (p.dp, z))

    def onward(self, z):
        p = self.place
        target = jnp.where(z < p.z, p.z + 1, p.z - 1)
        copy = self.pass_on(z, 8, p.a, p.b, p.core, (p.dp, target))
        return (target >= 0) & (target < p.n_tensor), copy

    def start(self):
        p = self.place
        for z in (p.z - 1, p.z + 1):
            pl.when((z >= 0) & (z < p.n_tensor))(self.along(z).start)

    def first(self, z):
        p = self.place
        self.pass_on(z, 0, p.a, p.b, p.core, p.to_core).wait_recv()
        there, copy = self.onward(z)
        pl.when(there)(copy.start)
        self.hand_out(z)

    def finish(self):
        p = self.place
        for z in (p.z - 1, p.z + 1):
            pl.when((z >= 0) & (z < p.n_tensor))(self.along(z).wait_send)
        for z in p.others:
            there, copy = self.onward(z)
            pl.when(there)(copy.wait_send)
            self.sent(z)


FORWARD_PLAN = (
    {
        4: (0,),
        19: (100, 1, 10, 200, 2, 300,),
        10: (101,),
        11: (11,),
        14: (110,),
        29: (12, 102, 201, 301,),
        20: (111,),
        21: (20,),
        23: (210,),
        39: (310, 202, 21, 112, 302,),
        30: (211,),
        31: (22,),
        33: (311,),
        34: (120,),
        40: (121, 212,),
        41: (312, 122,),
        46: (220, 221, 320,),
        47: (222, 321,),
        48: (322,),
    },
    {
        4: (0, 1,),
        19: (2, 100, 10, 11, 101, 12, 102, 200, 300,),
        10: (110,),
        12: (20,),
        13: (111,),
        29: (202, 201, 21, 302, 301,),
        20: (22, 112, 210,),
        23: (120,),
        24: (310,),
        30: (211,),
        33: (311,),
        35: (121,),
        40: (122, 212,),
        41: (220, 312,),
        46: (320,),
        47: (221, 222, 321,),
        48: (322,),
    },
)


def in_bands(start, count, work):
    band = 96

    def one(at, carry):
        offset = pl.multiple_of(at * band, 16)
        work(pl.ds(pl.multiple_of(start + offset, 16), band), pl.ds(offset, band))
        return carry

    lax.fori_loop(0, count // band, one, 0)


class Reduce:
    def __init__(self, place, grads, lands, pieces, send, recv, wide, group, block, near_land=None):
        matrix, base, size = block
        self.near_land = near_land
        self.near = place.others[0]
        self.far = place.others if near_land is None else place.others[1:]
        self.place, self.send, self.recv, self.group = place, send, recv, group
        self.half, self.quarter, self.side = size // 2, size // 4, grads.shape[3] // 2

        def rows(ref, parts):
            return ref.at[matrix, :, pl.ds(base // parts, size // parts)]

        core_land, first_land, second_land, far_land = lands
        self.grads = rows(grads, 1)
        self.core_land = core_land.at[max(matrix - 1, 0)]
        self.first_land, self.second_land, self.far_land = (
            rows(first_land, 2),
            rows(second_land, 4),
            rows(far_land, 4),
        )
        self.piece = pieces.at[matrix, pl.ds(base // 4, size // 4)]
        self.wide_flips, wide_out, wide_land, self.wide_send, self.wide_recv = wide
        if self.wide_flips:
            self.wide_out, self.wide_land = rows(wide_out, 4), rows(wide_land, 4)

    def columns(self, side):
        return pl.ds(pl.multiple_of(side * self.side, 128), self.side)

    def axes(self, z):
        p = self.place
        odd = lax.rem(z + self.group, 2)
        ahead, behind = odd * p.b + (1 - odd) * p.a, odd * p.a + (1 - odd) * p.b
        to_first = odd * p.to_b[0] + (1 - odd) * p.to_a[0]
        to_second = odd * p.to_a[0] + (1 - odd) * p.to_b[0]
        return ahead, behind, (to_first, p.z), (to_second, p.z)

    def rows(self, start, size):
        return pl.ds(pl.multiple_of(start, 16), size)

    def copy(self, z, slot, source, target_ref, target):
        send, recv = self.send.at[self.group, z, slot], self.recv.at[self.group, z, slot]
        return remote(source, target_ref, send, recv, target)

    def core_copy(self, z):
        p = self.place
        source = self.grads.at[z, :, self.columns(1 - p.core)]
        return self.copy(z, 0, source, self.core_land.at[z], p.to_core)

    def first_copy(self, z):
        ahead, _, target, _ = self.axes(z)
        source = self.core_land.at[z, self.rows((1 - ahead) * self.half, self.half)]
        return self.copy(z, 1, source, self.first_land.at[z], target)

    def second_copy(self, z):
        ahead, behind, _, target = self.axes(z)
        start = ahead * self.half + (1 - behind) * self.quarter
        source = self.core_land.at[z, self.rows(start, self.quarter)]
        return self.copy(z, 2, source, self.second_land.at[z], target)

    def kept_start(self, z):
        ahead, behind, _, _ = self.axes(z)
        return ahead * self.half + behind * self.quarter

    def kept(self, z):
        return self.rows(self.kept_start(z), self.quarter)

    def far_slot(self, source, target):
        return lax.rem(source - target + self.place.n_tensor, self.place.n_tensor) - 1

    def far_copy(self, z):
        p, group = self.place, self.group
        source = self.core_land.at[z, self.kept(z)]
        send, recv = self.send.at[group, z, 3], self.recv.at[group, p.z, 3]
        return remote(source, self.far_land.at[self.far_slot(p.z, z)], send, recv, (p.dp, z))

    def far_arrival(self, z):
        p, group = self.place, self.group
        land = self.far_land.at[self.far_slot(z, p.z)]
        return remote(land, land, self.send.at[group, z, 3], self.recv.at[group, z, 3], (p.dp, z))

    def wide_copy(self, at):
        group = self.group
        sems = self.wide_send.at[group, at], self.wide_recv.at[group, at]
        target = (self.wide_flips[at], self.place.z)
        return remote(self.wide_out.at[at], self.wide_land.at[at], *sems, target)

    def start(self, z):
        self.core_copy(z).start()

    def add(self, target, start, count, other):
        def work(rows, part):
            target[rows] = target[rows] + other[part]

        in_bands(start, count, work)

    def near_copy(self):
        p, group = self.place, self.group
        sems = self.send.at[group, self.near, 3], self.recv.at[group, p.z, 3]
        return remote(self.core_land.at[self.near], self.near_land, *sems, (p.dp, self.near))

    def near_arrival(self):
        p, group = self.place, self.group
        sems = self.send.at[group, self.near, 3], self.recv.at[group, self.near, 3]
        return remote(self.near_land, self.near_land, *sems, (p.dp, self.near))

    def first(self, z):
        p = self.place
        self.core_copy(z).wait_recv()
        mine = self.grads.at[z, :, self.columns(p.core)]
        land = self.core_land.at[z]
        self.add(land, 0, 2 * self.half, mine)
        if self.near_land is not None and z is self.near:
            self.near_copy().start()
            return
        if self.near_land is not None and z is p.z:
            self.near_arrival().wait_recv()
            self.add(land, 0, 2 * self.half, self.near_land)
        self.first_copy(z).start()

    def second(self, z):
        ahead, _, _, _ = self.axes(z)
        self.first_copy(z).wait_recv()
        land = self.core_land.at[z]
        self.add(land, ahead * self.half, self.half, self.first_land.at[z])
        self.second_copy(z).start()

    def third(self, z):
        self.second_copy(z).wait_recv()
        land = self.core_land.at[z]
        self.add(land, self.kept_start(z), self.quarter, self.second_land.at[z])
        if z is not self.place.z:
            self.far_copy(z).start()

    def fourth(self):
        p = self.place
        for z in self.far:
            self.far_arrival(z).wait_recv()

        def gather_up(rows, part):
            total = self.core_land[p.z, rows].astype(HIGH)
            for z in self.far:
                total = total + self.far_land[self.far_slot(z, p.z), part].astype(HIGH)
            self.piece[part] = total.astype(LOW)

        in_bands(self.kept_start(p.z), self.quarter, gather_up)
        for at in range(len(self.wide_flips)):
            copy = self.wide_copy(at)

            def set_out(rows, part, at=at):
                self.wide_out[at, part] = self.piece[part]

            def take_in(rows, part, at=at):
                self.piece[part] = self.wide_out[at, part] + self.wide_land[at, part]

            in_bands(0, self.quarter, set_out)
            copy.start()
            copy.wait_recv()
            in_bands(0, self.quarter, take_in)

    def finish(self):
        p = self.place
        for z in [p.z] + p.others:
            self.core_copy(z).wait_send()
        for z in [p.z] + self.far:
            self.first_copy(z).wait_send()
            self.second_copy(z).wait_send()
        for z in self.far:
            self.far_copy(z).wait_send()
        if self.near_land is not None:
            self.near_copy().wait_send()
        for at in range(len(self.wide_flips)):
            self.wide_copy(at).wait_send()


class Return(Spread):
    def __init__(self, place, whole, pieces, send, recv, keep_sem, group, block):
        super().__init__(place, whole, send, recv, group, block)
        self.mine = pieces.at[self.matrix, pl.ds(self.base // 4, self.quarter)]
        p = place
        self.keep = pltpu.make_async_copy(self.mine, self.piece(0, p.a, p.b, p.core), keep_sem.at[group])

    def hand_out(self, z):
        super().hand_out(z)
        self.keep.start()

    def sent(self, z):
        super().sent(z)
        self.keep.wait()

    def odd(self, z):
        return lax.rem(self.place.z + self.group, 2)


class Fold:
    def __init__(self, place, flips, stages, lands, far, send, recv):
        self.place, self.flips, self.bits = place, flips, len(flips)
        self.stages, self.lands, self.far, self.send, self.recv = stages, lands, far, send, recv

    def copy(self, bit):
        sems = self.send.at[bit], self.recv.at[bit]
        return remote(self.stages.at[bit], self.lands.at[bit], *sems, (self.flips[bit], self.place.z))

    def start(self):
        self.copy(0).start()

    def fold(self, bit):
        self.copy(bit).wait_recv()
        self.stages[bit + 1] = self.stages[bit] + self.lands[bit]
        if bit + 1 < self.bits:
            self.copy(bit + 1).start()
        else:
            for z in self.place.others:
                self.far_copy(z).start()
            self.far[self.place.z] = self.tile(self.place.z)[...]

    def tile(self, z):
        return self.stages.at[self.bits, z if self.stages.shape[1] > 1 else 0]

    def far_copy(self, z):
        p = self.place
        sems = self.send.at[self.bits + z], self.recv.at[self.bits + p.z]
        return remote(self.tile(z), self.far.at[p.z], *sems, (p.dp, z))

    def total(self):
        p = self.place
        for z in p.others:
            sems = self.send.at[self.bits + z], self.recv.at[self.bits + z]
            remote(self.tile(z), self.far.at[z], *sems, (p.dp, z)).wait_recv()
        total = self.far[0]
        for z in range(1, self.far.shape[0]):
            total = total + self.far[z]
        return total

    def finish(self):
        for bit in range(self.bits):
            self.copy(bit).wait_send()
        for z in self.place.others:
            self.far_copy(z).wait_send()


BACKWARD_PLAN = (
    {
        11: (32, 22,),
        20: (30,),
        21: (20,),
        30: (31,),
        31: (21,),
        50: (132, 122, 33,),
        104: (130, 131,),
        107: (232, 23,),
        116: (121,),
        110: (2, 12,),
        112: (222,),
        113: (133,),
        117: (231, 230, 221,),
        120: (0,),
        121: (123, 102, 10,),
        124: (112,),
        125: (100,),
        127: (233, 223, 202, 323, 333,),
        136: (212,),
        130: (1, 110, 11,),
        132: (200,),
        135: (423,),
        137: (210, 433,),
        200: (111, 3, 101, 13, 523,),
        201: (701, 533, 201, 623, 211,),
        202: (633, 113, 103, 702, 703,),
        203: (213, 313, 203, 303, 413, 403,),
        204: (513, 503, 613, 603,),
    },
    {
        11: (32, 22,),
        20: (30,),
        21: (20,),
        30: (31,),
        31: (21,),
        50: (132, 122, 33,),
        105: (130, 121,),
        107: (222, 23,),
        110: (131, 2, 12,),
        113: (232, 133,),
        117: (221, 230,),
        126: (231,),
        120: (0,),
        121: (123, 112, 10,),
        124: (102,),
        125: (100,),
        127: (233, 223,),
        136: (212, 202,),
        130: (1,),
        131: (110, 11, 323,),
        132: (200,),
        134: (333,),
        135: (101,),
        137: (210, 111,),
        200: (423, 701, 3, 13, 433,),
        201: (201, 211, 103, 523, 702,),
        202: (703, 623, 533, 113, 203,),
        203: (303, 633, 213, 313, 403, 413,),
        204: (503, 513, 603, 613,),
    },
)


def layer_kernel(
    n_tensor,
    heads,
    scale,
    layer_input,
    segment_ids,
    local_qkv,
    w_out,
    w_up,
    w_down,
    in_cotangent,
    qv_bias,
    up_bias,
    out_bias,
    norm1_gain,
    norm1_bias,
    down_bias,
    norm2_gain,
    norm2_bias,
    out_layer,
    out_partial,
    out_landed,
    out_summed,
    out_sums,
    local_small,
    small,
    weights,
    core_land,
    first_land,
    second_land,
    far_land,
    near_land,
    pieces,
    activation,
    slope,
    row_input,
    bias,
    q_and_mixed,
    k_and_v,
    totals,
    head_totals,
    queries,
    keys,
    values,
    grad_mixed,
    grad_k,
    grad_v,
    inverse,
    live_rows,
    terms,
    hidden_low,
    grad_low,
    spare,
    sums,
    sums_land,
    sums_far,
    late_sums,
    late_land,
    late_far,
    wide_out,
    wide_land,
    gather_send,
    gather_recv,
    small_send,
    small_recv,
    copy_sem,
    send,
    recv,
    final_send,
    final_recv,
    wide_send,
    wide_recv,
    term_send,
    term_recv,
    sums_send,
    sums_recv,
    late_send,
    late_recv,
    save_sem,
    keep_sem,
):
    place = Place(n_tensor)
    share = hidden_low.shape[0]
    length, width = row_input.shape
    shares_per_row = length // share
    group_rows = k_and_v.shape[2] // 2
    size = group_rows // heads
    my_share = lax.rem(place.z, shares_per_row)
    in_row = pl.ds(pl.multiple_of(my_share * share, share), share)
    row_start = pl.multiple_of(place.z // shares_per_row * length, length)
    near, middle, far = place.others
    bits = sums_land.shape[0]
    flips = [place.dp + (1 << bit) - (2 << bit) * lax.rem(place.dp // (1 << bit), 2) for bit in range(bits)]

    accum, xhat = terms.at[0], terms.at[1]

    mine = weights.at[0, place.z]
    pairs = [
        (local_qkv, mine.at[pl.ds(0, 3 * group_rows)]),
        (w_out, mine.at[pl.ds(3 * group_rows, group_rows)]),
        (w_up, weights.at[1, place.z]),
        (w_down, weights.at[2, place.z]),
    ]
    own = [
        pltpu.make_async_copy(source, target, copy_sem.at[at]) for at, (source, target) in enumerate(pairs)
    ]
    load_input = pltpu.make_async_copy(
        layer_input.at[pl.ds(row_start, length)], row_input, copy_sem.at[4]
    )
    for copy in own:
        copy.start()
    load_input.start()
    load_cotangent = pltpu.make_async_copy(in_cotangent, spare.at[0], copy_sem.at[5])
    load_cotangent.start()
    partners = [(flip, place.z) for flip in flips] + [(place.dp, z) for z in place.others]
    greet(partners)
    biases = qv_bias[...].astype(HIGH)
    local_small[...] = jnp.zeros(local_small.shape, HIGH)
    for row in range(2):
        parts = [biases[head : head + 1, row * size : (row + 1) * size] for head in range(heads)]
        local_small[row : row + 1, :group_rows] = jnp.concatenate(parts, axis=1)
    local_small[2:3] = as_row(up_bias)
    meet(partners)
    gathers = [Gather(place, weights, gather_send, gather_recv, group, (group, 0, width)) for group in range(3)]
    gather_a, gather_b, gather_c = gathers

    def small_copy(z):
        sems = small_send.at[z], small_recv.at[place.z]
        return remote(local_small, small.at[place.z], *sems, (place.dp, z))

    def small_arrival(z):
        return remote(local_small, small.at[z], small_send.at[z], small_recv.at[z], (place.dp, z))

    own[0].wait()
    own[1].wait()
    gather_a.start()
    for z in place.others:
        small_copy(z).start()
    small[place.z] = local_small[...]
    own_start = pl.multiple_of(place.z * share, share)
    own_segments, row_segments = segment_rows(segment_ids, own_start, share, row_start, length)
    bias[...] = segment_bias(own_segments, row_segments)
    live_rows[...] = (own_segments >= 0).astype(HIGH)
    load_input.wait()

    at_end = (place.z == 0) | (place.z == n_tensor - 1)

    def pass_pieces(slot, there=True):
        for inside, plan in enumerate(FORWARD_PLAN):
            steps = plan.get(slot, ())
            if not steps:
                continue

            def run(steps=steps):
                for step in steps:
                    part = gathers[step // 10 % 10]
                    stage = (part.first, part.second, part.third, part.last)[step // 100]
                    stage(place.others[step % 10])

            pl.when(jnp.logical_and(at_end != bool(inside), there))(run)

    def start_b():
        own[2].wait()
        gather_b.start()

    def start_c():
        own[3].wait()
        gather_c.start()

    def attend_forward(turn, z):
        q_rows, k_rows, v_rows = (
            jnp.concatenate([weights[0, z, pl.ds((3 * head + kind) * size, size)] for head in range(heads)], axis=0)
            for kind in range(3)
        )
        q_bias, v_bias = small[z, 0:1, :group_rows], small[z, 1:2, :group_rows]
        x_row = row_input[...]
        q = (dot_nt(row_input[in_row], q_rows) + q_bias).astype(LOW) * scale
        k = dot_nt(x_row, k_rows).astype(LOW)
        v = (dot_nt(x_row, v_rows) + v_bias).astype(LOW)
        k_and_v[z] = jnp.concatenate([k, v], axis=1)
        for head in range(heads):
            part = slice(head * size, (head + 1) * size)
            queries[head], keys[head], values[head] = q[:, part], k[:, part], v[:, part]

        def one_head(head, carry):
            chunk = share // 2
            for part in range(2):
                rows = pl.ds(part * chunk, chunk)
                scores = dot_nt(queries[head, rows], keys[head]) + bias[rows]
                top = jnp.max(scores, axis=-1, keepdims=True)
                raised = jnp.exp(scores - top)
                total = jnp.sum(raised, axis=-1, keepdims=True)
                summed = dot_nn(raised.astype(LOW), values[head])
                grad_mixed[head, rows] = (summed / total).astype(LOW)
                head_totals[head, rows] = top + jnp.log(total)
                for index in range(heads):
                    pass_pieces(10 * turn + 2 * index + part, head == index)
                    if (turn, index, part) == (1, 0, 1):
                        pl.when(head == index)(start_c)
            return carry

        lax.fori_loop(0, heads, one_head, 0)
        columns = [queries[head] for head in range(heads)] + [grad_mixed[head] for head in range(heads)]
        q_and_mixed[z] = jnp.concatenate(columns, axis=-1)
        totals[z] = jnp.concatenate([head_totals[head] for head in range(heads)], axis=-1)

    attend_forward(0, place.z)
    start_b()
    pass_pieces(19)
    for z in place.others:
        small_arrival(z).wait_recv()
    attend_forward(1, near)
    pass_pieces(29)
    attend_forward(2, middle)
    pass_pieces(39)
    attend_forward(3, far)

    band = min(256, share)
    own_first = my_share * share
    out_shift, gain_first, shift_first = as_row(out_bias), as_row(norm1_gain), as_row(norm1_bias)
    down_shift = as_row(down_bias)

    def project_out(at, carry):
        rows = pl.ds(pl.multiple_of(at * band, band), band)
        own_rows = pl.ds(pl.multiple_of(own_first + at * band, band), band)
        first_sum = row_input[own_rows].astype(HIGH) + out_shift
        for z in range(n_tensor):
            first_sum = first_sum + dot_nn(q_and_mixed[z, rows, group_rows:], weights[0, z, 3 * group_rows :])
        normed, spread = norm_forward(first_sum)
        xhat[rows] = normed
        inverse[rows] = spread
        hidden = normed * gain_first + shift_first
        hidden_low[rows] = hidden.astype(LOW)
        accum[rows] = hidden + down_shift
        return carry

    lax.fori_loop(0, share // band, project_out, 0)

    def feed_forward(at, carry):
        z = place.pick(at, [place.z] + place.others)

        for index in range(n_tensor):
            pass_pieces(40 + index, at == index)
        pl.when(at == 1)(gather_a.finish)
        pl.when(at == 2)(gather_b.finish)
        raw = dot_nn(hidden_low[...], weights[1, z]) + small[z, 2:3]
        value, rise = gelu_parts(raw)
        activation[z] = value.astype(LOW)
        slope[z] = rise.astype(LOW)
        for index in range(n_tensor):
            pass_pieces(45 + index, at == index)
        accum[...] += dot_nn(activation[z], weights[2, z])
        return carry

    lax.fori_loop(0, n_tensor, feed_forward, 0)
    gather_c.finish()

    order = [far, near, middle, place.z]
    lands = (core_land, first_land, second_land, far_land)
    wide = (flips[3:], wide_out, wide_land, wide_send, wide_recv)
    blocks = [(0, 0, width // 2), (0, width // 2, width // 2), (1, 0, width), (2, 0, width)]
    reduces = [
        Reduce(place, weights, lands, pieces, send, recv, wide, group, block, near_land if group == 2 else None)
        for group, block in enumerate(blocks)
    ]
    for half in range(2):
        side = pl.ds(half * width // 2, width // 2)
        reduces[half].core_land = activation.at[:, pl.ds(0, width // 2), side]
    returns = [
        Return(place, out_summed, pieces, final_send, final_recv, keep_sem, group, block)
        for group, block in enumerate(blocks)
    ]
    first_half, second_half, reduce_b, reduce_c = reduces
    fold = Fold(place, flips, sums, sums_land, sums_far, sums_send, sums_recv)
    late_fold = Fold(place, flips, late_sums, late_land, late_far, late_send, late_recv)
    sums[0] = jnp.zeros(sums.shape[1:], HIGH)
    late_sums[0] = jnp.zeros(late_sums.shape[1:], HIGH)

    shards = (near, middle, far, place.z)

    def finish_sum(reduce, spread):
        reduce.fourth()
        spread.hand_out(0)

    def take(step):
        stage, block, shard = step // 100, step // 10 % 10, step % 10
        if stage == 7:
            return next_term(shard)
        reduce, spread = reduces[block], returns[block]
        if stage < 3:
            return (reduce.first, reduce.second, reduce.third)[stage](shards[shard])
        if stage == 3:
            return finish_sum(reduce, spread)
        return (spread.second, spread.third, spread.last)[stage - 4](0)

    def serve(slot, there=True):
        for inside, plan in enumerate(BACKWARD_PLAN):
            steps = plan.get(slot, ())
            if not steps:
                continue

            def run(steps=steps):
                for step in steps:
                    take(step)

            pl.when(jnp.logical_and(at_end != bool(inside), there))(run)

    def serve_loop(at, slot):
        for index in range(n_tensor):
            serve(10 * index + slot, at == index)

    gain_second, shift_second = as_row(norm2_gain), as_row(norm2_bias)

    load_cotangent.wait()
    def second_norm(at, carry):
        rows = pl.ds(pl.multiple_of(at * band, band), band)
        normed, spread = norm_forward(accum[rows])
        cotangent = spare[0, rows].astype(HIGH) * live_rows[rows]
        spare[0, rows] = (normed * gain_second + shift_second).astype(LOW)
        grad_second = norm_backward(normed, spread, cotangent * gain_second)
        sums[0, 0, 6:7] += column_sum(cotangent * normed)
        sums[0, 0, 7:8] += column_sum(cotangent)
        sums[0, 0, 5:6] += column_sum(grad_second)
        grad_low[rows] = grad_second.astype(LOW)
        accum[rows] = grad_second
        return carry

    lax.fori_loop(0, share // band, second_norm, 0)
    save_layer = pltpu.make_async_copy(spare.at[0], out_layer, save_sem.at[0])
    save_layer.start()

    def feed_backward(at, carry):
        z = place.pick(at, order)
        low = grad_low[...]
        grad_up = (dot_nt(low, weights[2, z]) * slope[z].astype(HIGH)).astype(LOW)
        weights[2, z] = dot_tn(activation[z], low).astype(LOW)
        reduce_c.start(z)
        serve_loop(at, 0)
        accum[...] += dot_nt(grad_up, weights[1, z])
        weights[1, z] = dot_tn(hidden_low[...], grad_up).astype(LOW)
        reduce_b.start(z)
        sums[0, z, 1:2] = column_sum(grad_up.astype(HIGH))
        serve_loop(at, 1)
        return carry

    lax.fori_loop(0, n_tensor, feed_backward, 0)

    def first_norm(at, carry):
        rows = pl.ds(pl.multiple_of(at * band, band), band)
        grad_hidden, normed = accum[rows], xhat[rows]
        grad_first = norm_backward(normed, inverse[rows], grad_hidden * gain_first)
        sums[0, 0, 2:3] += column_sum(grad_first)
        sums[0, 0, 3:4] += column_sum(grad_hidden * normed)
        sums[0, 0, 4:5] += column_sum(grad_hidden)
        accum[rows] = grad_first
        grad_low[rows] = grad_first.astype(LOW)
        return carry

    lax.fori_loop(0, share // band, first_norm, 0)
    for step in range(1, shares_per_row):
        terms[step] = jnp.zeros(accum.shape, HIGH)
    for z in range(1, n_tensor):
        sums[0, z, 2:8] = sums[0, 0, 2:8]
    fold.start()
    serve(50)

    parts = 4
    part_rows = share // parts

    def term_copy(step, part):
        rows = pl.ds(part * part_rows, part_rows)
        partner = place.z - my_share + lax.rem(my_share + step, shares_per_row)
        sems = term_send.at[step - 1, part], term_recv.at[step - 1, part]
        return remote(spare.at[step - 1, rows], out_landed.at[step - 1, rows], *sems, (place.dp, partner))

    def fold_some(turn):
        for bit in range(bits):
            if min(bit, 2) == turn:
                fold.fold(bit)

    def send_terms():
        save_layer.wait()
        for step in range(1, shares_per_row):
            spare[step - 1] = terms[step].astype(LOW)
            term_copy(step, 0).start()

    def next_term(part):
        for step in range(1, shares_per_row):
            term_copy(step, part).start()

    def attend_backward(at, carry):
        z = place.pick(at, order)
        incoming = dot_nt(grad_low[...], weights[0, z, 3 * group_rows :]).astype(LOW)
        weights[0, z, 3 * group_rows :] = dot_tn(q_and_mixed[z, :, group_rows:], grad_low[...]).astype(LOW)
        for head in range(heads):
            part = slice(head * size, (head + 1) * size)
            queries[head], grad_mixed[head] = q_and_mixed[z, :, part], incoming[:, part]
            keys[head], values[head] = k_and_v[z, :, part], k_and_v[z, :, group_rows:][:, part]
            head_totals[head] = totals[z, :, head : head + 1]
        serve_loop(at, 106)

        def one_head(head, inner):
            k, v = keys[head], values[head]
            grad_kt = jnp.zeros((size, length), HIGH)
            grad_vt = jnp.zeros((size, length), HIGH)
            chunk = share // 2
            for part in range(2):
                rows = pl.ds(part * chunk, chunk)
                q, up = queries[head, rows], grad_mixed[head, rows]
                chance = jnp.exp(dot_nt(q, k) + bias[rows] - head_totals[head, rows])
                change = chance * dot_nt(up, v)
                change = change - chance * jnp.sum(change, axis=-1, keepdims=True)
                change = change.astype(LOW)
                grad_kt = grad_kt + dot_nn(q.T, change)
                grad_vt = grad_vt + dot_nn(up.T, chance.astype(LOW))
                grad_mixed[head, rows] = (dot_nn(change, k) * scale).astype(LOW)
                for index in range(heads):
                    for turn in range(n_tensor):
                        serve(100 + 10 * turn + 2 * index + part, (head == index) & (at == turn))
            grad_k[head] = grad_kt.astype(LOW)
            grad_v[head] = grad_vt.astype(LOW)
            for turn, bit in ((0, 0), (1, 1), (2, 2)):
                pl.when((head == heads - 1) & (at == turn))(functools.partial(fold_some, bit))
            return inner

        lax.fori_loop(0, heads, one_head, 0)
        dq = jnp.concatenate([grad_mixed[head] for head in range(heads)], axis=-1)
        dk = grad_k[...].reshape(group_rows, length)
        dv = grad_v[...].reshape(group_rows, length)
        x_row = row_input[...]
        q_rows, k_rows, v_rows = (
            jnp.concatenate([weights[0, z, pl.ds((3 * head + kind) * size, size)] for head in range(heads)], axis=0)
            for kind in range(3)
        )

        def share_term(step):
            first_token = lax.rem(my_share + step, shares_per_row) * share
            tokens = pl.ds(pl.multiple_of(first_token, share), share)
            grad_keys = grad_k[:, :, tokens].reshape(group_rows, share)
            grad_values = grad_v[:, :, tokens].reshape(group_rows, share)
            return dot_tn(grad_keys, k_rows) + dot_tn(grad_values, v_rows)

        for step in range(1, shares_per_row):
            terms[step] += share_term(step)
        pl.when(at == n_tensor - 1)(send_terms)
        for kind, (left, right) in enumerate(((dq.T, row_input[in_row]), (dk, x_row), (dv, x_row))):
            grad = dot_nn(left, right).astype(LOW)
            for head in range(heads):
                weights[0, z, pl.ds((3 * head + kind) * size, size)] = grad[head * size : (head + 1) * size]
        first_half.start(z)
        second_half.start(z)
        accum[...] += share_term(0) + dot_nn(dq, q_rows)
        ones = jnp.ones((8, length), LOW)
        q_sums, v_sums = dot_nn(ones[:, :share], dq)[0:1], dot_nt(ones, dv)[0:1]
        for head in range(heads):
            part = slice(head * size, (head + 1) * size)
            pair = jnp.concatenate([q_sums[:, part], v_sums[:, part]], axis=1)
            at_row = lax.broadcasted_iota(jnp.int32, (8, 2 * size), 0) == z
            late_sums[0, 0, :, 2 * head * size : 2 * (head + 1) * size] += jnp.where(at_row, pair, 0.0)
        serve_loop(at, 107)
        return carry

    lax.fori_loop(0, n_tensor, attend_backward, 0)

    def keep_row(values, z):
        out_sums[0:1] = values[z : z + 1]

    late_fold.start()
    save_partial = pltpu.make_async_copy(accum, out_partial, save_sem.at[1])
    save_partial.start()
    for bit in range(bits):
        if bit < 3:
            serve(200 + bit)
        late_fold.fold(bit)
    for reduce in reduces[2:]:
        reduce.finish()
    fold.finish()
    serve(203)
    for step in range(1, shares_per_row):
        for part in range(parts):
            term_copy(step, part).wait_send()
            term_copy(step, part).wait_recv()
    out_sums[...] = fold.total()
    late_total = late_fold.total()
    for z in range(n_tensor):
        pl.when(place.z == z)(functools.partial(keep_row, late_total, z))
    serve(204)
    late_fold.finish()
    for reduce in reduces[:2]:
        reduce.finish()
    for part in returns:
        part.sent(0)
    for z in place.others:
        small_copy(z).wait_send()
    save_partial.wait()


def finish_kernel(
    heads,
    in_layer,
    in_partial,
    in_landed,
    in_summed,
    sums,
    out_layer,
    out_input,
    out_qkv,
    qv_bias,
    out_out,
    out_bias,
    gain_first,
    shift_first,
    out_up,
    up_bias,
    out_down,
    down_bias,
    gain_second,
    shift_second,
    layer,
    partial,
    landed,
    summed,
    qkv,
    rest,
    matrices,
    load_sem,
    save_sem,
):
    size = qkv.shape[1]
    pairs = [(in_summed.at[2, 0], summed.at[2]), (in_summed.at[1, 0], summed.at[1]), (in_partial, partial)]
    pairs += [(in_landed, landed), (in_summed.at[0, 0], summed.at[0]), (in_layer, layer)]
    loads = [
        pltpu.make_async_copy(source, target, load_sem.at[at]) for at, (source, target) in enumerate(pairs)
    ]
    for copy in loads:
        copy.start()
    for at, vector in enumerate(
        [up_bias, out_bias, gain_first, shift_first, down_bias, gain_second, shift_second]
    ):
        vector[...] = sums[1 + at : 2 + at].reshape(vector.shape)
    for head in range(heads):
        width = qv_bias.shape[1]
        qv_bias[head : head + 1] = sums[0:1, head * width : (head + 1) * width]
    saves = []

    def save(source, target):
        copy = pltpu.make_async_copy(source, target, save_sem.at[len(saves)])
        copy.start()
        saves.append(copy)

    for at, target in ((2, out_down), (1, out_up)):
        loads[2 - at].wait()
        matrices[at - 1] = summed[at].astype(HIGH)
        save(matrices.at[at - 1], target)
    loads[2].wait()
    loads[3].wait()
    for step in range(landed.shape[0]):
        partial[...] += landed[step].astype(HIGH)
    save(partial, out_input)
    loads[4].wait()
    rest[...] = summed[0, heads * size :].astype(HIGH)
    save(rest, out_out)
    for head in range(heads):
        qkv[head] = summed[0, head * size : (head + 1) * size].astype(HIGH)
    save(qkv, out_qkv)
    loads[5].wait()
    save(layer, out_layer)
    for copy in saves:
        copy.wait()


def on_device(
    layer_input,
    segment_ids,
    w_qkv,
    qv_bias,
    w_out,
    out_bias,
    norm1_gain,
    norm1_bias,
    w_up,
    up_bias,
    w_down,
    down_bias,
    norm2_gain,
    norm2_bias,
    out_cotangent,
):
    n_tensor = lax.axis_size("tensor")
    place = lax.axis_index("tensor")
    n_dp = lax.axis_size("dp")
    bits = n_dp.bit_length() - 1
    tokens, width = layer_input.shape
    share = tokens // n_tensor
    heads = qv_bias.shape[0]
    head_dim = qv_bias.shape[1] // 2
    score_scale = float(head_dim) ** (-0.5)
    shares_per_row = SEQ // share
    group_rows = heads * head_dim

    local_qkv = w_qkv.transpose(1, 2, 0).reshape(3 * group_rows, width)
    vmem = pl.BlockSpec(memory_space=pltpu.VMEM)
    anywhere = pl.BlockSpec(memory_space=pl.ANY)

    def low(*shape):
        return jax.ShapeDtypeStruct(shape, LOW)

    def high(*shape):
        return jax.ShapeDtypeStruct(shape, HIGH)

    def low_scratch(*shape):
        return pltpu.VMEM(shape, LOW)

    def high_scratch(*shape):
        return pltpu.VMEM(shape, HIGH)

    dma = pltpu.SemaphoreType.DMA
    side, quarter = width // 2, width // 4
    wide = bits - 3
    wide_shape = (3, wide, quarter, side) if wide else (3, 1, 64, 128)
    layer_output, partial, landed, summed, sums = pl.pallas_call(
        functools.partial(layer_kernel, n_tensor, heads, score_scale),
        out_shape=(
            low(share, width),
            high(share, width),
            low(shares_per_row - 1, share, width),
            low(3, 1, width, width),
            high(8, width),
        ),
        in_specs=[anywhere, vmem] + [anywhere] * 5 + [vmem] * 8,
        out_specs=(anywhere,) * 4 + (vmem,),
        scratch_shapes=[
            high_scratch(8, width),
            high_scratch(n_tensor, 8, width),
            low_scratch(3, n_tensor, width, width),
            low_scratch(2, n_tensor, width, side),
            low_scratch(3, n_tensor, 2 * quarter, side),
            low_scratch(3, n_tensor, quarter, side),
            low_scratch(3, n_tensor - 1, quarter, side),
            low_scratch(width, side),
            low_scratch(3, quarter, side),
            low_scratch(n_tensor, share, width),
            low_scratch(n_tensor, share, width),
            low_scratch(SEQ, width),
            high_scratch(share, SEQ),
            low_scratch(n_tensor, share, 2 * group_rows),
            low_scratch(n_tensor, SEQ, 2 * group_rows),
            high_scratch(n_tensor, share, heads),
            high_scratch(heads, share, 1),
            low_scratch(heads, share, head_dim),
            low_scratch(heads, SEQ, head_dim),
            low_scratch(heads, SEQ, head_dim),
            low_scratch(heads, share, head_dim),
            low_scratch(heads, head_dim, SEQ),
            low_scratch(heads, head_dim, SEQ),
            high_scratch(share, 1),
            high_scratch(share, 1),
            high_scratch(shares_per_row, share, width),
            low_scratch(share, width),
            low_scratch(share, width),
            low_scratch(shares_per_row - 1, share, width),
            high_scratch(bits + 1, n_tensor, 8, width),
            high_scratch(bits, n_tensor, 8, width),
            high_scratch(n_tensor, 8, width),
            high_scratch(bits + 1, 1, 8, width),
            high_scratch(bits, 1, 8, width),
            high_scratch(n_tensor, 8, width),
            low_scratch(*wide_shape),
            low_scratch(*wide_shape),
            dma((3, n_tensor, 9)),
            dma((3, n_tensor, 8)),
            dma((n_tensor,)),
            dma((n_tensor,)),
            dma((6,)),
            dma((4, n_tensor, 4)),
            dma((4, n_tensor, 4)),
            dma((4, 1, 9)),
            dma((4, 1, 8)),
            dma((4, max(wide, 1))),
            dma((4, max(wide, 1))),
            dma((shares_per_row - 1, 4)),
            dma((shares_per_row - 1, 4)),
            dma((bits + n_tensor,)),
            dma((bits + n_tensor,)),
            dma((bits + n_tensor,)),
            dma((bits + n_tensor,)),
            dma((3,)),
            dma((4,)),
        ],
        compiler_params=pltpu.CompilerParams(
            collective_id=0, has_side_effects=True, vmem_limit_bytes=VMEM_LIMIT
        ),
        name="layer",
    )(
        layer_input,
        segment_ids,
        local_qkv,
        w_out,
        w_up,
        w_down,
        out_cotangent,
        qv_bias,
        up_bias,
        out_bias,
        norm1_gain,
        norm1_bias,
        down_bias,
        norm2_gain,
        norm2_bias,
    )

    vector = high(width)
    matrix = high(width, width)
    layer_output, input_grad, grad_qkv, *rest = pl.pallas_call(
        functools.partial(finish_kernel, heads),
        out_shape=(
            low(share, width),
            high(share, width),
            high(heads, 3 * head_dim, width),
            high(heads, 2 * head_dim),
            high(group_rows, width),
            vector,
            vector,
            vector,
            matrix,
            vector,
            matrix,
            vector,
            vector,
            vector,
        ),
        in_specs=[anywhere] * 4 + [vmem],
        out_specs=(anywhere,) * 3 + (vmem, anywhere, vmem, vmem, vmem, anywhere, vmem, anywhere, vmem, vmem, vmem),
        scratch_shapes=[
            low_scratch(share, width),
            high_scratch(share, width),
            low_scratch(shares_per_row - 1, share, width),
            low_scratch(3, width, width),
            high_scratch(heads, 3 * head_dim, width),
            high_scratch(group_rows, width),
            high_scratch(2, width, width),
            dma((6,)),
            dma((6,)),
        ],
        compiler_params=pltpu.CompilerParams(vmem_limit_bytes=VMEM_LIMIT),
        name="finish",
    )(layer_output, partial, landed, summed, sums)
    return (layer_output, input_grad, grad_qkv.transpose(2, 0, 1), *rest)


def solution(mesh):
    return jax.shard_map(
        on_device,
        mesh=mesh,
        in_specs=(
            P("dp", None),
            P("dp"),
            P(None, "tensor", None),
            P("tensor", None),
            P("tensor", None),
            P(),
            P(),
            P(),
            P(None, "tensor"),
            P("tensor"),
            P("tensor", None),
            P(),
            P(),
            P(),
            P(("dp", "tensor"), None),
        ),
        out_specs=(
            P(("dp", "tensor"), None),
            P(("dp", "tensor"), None),
            P(None, "tensor", None),
            P("tensor", None),
            P("tensor", None),
            P(),
            P(),
            P(),
            P(None, "tensor"),
            P("tensor"),
            P("tensor", None),
            P(),
            P(),
            P(),
        ),
        check_vma=False,
    )
```
